128 devices in a mesh: zonal: 16 (over z_lo, y, core), merid: 8 (over x, z_hi).
Axes of the slice: x: 4, y: 4, z: 4 (z_hi: 2, z_lo: 2; z = z_hi * 2 + z_lo), core: 2. Of those that a mesh axis runs over, the one named last changes fastest.
Arguments:
- field: bfloat16 [200, 128, 2048], P(None, 'merid', 'zonal'), may hold values from -6 to 6
- land_mask: int32 [128, 2048], P('merid', 'zonal'), may hold values 0 or 1
- fold_partner: int32 [2048], replicated, may hold values from 0 to 2047, as said below
- dw_kernel: bfloat16 [3, 200, 7, 7], replicated, may hold values from -0.875 to 0.875
- norm_gain: bfloat16 [3, 200], replicated, may hold values from 0.25 to 1.75
- w_in: bfloat16 [3, 200, 800], replicated, may hold values from -0.4375 to 0.4375
- w_out: bfloat16 [3, 800, 200], replicated, may hold values from -0.21875 to 0.21875
Outputs:
- state: bfloat16 [200, 128, 2048], P(None, 'merid', 'zonal')
The draws below stay inside these ranges and needn't reach their ends.
Inputs may be any that keep to these rules, and one draw needn't show every extreme that they name: fold_partner[j] = (s - j) mod 2048 for one s.
All inputs are finite; a program needn't handle non-finite values. No bound on the sum of `land_mask` on one device may be relied on, other than what follows from the above.
Results may differ from the reference program's by a relative error of at most 0.012.
Values may be sent and summed in bfloat16 or wider, within the bound.
No kernel may reach another device: no remote copies, remote signals or barrier semaphores. Data moves between devices by JAX's collectives and lax.ppermute only.
A program may use at most 128 MiB of HBM per device.

```python
import math
import jax
import jax.numpy as jnp
from jax import lax

C = 200
H = 800
BLOCKS = 3
NX = 2048
NY = 128


def draw_fold_partner(key, part):
    mirror = jax.random.randint(key, (), 0, NX, dtype=jnp.int32)
    places = jnp.arange(NX, dtype=jnp.int32)
    return jnp.mod(mirror - places, NX).astype(jnp.int32)


def with_ends(drawn, key, least, largest):
    dims = drawn.shape
    place = [jax.random.randint(jax.random.fold_in(key, axis), (), 0, dims[axis]) for axis in range(len(dims))]
    drawn = drawn.at[tuple(place)].set(least)
    longest = dims.index(max(dims))
    place[longest] = (place[longest] + 1) % dims[longest]
    return drawn.at[tuple(place)].set(largest)


def shard_levels(rng, extent, shards, smallest, largest):
    level, own = 1.0, jax.random.fold_in(rng, 6)
    for axis_at, parts in shards:
        draws = jnp.exp(jax.random.uniform(jax.random.fold_in(own, axis_at), (parts,), jnp.float32, smallest / len(shards), largest / len(shards)))
        level = level * jnp.repeat(draws, extent[axis_at] // parts).reshape([-1 if axis == axis_at else 1 for axis in range(len(extent))])
    return level


def bell_draw(rng, shape, scale, bound, cuts=(), kind=jnp.bfloat16):
    factor_of = shard_levels(rng, shape, cuts, -0.22, 0.18) if cuts else 1.0
    result = jax.random.normal(rng, shape, jnp.float32) * scale * factor_of
    return jnp.minimum(jnp.maximum(result, -bound), bound).astype(kind)


def setup_inputs(seed: int = 0) -> dict:
    splits = jax.random.split(jax.random.key(seed), 8)
    field = bell_draw(splits[0], (C, NY, NX), 1.0, 6.0, ((1, 8), (2, 16)))
    land_mask = with_ends((jax.random.randint(splits[1], (NY, NX), 0, 4) < 3).astype(jnp.int32), jax.random.fold_in(splits[1], 1), 0, 1)
    fold_partner = draw_fold_partner(jax.random.fold_in(splits[7], 71), 0)
    dw_kernel = bell_draw(splits[3], (BLOCKS, C, 7, 7), 49 ** -0.5, 0.875)
    norm_gain = jnp.clip(1.0 + 0.15 * jax.random.normal(splits[4], (BLOCKS, C), jnp.float32), 0.25, 1.75).astype(jnp.bfloat16)
    w_in = bell_draw(splits[5], (BLOCKS, C, H), C ** -0.5, 0.4375)
    w_out = bell_draw(splits[6], (BLOCKS, H, C), H ** -0.5, 0.21875)
    return dict(field=field, land_mask=land_mask, fold_partner=fold_partner, dw_kernel=dw_kernel, norm_gain=norm_gain, w_in=w_in, w_out=w_out)


epsilon = 1e-05

def block_tile(padded, center, sea_mask, kernel, gain, weight_in, weight_out):
    channels = center.shape[0]
    row_count = center.shape[1]
    col_count = center.shape[2]
    source = padded.astype(jnp.float32)
    taps = kernel.astype(jnp.float32)
    convolved = jnp.zeros((channels, row_count, col_count), jnp.float32)
    for row_off in range(7):
        for col_off in range(7):
            convolved = convolved + taps[:, row_off, col_off][:, None, None] * source[:, row_off:row_off + row_count, col_off:col_off + col_count]
    mean_chan = lax.optimization_barrier(jnp.mean(convolved, axis=0))
    centered = convolved - mean_chan
    spread = lax.optimization_barrier(jnp.mean(centered * centered, axis=0))
    normed = (centered * lax.rsqrt(spread + epsilon) * gain.astype(jnp.float32)[:, None, None]).astype(jnp.bfloat16)
    flat = normed.reshape(channels, row_count * col_count)
    hidden = jnp.dot(weight_in.T, flat, preferred_element_type=jnp.float32)
    hidden = jax.nn.gelu(hidden, approximate=False).astype(jnp.bfloat16)
    output = jnp.dot(weight_out.T, hidden, preferred_element_type=jnp.float32).reshape(channels, row_count, col_count)
    return ((center.astype(jnp.float32) + output) * sea_mask).astype(jnp.bfloat16)

def fold_pad(current, partner):
    channels, row_total, col_total = current.shape
    flipped = current[:, row_total - 3:, :][:, ::-1, :]
    folded = jnp.take(flipped, partner, axis=2)
    below = jnp.zeros((channels, 3, col_total), current.dtype)
    stacked = jnp.concatenate([below, current, folded], axis=1)
    return jnp.concatenate([stacked[:, :, col_total - 3:], stacked, stacked[:, :, :3]], axis=2)

def reference(field, land_mask, fold_partner, dw_kernel, norm_gain, w_in, w_out):
    channels, row_total, col_total = field.shape
    step_rows = math.gcd(row_total, 16)
    sea_mask = land_mask.astype(jnp.float32)
    current = field
    for block_index in range(BLOCKS):
        padded = fold_pad(current, fold_partner)
        kernel = dw_kernel[block_index]
        gain = norm_gain[block_index]
        weight_in = w_in[block_index]
        weight_out = w_out[block_index]
        state_now = current

        def one_tile(tile_index):
            start = (tile_index * step_rows).astype(jnp.int32)
            tile = lax.dynamic_slice_in_dim(padded, start, step_rows + 6, 1)
            center = lax.dynamic_slice_in_dim(state_now, start, step_rows, 1)
            sea_part = lax.dynamic_slice_in_dim(sea_mask, start, step_rows, 0)
            return block_tile(tile, center, sea_part, kernel, gain, weight_in, weight_out)
        tiles = lax.map(one_tile, jnp.arange(row_total // step_rows).astype(jnp.int32))
        current = jnp.transpose(tiles, (1, 0, 2, 3)).reshape(channels, row_total, col_total)
    return current
```

```python
import jax
import jax.numpy as jnp
import numpy as np
from jax import lax
from jax.experimental import pallas as pl
from jax.experimental.pallas import tpu as pltpu
from jax.sharding import PartitionSpec as P

BLOCKS = 3
C = 200
H = 800
ROWS = 16
LANES = 128
GROUPS = C // 8
PER_E = 8 * ROWS + 8 * 6
DEPTH = 7 * PER_E
EPS = 1e-05
F32 = jnp.float32
BF16 = jnp.bfloat16


def slot_row(slot):
    if slot < 8 * ROWS:
        return slot // ROWS, slot % ROWS + 3
    k, c = divmod(slot - 8 * ROWS, 8)
    return c, (k if k < 3 else k + ROWS)


def make_constants():
    spread = np.zeros((ROWS, 64, DEPTH), np.float32)
    own = np.zeros((16, DEPTH), np.float32)
    for e in range(7):
        for slot in range(PER_E):
            c, row = slot_row(slot)
            own[c, e * PER_E + slot] = 1
            own[c + 8, e * PER_E + slot] = 1
            for i in range(ROWS):
                a = row - i
                if 0 <= a < 7:
                    spread[i, a * 7 + e, e * PER_E + slot] = 1
    edge_of = [125, 126, 127, 0, 1, 2]
    pack_own = np.zeros((16 * LANES, LANES), np.float32)
    for c in range(16):
        for e in range(6):
            pack_own[c * LANES + edge_of[e], 8 * c + e] = 1
    pack_halo = np.zeros((6 * LANES, LANES), np.float32)
    for k in range(6):
        for e in range(6):
            pack_halo[k * LANES + edge_of[e], 8 * k + e] = 1
    open_own = np.zeros((2 * LANES, 16 * LANES), np.float32)
    for c in range(16):
        for e in range(3):
            open_own[8 * c + e, c * LANES + 125 + e] = 1
            open_own[LANES + 8 * c + 3 + e, c * LANES + e] = 1
    open_halo = open_own[:, : 6 * LANES].copy()
    as_bf = lambda v: np.asarray(v, dtype=BF16)
    return tuple(as_bf(v) for v in (spread, own, pack_own, pack_halo, open_own, open_halo))


SPREAD, OWN, PACK_OWN, PACK_HALO, OPEN_OWN, OPEN_HALO = make_constants()


def dot32(a, b):
    return jnp.dot(a, b, preferred_element_type=F32)


def band_kernel(taps_ref, spread_ref, own_ref, band_ref):
    own = own_ref[...]

    def pair(p, carry):
        even = dot32(taps_ref[...], spread_ref[2 * p]).reshape(GROUPS, 8, DEPTH)
        odd = dot32(taps_ref[...], spread_ref[2 * p + 1]).reshape(GROUPS, 8, DEPTH)
        both = jnp.concatenate([even, odd], axis=1).astype(BF16)
        band_ref[:, pl.ds(pl.multiple_of(16 * p, 16), 16), :] = both * own[None]
        return carry

    lax.fori_loop(0, ROWS // 2, pair, 0)


def make_bands(taps):
    return pl.pallas_call(
        band_kernel,
        out_shape=jax.ShapeDtypeStruct((GROUPS, LANES, DEPTH), BF16),
        in_specs=[pl.BlockSpec(memory_space=pltpu.VMEM)] * 3,
        out_specs=pl.BlockSpec(memory_space=pltpu.VMEM),
        compiler_params=pltpu.CompilerParams(vmem_limit_bytes=40 * 2**20),
        cost_estimate=pl.CostEstimate(flops=2 * 16 * 256 * 256 * 1280, bytes_accessed=10_000_000, transcendentals=0),
    )(taps, jnp.asarray(SPREAD), jnp.asarray(OWN))


def edge_kernel(scal_ref, x_ref, below_ref, above_ref, fold_a_ref, fold_b_ref, pack_own_ref, pack_halo_ref,
                halo_ref, send_ref, rows_ref):
    off = scal_ref[0]
    at_top = scal_ref[1]
    src = lax.broadcasted_iota(jnp.int32, (LANES, LANES), 0)
    dst = lax.broadcasted_iota(jnp.int32, (LANES, LANES), 1)
    pick_a = jnp.where(src + dst == off + 127, 1.0, 0.0).astype(BF16)
    pick_b = jnp.where(src + dst == off - 1, 1.0, 0.0).astype(BF16)
    corner = jnp.zeros((C, LANES), F32)
    for k in range(6):
        if k < 3:
            row = below_ref[k].astype(F32)
        else:
            q = 5 - k
            folded = dot32(fold_a_ref[q], pick_a) + dot32(fold_b_ref[q], pick_b)
            row = jnp.where(at_top == 1, folded, above_ref[k - 3].astype(F32))
        rows_ref[k] = row.reshape(GROUPS, 8, LANES)
        corner += dot32(row.astype(BF16), pack_halo_ref[k * LANES : (k + 1) * LANES, :])
    for g in range(GROUPS):
        halo_ref[g] = rows_ref[:, g].reshape(48, LANES).astype(BF16)
    send_ref[208:408, :] = corner.astype(BF16)
    send_ref[408:416, :] = jnp.zeros((8, LANES), BF16)
    own = jnp.zeros((208, LANES), F32)
    for c in range(16):
        tiles = [x_ref[16 * q + c] if 16 * q + c < C else jnp.zeros((ROWS, LANES), BF16) for q in range(13)]
        own += dot32(jnp.concatenate(tiles, axis=0), pack_own_ref[c * LANES : (c + 1) * LANES, :])
    send_ref[0:208, :] = own.astype(BF16)


def prepare_edges(scal, x, below, above, fold_a, fold_b):
    vm = pl.BlockSpec(memory_space=pltpu.VMEM)
    return pl.pallas_call(
        edge_kernel,
        out_shape=(
            jax.ShapeDtypeStruct((GROUPS, 48, LANES), BF16),
            jax.ShapeDtypeStruct((416, LANES), BF16),
        ),
        in_specs=[pl.BlockSpec(memory_space=pltpu.SMEM)] + [vm] * 7,
        out_specs=(vm, vm),
        scratch_shapes=[pltpu.VMEM((6, GROUPS, 8, LANES), F32)],
        compiler_params=pltpu.CompilerParams(vmem_limit_bytes=24 * 2**20),
    )(scal, x, below, above, fold_a, fold_b, jnp.asarray(PACK_OWN), jnp.asarray(PACK_HALO))


def gelu(h):
    return h * (0.5 + 0.5 * lax.erf(h * np.float32(0.5**0.5)))


def block_kernel(x_ref, band_ref, west_ref, east_ref, halo_ref, w1_ref, w2_ref, gain_ref, mask_ref,
                 open_own_ref, open_halo_ref, out_ref, top_ref, bot_ref,
                 side_ref, halo_side_ref, hs32_ref, rhs_ref, conv_ref, o_ref):
    sides = jnp.concatenate([west_ref[0:208, :], east_ref[0:208, :]], axis=1)
    for c in range(16):
        opened = dot32(sides, open_own_ref[:, c * LANES : (c + 1) * LANES]).astype(BF16)
        side_ref[:, c] = opened.reshape(13, ROWS, LANES)
    corners = jnp.concatenate([west_ref[208:416, :], east_ref[208:416, :]], axis=1)
    for k in range(6):
        opened = dot32(corners, open_halo_ref[:, k * LANES : (k + 1) * LANES])
        hs32_ref[k] = opened.reshape(26, 8, LANES)
    for g in range(GROUPS):
        halo_side_ref[g] = hs32_ref[:, g].reshape(48, LANES).astype(BF16)

    lane = lax.broadcasted_iota(jnp.int32, (PER_E, LANES), 1).astype(F32).astype(BF16)

    def conv(g, carry):
        q, odd = g // 2, g % 2
        main = x_ref[pl.ds(8 * g, 8)].reshape(128, LANES)
        side = side_ref[q, pl.ds(8 * odd, 8)].reshape(128, LANES)
        full = jnp.concatenate([main, halo_ref[g]], axis=0)
        ends = jnp.concatenate([side, halo_side_ref[g]], axis=0)
        for e in range(7):
            s = e - 3
            if s > 0:
                v = pltpu.roll(jnp.where(lane < s, ends, full), LANES - s, 1)
            elif s < 0:
                v = pltpu.roll(jnp.where(lane >= LANES + s, ends, full), -s, 1)
            else:
                v = full
            rhs_ref[e * PER_E : (e + 1) * PER_E, :] = v
        conv_ref[:, g] = dot32(band_ref[g], rhs_ref[...]).reshape(ROWS, 8, LANES)
        return carry

    lax.fori_loop(0, GROUPS, conv, 0)

    def mlp(p, carry):
        parts = []
        for r in range(2):
            y = conv_ref[2 * p + r].reshape(C, LANES)
            mean = jnp.sum(y, axis=0, keepdims=True) * np.float32(1 / C)
            y = y - mean
            var = jnp.sum(y * y, axis=0, keepdims=True) * np.float32(1 / C)
            parts.append((y * lax.rsqrt(var + EPS) * gain_ref[...]).astype(BF16))
        hidden = gelu(dot32(w1_ref[...], jnp.concatenate(parts, axis=1))).astype(BF16)
        o = dot32(w2_ref[...], hidden)
        for r in range(2):
            o_ref[pl.ds(2 * p + r, C, stride=ROWS), :] = o[:, r * LANES : (r + 1) * LANES]
        return carry

    lax.fori_loop(0, ROWS // 2, mlp, 0)

    mask = mask_ref[...]

    def finish(g, carry):
        at = pl.ds(pl.multiple_of(128 * g, 128), 128)
        o = o_ref[at, :].reshape(8, ROWS, LANES)
        res = (x_ref[pl.ds(8 * g, 8)].astype(F32) + o) * mask[None]
        out_ref[pl.ds(8 * g, 8)] = res.astype(BF16)
        o_ref[at, :] = res.reshape(128, LANES)
        return carry

    lax.fori_loop(0, GROUPS, finish, 0)
    for k in range(3):
        top_ref[k] = o_ref[pl.ds(ROWS - 3 + k, C, stride=ROWS), :].astype(BF16)
        bot_ref[k] = o_ref[pl.ds(k, C, stride=ROWS), :].astype(BF16)


def run_block(x, bands, west, east, halo, w1, w2, gain, mask):
    vm = pl.BlockSpec(memory_space=pltpu.VMEM)
    return pl.pallas_call(
        block_kernel,
        out_shape=(
            jax.ShapeDtypeStruct((C, ROWS, LANES), BF16),
            jax.ShapeDtypeStruct((3, C, LANES), BF16),
            jax.ShapeDtypeStruct((3, C, LANES), BF16),
        ),
        in_specs=[vm] * 11,
        out_specs=(vm, vm, vm),
        scratch_shapes=[
            pltpu.VMEM((13, 16, ROWS, LANES), BF16),
            pltpu.VMEM((GROUPS, 48, LANES), BF16),
            pltpu.VMEM((6, 26, 8, LANES), F32),
            pltpu.VMEM((DEPTH, LANES), BF16),
            pltpu.VMEM((ROWS, GROUPS, 8, LANES), F32),
            pltpu.VMEM((C * ROWS, LANES), F32),
        ],
        compiler_params=pltpu.CompilerParams(vmem_limit_bytes=48 * 2**20),
    )(x, bands, west, east, halo, w1, w2, gain, mask, jnp.asarray(OPEN_OWN), jnp.asarray(OPEN_HALO))


def local(field, land_mask, fold_partner, dw_kernel, norm_gain, w_in, w_out):
    zonal = lax.axis_size("zonal")
    merid = lax.axis_size("merid")
    total = fold_partner.shape[0]
    start = jnp.mod(fold_partner[0] - (LANES - 1), total)
    turn = start // LANES
    at_top = (lax.axis_index("merid") == merid - 1).astype(jnp.int32)
    scal = jnp.stack([start % LANES, at_top])
    place = lambda m, z: z * merid + m

    def fold_branch(shift):
        def branch(rows):
            def send(step):
                pairs = [(place(merid - 1, z), place(merid - 1, (shift + step - z) % zonal)) for z in range(zonal)]
                return lax.ppermute(rows, ("zonal", "merid"), pairs)

            return send(0), send(1)

        return branch

    branches = [fold_branch(t) for t in range(zonal)]
    taps = jnp.pad(dw_kernel.reshape(BLOCKS, C, 49), ((0, 0), (0, 0), (0, 15)))
    gains = jnp.broadcast_to(norm_gain.astype(F32)[:, :, None], (BLOCKS, C, LANES))
    w1 = jnp.swapaxes(w_in, 1, 2)
    w2 = jnp.swapaxes(w_out, 1, 2)
    mask = land_mask.astype(F32)
    x = field
    top = jnp.swapaxes(field[:, ROWS - 3 :, :], 0, 1)
    bot = jnp.swapaxes(field[:, :3, :], 0, 1)
    for b in range(BLOCKS):
        bands = make_bands(taps[b])
        below = lax.ppermute(top, "merid", [(m, m + 1) for m in range(merid - 1)])
        above = lax.ppermute(bot, "merid", [(m + 1, m) for m in range(merid - 1)])
        fold_a, fold_b = lax.switch(turn, branches, top)
        halo, send = prepare_edges(scal, x, below, above, fold_a, fold_b)
        west = lax.ppermute(send, "zonal", [(z, (z + 1) % zonal) for z in range(zonal)])
        east = lax.ppermute(send, "zonal", [((z + 1) % zonal, z) for z in range(zonal)])
        x, top, bot = run_block(x, bands, west, east, halo, w1[b], w2[b], gains[b], mask)
    return x


def solution(mesh):
    in_specs = (P(None, "merid", "zonal"), P("merid", "zonal"), P(), P(), P(), P(), P())
    out_specs = P(None, "merid", "zonal")
    return jax.shard_map(local, mesh=mesh, in_specs=in_specs, out_specs=out_specs, check_vma=False)
```

```python
import jax
import jax.numpy as jnp
import numpy as np
from jax import lax
from jax.experimental import pallas as pl
from jax.experimental.pallas import tpu as pltpu
from jax.sharding import PartitionSpec as P

BLOCKS = 3
C = 200
PAD = 208
H = 800
ROWS = 16
LANES = 128
GROUPS = C // 8
MAIN = 8 * ROWS
SIDE = 8 * 6
EPS = 1e-05
F32 = jnp.float32
BF16 = jnp.bfloat16
EDGE_ROWS = (0, 1, 2, 13, 14, 15)
SEND = 5 * PAD
SWAP = 4 * PAD
VM = pl.BlockSpec(memory_space=pltpu.VMEM)
SM = pl.BlockSpec(memory_space=pltpu.SMEM)


def make_constants():
    main = np.zeros((ROWS, 64, 7 * MAIN), np.float32)
    side = np.zeros((6, 64, 7 * SIDE), np.float32)
    own_main = np.zeros((16, 7 * MAIN), np.float32)
    own_side = np.zeros((16, 7 * SIDE), np.float32)
    for e in range(7):
        for c in range(8):
            for r in range(ROWS):
                own_main[[c, c + 8], e * MAIN + c * ROWS + r] = 1
                for i in range(ROWS):
                    a = r + 3 - i
                    if 0 <= a < 7:
                        main[i, a * 7 + e, e * MAIN + c * ROWS + r] = 1
            for k in range(6):
                own_side[[c, c + 8], e * SIDE + k * 8 + c] = 1
                row = k if k < 3 else k + ROWS
                for n, i in enumerate(EDGE_ROWS):
                    a = row - i
                    if 0 <= a < 7:
                        side[n, a * 7 + e, e * SIDE + k * 8 + c] = 1
    return tuple(np.asarray(v, dtype=BF16) for v in (main, side, own_main, own_side))


SPREAD_MAIN, SPREAD_SIDE, OWN_MAIN, OWN_SIDE = make_constants()


def dot32(a, b):
    return jnp.dot(a, b, preferred_element_type=F32)


def lanes_bf16(rows):
    return lax.broadcasted_iota(jnp.int32, (rows, LANES), 1).astype(F32).astype(BF16)


def pad_rows(v):
    return jnp.concatenate([v, jnp.zeros((PAD - C, LANES), v.dtype)], axis=0)


def band_kernel(taps_ref, spread_main_ref, spread_side_ref, own_main_ref, own_side_ref, w_in_ref, w_out_ref,
                main_ref, side_ref, w1_ref, w2_ref):
    def pair(spread_ref, own_ref, out_ref, p):
        depth = own_ref.shape[1]
        even = dot32(taps_ref[...], spread_ref[2 * p]).reshape(GROUPS, 8, depth)
        odd = dot32(taps_ref[...], spread_ref[2 * p + 1]).reshape(GROUPS, 8, depth)
        both = jnp.concatenate([even, odd], axis=1).astype(BF16)
        out_ref[:, pl.ds(pl.multiple_of(16 * p, 16), 16), :] = both * own_ref[...][None]

    def main_pair(p, carry):
        pair(spread_main_ref, own_main_ref, main_ref, p)
        return carry

    lax.fori_loop(0, ROWS // 2, main_pair, 0)
    for p in range(3):
        pair(spread_side_ref, own_side_ref, side_ref, p)
    w1_ref[...] = w_in_ref[...].T
    w2_ref[...] = w_out_ref[...].T


def make_bands(taps, w_in, w_out):
    return pl.pallas_call(
        band_kernel,
        out_shape=(
            jax.ShapeDtypeStruct((GROUPS, MAIN, 7 * MAIN), BF16),
            jax.ShapeDtypeStruct((GROUPS, SIDE, 7 * SIDE), BF16),
            jax.ShapeDtypeStruct((H, C), BF16),
            jax.ShapeDtypeStruct((C, H), BF16),
        ),
        in_specs=[VM] * 7,
        out_specs=(VM,) * 4,
        compiler_params=pltpu.CompilerParams(vmem_limit_bytes=20 * 2**20),
        cost_estimate=pl.CostEstimate(flops=2 * 16 * 256 * 256 * 1024, bytes_accessed=9_000_000, transcendentals=0),
    )(taps, jnp.asarray(SPREAD_MAIN), jnp.asarray(SPREAD_SIDE), jnp.asarray(OWN_MAIN), jnp.asarray(OWN_SIDE), w_in, w_out)


def emit_edges(tile_of, o_ref, out_ref, send_ref, top_ref, bot_ref):
    lane = lanes_bf16(ROWS)

    def some(first, count):
        v = tile_of(first, count)
        o_ref[pl.ds(first * ROWS, count * ROWS), :] = v.reshape(count * ROWS, LANES)
        v = v.astype(BF16)
        if out_ref is not None:
            out_ref[pl.ds(first, count)] = v
        packed = pltpu.roll(v[0], 3, 1)
        for c in range(1, count):
            packed = jnp.where(lane >= 8 * c, pltpu.roll(v[c], 8 * c + 3, 1), packed)
        return packed

    def step(q, carry):
        send_ref[pl.ds(pl.multiple_of(16 * q, 16), 16), :] = some(pl.multiple_of(16 * q, 16), 16)
        return carry

    lax.fori_loop(0, 12, step, 0)
    send_ref[192:208, :] = some(192, 8)
    wide = lax.broadcasted_iota(jnp.int32, (C, LANES), 1)
    corner = jnp.zeros((C, LANES), F32)
    for k in range(3):
        low = o_ref[pl.ds(k, C, stride=ROWS), :]
        corner = low_corner = jnp.where((wide >= 8 * k) & (wide < 64), pltpu.roll(low, 8 * k + 3, 1), corner)
        bot_ref[k] = low.astype(BF16)
    for k in range(3):
        high = o_ref[pl.ds(ROWS - 3 + k, C, stride=ROWS), :]
        corner = jnp.where(wide >= 64 + 8 * k, pltpu.roll(high, 64 + 8 * k + 3, 1), corner)
        high = high.astype(BF16)
        top_ref[k] = high
        send_ref[(2 + k) * PAD : (3 + k) * PAD, :] = pad_rows(high)
    send_ref[PAD : 2 * PAD, :] = pad_rows(corner.astype(BF16))


EDGE_SHAPES = (
    jax.ShapeDtypeStruct((SEND, LANES), BF16),
    jax.ShapeDtypeStruct((3, C, LANES), BF16),
    jax.ShapeDtypeStruct((3, C, LANES), BF16),
)


def first_kernel(x_ref, send_ref, top_ref, bot_ref, o_ref):
    emit_edges(lambda first, count: x_ref[pl.ds(first, count)].astype(F32), o_ref, None, send_ref, top_ref, bot_ref)


def first_edges(x):
    return pl.pallas_call(
        first_kernel,
        out_shape=EDGE_SHAPES,
        in_specs=[VM],
        out_specs=(VM,) * 3,
        scratch_shapes=[pltpu.VMEM((C * ROWS, LANES), F32)],
        compiler_params=pltpu.CompilerParams(vmem_limit_bytes=10 * 2**20),
    )(x)


def turn_kernel(scal_ref, west_ref, east_ref, top_ref, bot_ref, q1_ref, q2_ref, rows_ref):
    off, at_top, odd = scal_ref[0], scal_ref[1], scal_ref[2]
    lane = lax.broadcasted_iota(jnp.int32, (PAD, LANES), 1)
    corner = jnp.where(
        (lane & 7) < 3, west_ref[PAD : 2 * PAD, :].astype(F32), east_ref[PAD : 2 * PAD, :].astype(F32)
    ).astype(BF16)
    rows_ref[3] = corner

    @pl.when(at_top == 0)
    def _():
        for k in range(3):
            rows_ref[k] = pad_rows(top_ref[k])

    @pl.when(at_top == 1)
    def _():
        src = lax.broadcasted_iota(jnp.int32, (LANES, LANES), 0)
        dst = lax.broadcasted_iota(jnp.int32, (LANES, LANES), 1)
        slot = dst & 7
        col = jnp.where(slot < 3, slot - 3, slot + 125)
        used = slot < 6
        pick, pick_corner = [], []
        for part in range(3):
            local_col = src + 128 * (part - 1)
            pick.append(jnp.where(local_col + dst == off + 127, 1.0, 0.0).astype(BF16))
            hit = jnp.where(used & (local_col + col == off + 127), 1.0, 0.0)
            pick_corner.append([jnp.where(dst // 8 == k, hit, 0.0).astype(BF16) for k in range(3)])
        turned_corner = jnp.zeros((PAD, LANES), F32)
        for k in range(3):
            at = slice((4 - k) * PAD, (5 - k) * PAD)
            three = (west_ref[at, :], pad_rows(top_ref[2 - k]), east_ref[at, :])
            turned = jnp.zeros((PAD, LANES), F32)
            for part in range(3):
                turned += dot32(three[part], pick[part])
                turned_corner += dot32(three[part], pick_corner[part][k])
            rows_ref[k] = turned.astype(BF16)
        rows_ref[3] = turned_corner.astype(BF16)

    def put(up_ref, down_ref):
        for k in range(4):
            up_ref[k * PAD : (k + 1) * PAD, :] = rows_ref[k]
        for k in range(3):
            down_ref[k * PAD : (k + 1) * PAD, :] = pad_rows(bot_ref[k])
        down_ref[3 * PAD :, :] = corner

    pl.when(odd == 0)(lambda: put(q1_ref, q2_ref))
    pl.when(odd == 1)(lambda: put(q2_ref, q1_ref))


def turn_edges(scal, west, east, top, bot):
    return pl.pallas_call(
        turn_kernel,
        out_shape=(jax.ShapeDtypeStruct((SWAP, LANES), BF16),) * 2,
        in_specs=[SM] + [VM] * 4,
        out_specs=(VM, VM),
        scratch_shapes=[pltpu.VMEM((4, PAD, LANES), BF16)],
        compiler_params=pltpu.CompilerParams(vmem_limit_bytes=10 * 2**20),
    )(scal, west, east, top, bot)


def shifted(full, ends, lane, e):
    s = e - 3
    if s > 0:
        return pltpu.roll(jnp.where(lane < s, ends, full), LANES - s, 1)
    if s < 0:
        return pltpu.roll(jnp.where(lane >= LANES + s, ends, full), -s, 1)
    return full


UNROLL = 5


def conv_kernel(x_ref, band_ref, west_ref, east_ref, y_ref, side_ref, rhs_ref):
    lane = lanes_bf16(MAIN)
    tile_lane = lax.broadcasted_iota(jnp.int32, (ROWS, LANES), 1)
    for q in range(13):
        both = jnp.where(
            (tile_lane & 7) < 3,
            west_ref[16 * q : 16 * q + 16, :].astype(F32),
            east_ref[16 * q : 16 * q + 16, :].astype(F32),
        ).astype(BF16)
        for c in range(16 if q < 12 else 8):
            side_ref[16 * q + c] = pltpu.roll(both, LANES - (8 * c + 3), 1)

    def some(t, carry):
        for u in range(UNROLL):
            g = UNROLL * t + u
            full = x_ref[pl.ds(8 * g, 8)].reshape(MAIN, LANES)
            ends = side_ref[pl.ds(8 * g, 8)].reshape(MAIN, LANES)
            for e in range(7):
                rhs_ref[u, e * MAIN : (e + 1) * MAIN, :] = shifted(full, ends, lane, e)
            y_ref[:, g] = dot32(band_ref[g], rhs_ref[u]).reshape(ROWS, 8, LANES)
        return carry

    lax.fori_loop(0, GROUPS // UNROLL, some, 0)


def conv_own(x, band, west, east):
    return pl.pallas_call(
        conv_kernel,
        out_shape=jax.ShapeDtypeStruct((ROWS, GROUPS, 8, LANES), F32),
        in_specs=[VM] * 4,
        out_specs=VM,
        scratch_shapes=[
            pltpu.VMEM((C, ROWS, LANES), BF16),
            pltpu.VMEM((UNROLL, 7 * MAIN, LANES), BF16),
        ],
        compiler_params=pltpu.CompilerParams(vmem_limit_bytes=20 * 2**20),
        cost_estimate=pl.CostEstimate(flops=2 * 25 * 256 * 256 * 1024, bytes_accessed=9_000_000, transcendentals=0),
    )(x, band, west, east)


def gelu(h):
    return h * (0.5 + 0.5 * lax.erf(h * np.float32(0.5**0.5)))


def block_kernel(last, scal_ref, x_ref, y_ref, band_ref, r1_ref, r2_ref, w1_ref, w2_ref, gain_ref, mask_ref,
                 out_ref, *refs):
    edge_refs, (r32_ref, c32_ref, add_ref, o_ref) = refs[:-4], refs[-4:]
    odd = scal_ref[2]

    def put(below_ref, above_ref):
        for base, ref, lane in ((0, below_ref, 64), (3, above_ref, 0)):
            corner = ref[3 * PAD :, :].astype(F32)
            for k in range(3):
                r32_ref[base + k] = ref[k * PAD : (k + 1) * PAD, :].astype(F32).reshape(PAD // 8, 8, LANES)
                c32_ref[base + k] = pltpu.roll(corner, LANES - (lane + 8 * k + 3), 1).reshape(PAD // 8, 8, LANES)

    pl.when(odd == 0)(lambda: put(r2_ref, r1_ref))
    pl.when(odd == 1)(lambda: put(r1_ref, r2_ref))
    lane = lanes_bf16(SIDE)

    def halo(g, carry):
        full = r32_ref[:, g].reshape(SIDE, LANES).astype(BF16)
        ends = c32_ref[:, g].reshape(SIDE, LANES).astype(BF16)
        rhs = jnp.concatenate([shifted(full, ends, lane, e) for e in range(7)], axis=0)
        add_ref[:, g] = dot32(band_ref[g], rhs).reshape(6, 8, LANES)
        return carry

    lax.fori_loop(0, GROUPS, halo, 0, unroll=5)

    def mlp(i0, edges):
        parts = []
        for r in range(2):
            y = y_ref[i0 + r].reshape(C, LANES)
            if edges[r] is not None:
                y = y + add_ref[edges[r]].reshape(C, LANES)
            mean = jnp.sum(y, axis=0, keepdims=True) * np.float32(1 / C)
            y = y - mean
            var = jnp.sum(y * y, axis=0, keepdims=True) * np.float32(1 / C)
            parts.append((y * lax.rsqrt(var + EPS) * gain_ref[...]).astype(BF16))
        hidden = gelu(dot32(w1_ref[...], jnp.concatenate(parts, axis=1))).astype(BF16)
        o = dot32(w2_ref[...], hidden)
        for r in range(2):
            o_ref[pl.ds(i0 + r, C, stride=ROWS), :] = o[:, r * LANES : (r + 1) * LANES]

    mlp(0, (0, 1))
    mlp(2, (2, None))

    def inner(p, carry):
        mlp(2 * p, (None, None))
        return carry

    lax.fori_loop(2, 6, inner, 0)
    mlp(12, (None, 3))
    mlp(14, (4, 5))
    mask = mask_ref[...]

    def tile(first, count):
        o = o_ref[pl.ds(first * ROWS, count * ROWS), :].reshape(count, ROWS, LANES)
        return (x_ref[pl.ds(first, count)].astype(F32) + o) * mask[None]

    if last:
        def finish(g, carry):
            out_ref[pl.ds(8 * g, 8)] = tile(pl.multiple_of(8 * g, 8), 8).astype(BF16)
            return carry

        lax.fori_loop(0, GROUPS, finish, 0)
    else:
        emit_edges(tile, o_ref, out_ref, *edge_refs)


def run_block(last, scal, x, y, band, r1, r2, w1, w2, gain, mask):
    state = jax.ShapeDtypeStruct((C, ROWS, LANES), BF16)
    shapes = (state,) if last else (state,) + EDGE_SHAPES
    return pl.pallas_call(
        lambda *refs: block_kernel(last, *refs),
        out_shape=shapes,
        in_specs=[SM] + [VM] * 9,
        out_specs=(VM,) * len(shapes),
        scratch_shapes=[
            pltpu.VMEM((6, PAD // 8, 8, LANES), F32),
            pltpu.VMEM((6, PAD // 8, 8, LANES), F32),
            pltpu.VMEM((6, GROUPS, 8, LANES), F32),
            pltpu.VMEM((C * ROWS, LANES), F32),
        ],
        compiler_params=pltpu.CompilerParams(vmem_limit_bytes=20 * 2**20),
    )(scal, x, y, band, r1, r2, w1, w2, gain, mask)


def local(field, land_mask, fold_partner, dw_kernel, norm_gain, w_in, w_out):
    zonal = lax.axis_size("zonal")
    merid = lax.axis_size("merid")
    total = fold_partner.shape[0]
    start = jnp.mod(fold_partner[0] - (LANES // 2 - 1), total)
    turn = start // LANES
    level = lax.axis_index("merid")
    at_top = (level == merid - 1).astype(jnp.int32)
    scal = jnp.stack([start % LANES - LANES // 2, at_top, level % 2])
    place = lambda m, z: z * merid + m
    even_pairs = [(m, m ^ 1) for m in range(merid)]
    odd_pairs = [(m, ((m - 1) ^ 1) + 1) for m in range(1, merid - 1)]

    def branch_of(shift):
        def branch(q1, q2, x, band, west, east):
            pairs = [(place(m, z), place(n, z)) for m, n in odd_pairs for z in range(zonal)]
            pairs += [(place(merid - 1, z), place(merid - 1, (shift - z) % zonal)) for z in range(zonal)]
            r2 = lax.ppermute(q2, ("zonal", "merid"), pairs)
            r1 = lax.ppermute(q1, "merid", even_pairs)
            return r1, r2, conv_own(x, band, west, east)

        return branch

    branches = [branch_of(t) for t in range(zonal)]
    taps = jnp.pad(dw_kernel.reshape(BLOCKS, C, 49), ((0, 0), (0, 0), (0, 15)))
    gains = jnp.broadcast_to(norm_gain.astype(F32)[:, :, None], (BLOCKS, C, LANES))
    mask = land_mask.astype(F32)
    x = field
    send, top, bot = first_edges(x)
    for b in range(BLOCKS):
        west = lax.ppermute(send, "zonal", [(z, (z + 1) % zonal) for z in range(zonal)])
        east = lax.ppermute(send, "zonal", [((z + 1) % zonal, z) for z in range(zonal)])
        band_main, band_side, w1, w2 = make_bands(taps[b], w_in[b], w_out[b])
        q1, q2 = turn_edges(scal, west, east, top, bot)
        r1, r2, y = lax.switch(turn, branches, q1, q2, x, band_main, west, east)
        last = b == BLOCKS - 1
        x, *edges = run_block(last, scal, x, y, band_side, r1, r2, w1, w2, gains[b], mask)
        if not last:
            send, top, bot = edges
    return x


def solution(mesh):
    in_specs = (P(None, "merid", "zonal"), P("merid", "zonal"), P(), P(), P(), P(), P())
    out_specs = P(None, "merid", "zonal")
    return jax.shard_map(local, mesh=mesh, in_specs=in_specs, out_specs=out_specs, check_vma=False)
```

```python
import jax
import jax.numpy as jnp
import numpy as np
from jax import lax
from jax.experimental import pallas as pl
from jax.experimental.pallas import tpu as pltpu
from jax.sharding import PartitionSpec as P

BLOCKS = 3
C = 200
PAD = 208
H = 800
ROWS = 16
LANES = 128
GROUPS = C // 8
MAIN = 8 * ROWS
SIDE = 8 * 6
EPS = 1e-05
F32 = jnp.float32
BF16 = jnp.bfloat16
EDGE_ROWS = (0, 1, 2, 13, 14, 15)
SEND = 5 * PAD
SWAP = 4 * PAD
VM = pl.BlockSpec(memory_space=pltpu.VMEM)
SM = pl.BlockSpec(memory_space=pltpu.SMEM)


def dot32(a, b):
    return jnp.dot(a, b, preferred_element_type=F32)


def lanes_bf16(rows):
    return lax.broadcasted_iota(jnp.int32, (rows, LANES), 1).astype(F32).astype(BF16)


def pad_rows(v):
    return jnp.concatenate([v, jnp.zeros((PAD - C, LANES), v.dtype)], axis=0)


def band_kernel(block, taps_ref, w_in_ref, gain_ref, main_ref, side_ref, w1_ref, gains_ref):
    rows = [jnp.concatenate([taps_ref[block, a].astype(F32), jnp.zeros((1, C), F32)], axis=0) for a in range(7)]
    taps = jnp.concatenate(rows + [jnp.zeros((8, C), F32)], axis=0).T.astype(BF16)

    def place(first, second, tap_of, own, out_ref, at):
        depth = own.shape[1]
        tap = lax.broadcasted_iota(jnp.int32, (64, depth), 0)
        both = []
        for i in (first, second):
            spread = jnp.where(tap == tap_of(i), 1.0, 0.0).astype(BF16)
            both.append(dot32(taps, spread).reshape(GROUPS, 8, depth))
        both = jnp.concatenate(both, axis=1).astype(BF16)
        out_ref[:, pl.ds(at, 16), :] = both * own[None]

    lane = lax.broadcasted_iota(jnp.int32, (1, 7 * MAIN), 1)
    e, row = lane // MAIN, lane % ROWS

    def main_tap(i):
        a = row + 3 - i
        return jnp.where((a >= 0) & (a < 7), 8 * a + e, -1)

    wide = lax.broadcasted_iota(jnp.int32, (16, 7 * MAIN), 1)
    high = lax.broadcasted_iota(jnp.int32, (16, 7 * MAIN), 0)
    own_main = jnp.where((wide % MAIN) // ROWS == high % 8, 1.0, 0.0).astype(BF16)

    def main_pair(p, carry):
        place(2 * p, 2 * p + 1, main_tap, own_main, main_ref, pl.multiple_of(16 * p, 16))
        return carry

    lax.fori_loop(0, ROWS // 2, main_pair, 0)
    lane = lax.broadcasted_iota(jnp.int32, (1, 7 * SIDE), 1)
    e_side, slot = lane // SIDE, lane % SIDE
    k = slot // 8
    row_side = jnp.where(k < 3, k, k + ROWS)

    def side_tap(i):
        a = row_side - i
        return jnp.where((a >= 0) & (a < 7), 8 * a + e_side, -1)

    wide = lax.broadcasted_iota(jnp.int32, (16, 7 * SIDE), 1)
    high = lax.broadcasted_iota(jnp.int32, (16, 7 * SIDE), 0)
    own_side = jnp.where(wide % 8 == high % 8, 1.0, 0.0).astype(BF16)
    for p in range(3):
        place(EDGE_ROWS[2 * p], EDGE_ROWS[2 * p + 1], side_tap, own_side, side_ref, 16 * p)
    w1_ref[...] = w_in_ref[block].T
    gain = gain_ref[...].astype(F32)[block : block + 1]
    gains_ref[...] = jnp.broadcast_to(gain, (LANES, C)).T


def make_bands(block, taps, w_in, gain):
    return pl.pallas_call(
        lambda *refs: band_kernel(block, *refs),
        out_shape=(
            jax.ShapeDtypeStruct((GROUPS, MAIN, 7 * MAIN), BF16),
            jax.ShapeDtypeStruct((GROUPS, SIDE, 7 * SIDE), BF16),
            jax.ShapeDtypeStruct((H, C), BF16),
            jax.ShapeDtypeStruct((C, LANES), F32),
        ),
        in_specs=[VM] * 3,
        out_specs=(VM,) * 4,
        compiler_params=pltpu.CompilerParams(vmem_limit_bytes=20 * 2**20),
        cost_estimate=pl.CostEstimate(flops=2 * 16 * 256 * 256 * 1024, bytes_accessed=9_000_000, transcendentals=0),
    )(taps, w_in, gain)


def emit_edges(tile_of, o_ref, out_ref, send_ref, top_ref, bot_ref):
    lane = lanes_bf16(ROWS)

    def some(first, count):
        v = tile_of(first, count)
        o_ref[pl.ds(first * ROWS, count * ROWS), :] = v.reshape(count * ROWS, LANES)
        v = v.astype(BF16)
        if out_ref is not None:
            out_ref[pl.ds(first, count)] = v
        packed = pltpu.roll(v[0], 3, 1)
        for c in range(1, count):
            packed = jnp.where(lane >= 8 * c, pltpu.roll(v[c], 8 * c + 3, 1), packed)
        return packed

    def step(q, carry):
        send_ref[pl.ds(pl.multiple_of(16 * q, 16), 16), :] = some(pl.multiple_of(16 * q, 16), 16)
        return carry

    lax.fori_loop(0, 12, step, 0)
    send_ref[192:208, :] = some(192, 8)
    wide = lax.broadcasted_iota(jnp.int32, (C, LANES), 1)
    corner = jnp.zeros((C, LANES), F32)
    for k in range(3):
        low = o_ref[pl.ds(k, C, stride=ROWS), :]
        corner = jnp.where((wide >= 8 * k) & (wide < 64), pltpu.roll(low, 8 * k + 3, 1), corner)
        bot_ref[k] = low.astype(BF16)
    for k in range(3):
        high = o_ref[pl.ds(ROWS - 3 + k, C, stride=ROWS), :]
        corner = jnp.where(wide >= 64 + 8 * k, pltpu.roll(high, 64 + 8 * k + 3, 1), corner)
        high = high.astype(BF16)
        top_ref[k] = high
        send_ref[(2 + k) * PAD : (3 + k) * PAD, :] = pad_rows(high)
    send_ref[PAD : 2 * PAD, :] = pad_rows(corner.astype(BF16))


EDGE_SHAPES = (
    jax.ShapeDtypeStruct((SEND, LANES), BF16),
    jax.ShapeDtypeStruct((3, C, LANES), BF16),
    jax.ShapeDtypeStruct((3, C, LANES), BF16),
)


def first_kernel(x_ref, send_ref, top_ref, bot_ref, o_ref):
    emit_edges(lambda first, count: x_ref[pl.ds(first, count)].astype(F32), o_ref, None, send_ref, top_ref, bot_ref)


def first_edges(x):
    return pl.pallas_call(
        first_kernel,
        out_shape=EDGE_SHAPES,
        in_specs=[VM],
        out_specs=(VM,) * 3,
        scratch_shapes=[pltpu.VMEM((C * ROWS, LANES), F32)],
        compiler_params=pltpu.CompilerParams(vmem_limit_bytes=10 * 2**20),
    )(x)


def place_on_mesh():
    level = lax.axis_index("merid")
    return level == lax.axis_size("merid") - 1, level % 2


def turn_kernel(fold_ref, west_ref, east_ref, top_ref, bot_ref, q1_ref, q2_ref, rows_ref):
    at_top, odd = place_on_mesh()
    off = (fold_ref[0] + (LANES // 2 + 1)) % LANES - LANES // 2
    lane = lax.broadcasted_iota(jnp.int32, (PAD, LANES), 1)
    corner = jnp.where(
        (lane & 7) < 3, west_ref[PAD : 2 * PAD, :].astype(F32), east_ref[PAD : 2 * PAD, :].astype(F32)
    ).astype(BF16)
    rows_ref[3] = corner

    @pl.when(jnp.logical_not(at_top))
    def _():
        for k in range(3):
            rows_ref[k] = pad_rows(top_ref[k])

    @pl.when(at_top)
    def _():
        src = lax.broadcasted_iota(jnp.int32, (LANES, LANES), 0)
        dst = lax.broadcasted_iota(jnp.int32, (LANES, LANES), 1)
        slot = dst & 7
        col = jnp.where(slot < 3, slot - 3, slot + 125)
        used = slot < 6
        pick, pick_corner = [], []
        for part in range(3):
            local_col = src + 128 * (part - 1)
            pick.append(jnp.where(local_col + dst == off + 127, 1.0, 0.0).astype(BF16))
            hit = jnp.where(used & (local_col + col == off + 127), 1.0, 0.0)
            pick_corner.append([jnp.where(dst // 8 == k, hit, 0.0).astype(BF16) for k in range(3)])
        turned_corner = jnp.zeros((PAD, LANES), F32)
        for k in range(3):
            at = slice((4 - k) * PAD, (5 - k) * PAD)
            three = (west_ref[at, :], pad_rows(top_ref[2 - k]), east_ref[at, :])
            turned = jnp.zeros((PAD, LANES), F32)
            for part in range(3):
                turned += dot32(three[part], pick[part])
                turned_corner += dot32(three[part], pick_corner[part][k])
            rows_ref[k] = turned.astype(BF16)
        rows_ref[3] = turned_corner.astype(BF16)

    def put(up_ref, down_ref):
        for k in range(4):
            up_ref[k * PAD : (k + 1) * PAD, :] = rows_ref[k]
        for k in range(3):
            down_ref[k * PAD : (k + 1) * PAD, :] = pad_rows(bot_ref[k])
        down_ref[3 * PAD :, :] = corner

    pl.when(odd == 0)(lambda: put(q1_ref, q2_ref))
    pl.when(odd == 1)(lambda: put(q2_ref, q1_ref))


def turn_edges(fold, west, east, top, bot):
    return pl.pallas_call(
        turn_kernel,
        out_shape=(jax.ShapeDtypeStruct((SWAP, LANES), BF16),) * 2,
        in_specs=[SM] + [VM] * 4,
        out_specs=(VM, VM),
        scratch_shapes=[pltpu.VMEM((4, PAD, LANES), BF16)],
        compiler_params=pltpu.CompilerParams(vmem_limit_bytes=10 * 2**20),
    )(fold, west, east, top, bot)


def shifted(full, ends, lane, e):
    s = e - 3
    if s > 0:
        return pltpu.roll(jnp.where(lane < s, ends, full), LANES - s, 1)
    if s < 0:
        return pltpu.roll(jnp.where(lane >= LANES + s, ends, full), -s, 1)
    return full


UNROLL = 5


def conv_kernel(x_ref, band_ref, west_ref, east_ref, y_ref, side_ref, rhs_ref):
    lane = lanes_bf16(MAIN)
    tile_lane = lax.broadcasted_iota(jnp.int32, (ROWS, LANES), 1)
    for q in range(13):
        both = jnp.where(
            (tile_lane & 7) < 3,
            west_ref[16 * q : 16 * q + 16, :].astype(F32),
            east_ref[16 * q : 16 * q + 16, :].astype(F32),
        ).astype(BF16)
        for c in range(16 if q < 12 else 8):
            side_ref[16 * q + c] = pltpu.roll(both, LANES - (8 * c + 3), 1)

    def some(t, carry):
        for u in range(UNROLL):
            g = UNROLL * t + u
            full = x_ref[pl.ds(8 * g, 8)].reshape(MAIN, LANES)
            ends = side_ref[pl.ds(8 * g, 8)].reshape(MAIN, LANES)
            for e in range(7):
                rhs_ref[u, e * MAIN : (e + 1) * MAIN, :] = shifted(full, ends, lane, e)
            y_ref[:, g] = dot32(band_ref[g], rhs_ref[u]).reshape(ROWS, 8, LANES)
        return carry

    lax.fori_loop(0, GROUPS // UNROLL, some, 0)


def conv_own(x, band, west, east):
    return pl.pallas_call(
        conv_kernel,
        out_shape=jax.ShapeDtypeStruct((ROWS, GROUPS, 8, LANES), F32),
        in_specs=[VM] * 4,
        out_specs=VM,
        scratch_shapes=[
            pltpu.VMEM((C, ROWS, LANES), BF16),
            pltpu.VMEM((UNROLL, 7 * MAIN, LANES), BF16),
        ],
        compiler_params=pltpu.CompilerParams(vmem_limit_bytes=20 * 2**20),
        cost_estimate=pl.CostEstimate(flops=2 * 25 * 256 * 256 * 1024, bytes_accessed=9_000_000, transcendentals=0),
    )(x, band, west, east)


def gelu(h):
    return h * (0.5 + 0.5 * lax.erf(h * np.float32(0.5**0.5)))


def block_kernel(last, block, x_ref, y_ref, band_ref, r1_ref, r2_ref, w1_ref, w2_ref, gain_ref, mask_ref,
                 out_ref, *refs):
    edge_refs, (r32_ref, c32_ref, add_ref, o_ref) = refs[:-4], refs[-4:]
    odd = place_on_mesh()[1]

    def put(below_ref, above_ref):
        for base, ref, lane in ((0, below_ref, 64), (3, above_ref, 0)):
            corner = ref[3 * PAD :, :].astype(F32)
            for k in range(3):
                r32_ref[base + k] = ref[k * PAD : (k + 1) * PAD, :].astype(F32).reshape(PAD // 8, 8, LANES)
                c32_ref[base + k] = pltpu.roll(corner, LANES - (lane + 8 * k + 3), 1).reshape(PAD // 8, 8, LANES)

    pl.when(odd == 0)(lambda: put(r2_ref, r1_ref))
    pl.when(odd == 1)(lambda: put(r1_ref, r2_ref))
    lane = lanes_bf16(SIDE)

    def halo(g, carry):
        full = r32_ref[:, g].reshape(SIDE, LANES).astype(BF16)
        ends = c32_ref[:, g].reshape(SIDE, LANES).astype(BF16)
        rhs = jnp.concatenate([shifted(full, ends, lane, e) for e in range(7)], axis=0)
        add_ref[:, g] = dot32(band_ref[g], rhs).reshape(6, 8, LANES)
        return carry

    lax.fori_loop(0, GROUPS, halo, 0, unroll=5)

    def mlp(i0, edges):
        parts = []
        for r in range(2):
            y = y_ref[i0 + r].reshape(C, LANES)
            if edges[r] is not None:
                y = y + add_ref[edges[r]].reshape(C, LANES)
            mean = jnp.sum(y, axis=0, keepdims=True) * np.float32(1 / C)
            y = y - mean
            var = jnp.sum(y * y, axis=0, keepdims=True) * np.float32(1 / C)
            parts.append((y * lax.rsqrt(var + EPS) * gain_ref[...]).astype(BF16))
        hidden = gelu(dot32(w1_ref[...], jnp.concatenate(parts, axis=1))).astype(BF16)
        o = dot32(w2_ref[block], hidden)
        for r in range(2):
            o_ref[pl.ds(i0 + r, C, stride=ROWS), :] = o[:, r * LANES : (r + 1) * LANES]

    mlp(0, (0, 1))
    mlp(2, (2, None))

    def inner(p, carry):
        mlp(2 * p, (None, None))
        return carry

    lax.fori_loop(2, 6, inner, 0)
    mlp(12, (None, 3))
    mlp(14, (4, 5))
    mask = mask_ref[...].astype(F32)

    def tile(first, count):
        o = o_ref[pl.ds(first * ROWS, count * ROWS), :].reshape(count, ROWS, LANES)
        return (x_ref[pl.ds(first, count)].astype(F32) + o) * mask[None]

    if last:
        def finish(g, carry):
            out_ref[pl.ds(8 * g, 8)] = tile(pl.multiple_of(8 * g, 8), 8).astype(BF16)
            return carry

        lax.fori_loop(0, GROUPS, finish, 0)
    else:
        emit_edges(tile, o_ref, out_ref, *edge_refs)


def run_block(last, block, x, y, band, r1, r2, w1, w2, gain, mask):
    state = jax.ShapeDtypeStruct((C, ROWS, LANES), BF16)
    shapes = (state,) if last else (state,) + EDGE_SHAPES
    return pl.pallas_call(
        lambda *refs: block_kernel(last, block, *refs),
        out_shape=shapes,
        in_specs=[VM] * 9,
        out_specs=(VM,) * len(shapes),
        scratch_shapes=[
            pltpu.VMEM((6, PAD // 8, 8, LANES), F32),
            pltpu.VMEM((6, PAD // 8, 8, LANES), F32),
            pltpu.VMEM((6, GROUPS, 8, LANES), F32),
            pltpu.VMEM((C * ROWS, LANES), F32),
        ],
        compiler_params=pltpu.CompilerParams(vmem_limit_bytes=20 * 2**20),
    )(x, y, band, r1, r2, w1, w2, gain, mask)


def local(field, land_mask, fold_partner, dw_kernel, norm_gain, w_in, w_out):
    zonal = lax.axis_size("zonal")
    merid = lax.axis_size("merid")
    total = fold_partner.shape[0]
    start = jnp.mod(fold_partner[0] - (LANES // 2 - 1), total)
    turn = start // LANES
    place = lambda m, z: z * merid + m
    even_pairs = [(m, m ^ 1) for m in range(merid)]
    odd_pairs = [(m, ((m - 1) ^ 1) + 1) for m in range(1, merid - 1)]

    def branch_of(shift):
        def branch(q2):
            pairs = [(place(m, z), place(n, z)) for m, n in odd_pairs for z in range(zonal)]
            pairs += [(place(merid - 1, z), place(merid - 1, (shift - z) % zonal)) for z in range(zonal)]
            return lax.ppermute(q2, ("zonal", "merid"), pairs)

        return branch

    branches = [branch_of(t) for t in range(zonal)]
    taps = jnp.transpose(dw_kernel, (0, 2, 3, 1))
    w2 = jnp.swapaxes(w_out, 1, 2)
    x = field
    send, top, bot = first_edges(x)
    for b in range(BLOCKS):
        west = lax.ppermute(send, "zonal", [(z, (z + 1) % zonal) for z in range(zonal)])
        east = lax.ppermute(send, "zonal", [((z + 1) % zonal, z) for z in range(zonal)])
        band_main, band_side, w1, gain = make_bands(b, taps, w_in, norm_gain)
        q1, q2 = turn_edges(fold_partner, west, east, top, bot)
        r1 = lax.ppermute(q1, "merid", even_pairs)
        y = conv_own(x, band_main, west, east)
        r2 = lax.switch(turn, branches, q2)
        last = b == BLOCKS - 1
        x, *edges = run_block(last, b, x, y, band_side, r1, r2, w1, w2, gain, land_mask)
        if not last:
            send, top, bot = edges
    return x


def solution(mesh):
    in_specs = (P(None, "merid", "zonal"), P("merid", "zonal"), P(), P(), P(), P(), P())
    out_specs = P(None, "merid", "zonal")
    return jax.shard_map(local, mesh=mesh, in_specs=in_specs, out_specs=out_specs, check_vma=False)
```

```python
import jax
import jax.numpy as jnp
import numpy as np
from jax import lax
from jax.experimental import pallas as pl
from jax.experimental.pallas import tpu as pltpu
from jax.sharding import PartitionSpec as P

BLOCKS = 3
C = 200
PAD = 208
H = 800
ROWS = 16
LANES = 128
GROUPS = C // 8
MAIN = 8 * ROWS
SIDE = 8 * 6
EPS = 1e-05
F32 = jnp.float32
BF16 = jnp.bfloat16
EDGE_ROWS = (0, 1, 2, 13, 14, 15)
SEND = 5 * PAD
SWAP = 4 * PAD
VM = pl.BlockSpec(memory_space=pltpu.VMEM)
SM = pl.BlockSpec(memory_space=pltpu.SMEM)


def dot32(a, b):
    return jnp.dot(a, b, preferred_element_type=F32)


def lanes_bf16(rows):
    return lax.broadcasted_iota(jnp.int32, (rows, LANES), 1).astype(F32).astype(BF16)


def pad_rows(v):
    return jnp.concatenate([v, jnp.zeros((PAD - C, LANES), v.dtype)], axis=0)


def band_kernel(block, taps_ref, w_in_ref, gain_ref, main_ref, side_ref, w1_ref, gains_ref):
    rows = [jnp.concatenate([taps_ref[block, a].astype(F32), jnp.zeros((1, C), F32)], axis=0) for a in range(7)]
    taps = jnp.concatenate(rows + [jnp.zeros((8, C), F32)], axis=0).T.astype(BF16)

    def place(first, second, tap_of, own, out_ref, at):
        depth = own.shape[1]
        tap = lax.broadcasted_iota(jnp.int32, (64, depth), 0)
        both = []
        for i in (first, second):
            spread = jnp.where(tap == tap_of(i), 1.0, 0.0).astype(BF16)
            both.append(dot32(taps, spread).reshape(GROUPS, 8, depth))
        both = jnp.concatenate(both, axis=1).astype(BF16)
        out_ref[:, pl.ds(at, 16), :] = both * own[None]

    lane = lax.broadcasted_iota(jnp.int32, (1, 7 * MAIN), 1)
    e, row = lane // MAIN, lane % ROWS

    def main_tap(i):
        a = row + 3 - i
        return jnp.where((a >= 0) & (a < 7), 8 * a + e, -1)

    wide = lax.broadcasted_iota(jnp.int32, (16, 7 * MAIN), 1)
    high = lax.broadcasted_iota(jnp.int32, (16, 7 * MAIN), 0)
    own_main = jnp.where((wide % MAIN) // ROWS == high % 8, 1.0, 0.0).astype(BF16)

    def main_pair(p, carry):
        place(2 * p, 2 * p + 1, main_tap, own_main, main_ref, pl.multiple_of(16 * p, 16))
        return carry

    lax.fori_loop(0, ROWS // 2, main_pair, 0)
    lane = lax.broadcasted_iota(jnp.int32, (1, 7 * SIDE), 1)
    e_side, slot = lane // SIDE, lane % SIDE
    k = slot // 8
    row_side = jnp.where(k < 3, k, k + ROWS)

    def side_tap(i):
        a = row_side - i
        return jnp.where((a >= 0) & (a < 7), 8 * a + e_side, -1)

    wide = lax.broadcasted_iota(jnp.int32, (16, 7 * SIDE), 1)
    high = lax.broadcasted_iota(jnp.int32, (16, 7 * SIDE), 0)
    own_side = jnp.where(wide % 8 == high % 8, 1.0, 0.0).astype(BF16)
    for p in range(3):
        place(EDGE_ROWS[2 * p], EDGE_ROWS[2 * p + 1], side_tap, own_side, side_ref, 16 * p)
    w1_ref[...] = w_in_ref[block].T
    gain = gain_ref[...].astype(F32)[block : block + 1]
    gains_ref[...] = jnp.broadcast_to(gain, (LANES, C)).T


def make_bands(block, taps, w_in, gain):
    return pl.pallas_call(
        lambda *refs: band_kernel(block, *refs),
        out_shape=(
            jax.ShapeDtypeStruct((GROUPS, MAIN, 7 * MAIN), BF16),
            jax.ShapeDtypeStruct((GROUPS, SIDE, 7 * SIDE), BF16),
            jax.ShapeDtypeStruct((H, C), BF16),
            jax.ShapeDtypeStruct((C, LANES), F32),
        ),
        in_specs=[VM] * 3,
        out_specs=(VM,) * 4,
        compiler_params=pltpu.CompilerParams(vmem_limit_bytes=20 * 2**20),
        cost_estimate=pl.CostEstimate(flops=2 * 16 * 256 * 256 * 1024, bytes_accessed=9_000_000, transcendentals=0),
    )(taps, w_in, gain)


def emit_edges(tile_of, o_ref, out_ref, send_ref, top_ref, bot_ref):
    lane = lanes_bf16(ROWS)

    def some(first, count):
        v = tile_of(first, count)
        o_ref[pl.ds(first * ROWS, count * ROWS), :] = v.reshape(count * ROWS, LANES)
        v = v.astype(BF16)
        if out_ref is not None:
            out_ref[pl.ds(first, count)] = v
        packed = pltpu.roll(v[0], 3, 1)
        for c in range(1, count):
            packed = jnp.where(lane >= 8 * c, pltpu.roll(v[c], 8 * c + 3, 1), packed)
        return packed

    def step(q, carry):
        send_ref[pl.ds(pl.multiple_of(16 * q, 16), 16), :] = some(pl.multiple_of(16 * q, 16), 16)
        return carry

    lax.fori_loop(0, 12, step, 0)
    send_ref[192:208, :] = some(192, 8)
    wide = lax.broadcasted_iota(jnp.int32, (C, LANES), 1)
    corner = jnp.zeros((C, LANES), F32)
    for k in range(3):
        low = o_ref[pl.ds(k, C, stride=ROWS), :]
        corner = jnp.where((wide >= 8 * k) & (wide < 64), pltpu.roll(low, 8 * k + 3, 1), corner)
        bot_ref[k] = low.astype(BF16)
    for k in range(3):
        high = o_ref[pl.ds(ROWS - 3 + k, C, stride=ROWS), :]
        corner = jnp.where(wide >= 64 + 8 * k, pltpu.roll(high, 64 + 8 * k + 3, 1), corner)
        high = high.astype(BF16)
        top_ref[k] = high
        send_ref[(2 + k) * PAD : (3 + k) * PAD, :] = pad_rows(high)
    send_ref[PAD : 2 * PAD, :] = pad_rows(corner.astype(BF16))


EDGE_SHAPES = (
    jax.ShapeDtypeStruct((SEND, LANES), BF16),
    jax.ShapeDtypeStruct((3, C, LANES), BF16),
    jax.ShapeDtypeStruct((3, C, LANES), BF16),
)


def first_kernel(x_ref, send_ref, top_ref, bot_ref, o_ref):
    emit_edges(lambda first, count: x_ref[pl.ds(first, count)].astype(F32), o_ref, None, send_ref, top_ref, bot_ref)


def first_edges(x):
    return pl.pallas_call(
        first_kernel,
        out_shape=EDGE_SHAPES,
        in_specs=[VM],
        out_specs=(VM,) * 3,
        scratch_shapes=[pltpu.VMEM((C * ROWS, LANES), F32)],
        compiler_params=pltpu.CompilerParams(vmem_limit_bytes=10 * 2**20),
    )(x)


def place_on_mesh():
    level = lax.axis_index("merid")
    return level == lax.axis_size("merid") - 1, level % 2


def turn_kernel(fold_ref, west_ref, east_ref, top_ref, bot_ref, q1_ref, q2_ref, rows_ref):
    at_top, odd = place_on_mesh()
    off = (fold_ref[0] + (LANES // 2 + 1)) % LANES - LANES // 2
    lane = lax.broadcasted_iota(jnp.int32, (PAD, LANES), 1)
    corner = jnp.where(
        (lane & 7) < 3, west_ref[PAD : 2 * PAD, :].astype(F32), east_ref[PAD : 2 * PAD, :].astype(F32)
    ).astype(BF16)
    rows_ref[3] = corner

    @pl.when(jnp.logical_not(at_top))
    def _():
        for k in range(3):
            rows_ref[k] = pad_rows(top_ref[k])

    @pl.when(at_top)
    def _():
        src = lax.broadcasted_iota(jnp.int32, (LANES, LANES), 0)
        dst = lax.broadcasted_iota(jnp.int32, (LANES, LANES), 1)
        slot = dst & 7
        col = jnp.where(slot < 3, slot - 3, slot + 125)
        used = slot < 6
        pick, pick_corner = [], []
        for part in range(3):
            local_col = src + 128 * (part - 1)
            pick.append(jnp.where(local_col + dst == off + 127, 1.0, 0.0).astype(BF16))
            hit = jnp.where(used & (local_col + col == off + 127), 1.0, 0.0)
            pick_corner.append([jnp.where(dst // 8 == k, hit, 0.0).astype(BF16) for k in range(3)])
        turned_corner = jnp.zeros((PAD, LANES), F32)
        for k in range(3):
            at = slice((4 - k) * PAD, (5 - k) * PAD)
            three = (west_ref[at, :], pad_rows(top_ref[2 - k]), east_ref[at, :])
            turned = jnp.zeros((PAD, LANES), F32)
            for part in range(3):
                turned += dot32(three[part], pick[part])
                turned_corner += dot32(three[part], pick_corner[part][k])
            rows_ref[k] = turned.astype(BF16)
        rows_ref[3] = turned_corner.astype(BF16)

    def put(up_ref, down_ref):
        for k in range(4):
            up_ref[k * PAD : (k + 1) * PAD, :] = rows_ref[k]
        for k in range(3):
            down_ref[k * PAD : (k + 1) * PAD, :] = pad_rows(bot_ref[k])
        down_ref[3 * PAD :, :] = corner

    pl.when(odd == 0)(lambda: put(q1_ref, q2_ref))
    pl.when(odd == 1)(lambda: put(q2_ref, q1_ref))


def turn_edges(fold, west, east, top, bot):
    return pl.pallas_call(
        turn_kernel,
        out_shape=(jax.ShapeDtypeStruct((SWAP, LANES), BF16),) * 2,
        in_specs=[SM] + [VM] * 4,
        out_specs=(VM, VM),
        scratch_shapes=[pltpu.VMEM((4, PAD, LANES), BF16)],
        compiler_params=pltpu.CompilerParams(vmem_limit_bytes=10 * 2**20),
    )(fold, west, east, top, bot)


def shifted(full, ends, lane, e):
    s = e - 3
    if s > 0:
        return pltpu.roll(jnp.where(lane < s, ends, full), LANES - s, 1)
    if s < 0:
        return pltpu.roll(jnp.where(lane >= LANES + s, ends, full), -s, 1)
    return full


def conv_kernel(x_ref, band_ref, west_ref, east_ref, y_ref, rhs_ref):
    lane = lanes_bf16(MAIN)
    tile_lane = lax.broadcasted_iota(jnp.int32, (ROWS, LANES), 1)

    def group(g, q, odd):
        at = pl.ds(pl.multiple_of(16 * q, 16), 16)
        both = jnp.where((tile_lane & 7) < 3, west_ref[at, :].astype(F32), east_ref[at, :].astype(F32)).astype(BF16)
        ends = [pltpu.roll(both, LANES - (8 * (c + 8 * odd) + 3), 1) for c in range(8)]
        ends = jnp.concatenate(ends, axis=0)
        full = x_ref[pl.ds(8 * g, 8)].reshape(MAIN, LANES)
        for e in range(7):
            rhs_ref[odd, e * MAIN : (e + 1) * MAIN, :] = shifted(full, ends, lane, e)
        y_ref[:, g] = dot32(band_ref[g], rhs_ref[odd]).reshape(ROWS, 8, LANES)

    def some(q, carry):
        group(2 * q, q, 0)
        group(2 * q + 1, q, 1)
        return carry

    lax.fori_loop(0, GROUPS // 2, some, 0)
    group(GROUPS - 1, GROUPS // 2, 0)


def conv_own(x, band, west, east):
    return pl.pallas_call(
        conv_kernel,
        out_shape=jax.ShapeDtypeStruct((ROWS, GROUPS, 8, LANES), F32),
        in_specs=[VM] * 4,
        out_specs=VM,
        scratch_shapes=[
            pltpu.VMEM((2, 7 * MAIN, LANES), BF16),
        ],
        compiler_params=pltpu.CompilerParams(vmem_limit_bytes=20 * 2**20),
        cost_estimate=pl.CostEstimate(flops=2 * 25 * 256 * 256 * 1024, bytes_accessed=9_000_000, transcendentals=0),
    )(x, band, west, east)


def gelu(h):
    return h * (0.5 + 0.5 * lax.erf(h * np.float32(0.5**0.5)))


def block_kernel(last, block, x_ref, y_ref, band_ref, r1_ref, r2_ref, w1_ref, w2_ref, gain_ref, mask_ref,
                 out_ref, *refs):
    edge_refs, (r32_ref, c32_ref, add_ref, o_ref) = refs[:-4], refs[-4:]
    odd = place_on_mesh()[1]

    def put(below_ref, above_ref):
        for base, ref, lane in ((0, below_ref, 64), (3, above_ref, 0)):
            corner = ref[3 * PAD :, :].astype(F32)
            for k in range(3):
                r32_ref[base + k] = ref[k * PAD : (k + 1) * PAD, :].astype(F32).reshape(PAD // 8, 8, LANES)
                c32_ref[base + k] = pltpu.roll(corner, LANES - (lane + 8 * k + 3), 1).reshape(PAD // 8, 8, LANES)

    pl.when(odd == 0)(lambda: put(r2_ref, r1_ref))
    pl.when(odd == 1)(lambda: put(r1_ref, r2_ref))
    lane = lanes_bf16(SIDE)

    def halo(g, carry):
        full = r32_ref[:, g].reshape(SIDE, LANES).astype(BF16)
        ends = c32_ref[:, g].reshape(SIDE, LANES).astype(BF16)
        rhs = jnp.concatenate([shifted(full, ends, lane, e) for e in range(7)], axis=0)
        add_ref[:, g] = dot32(band_ref[g], rhs).reshape(6, 8, LANES)
        return carry

    lax.fori_loop(0, GROUPS, halo, 0, unroll=5)

    def mlp(i0, edges):
        parts = []
        for r in range(2):
            y = y_ref[i0 + r].reshape(C, LANES)
            if edges[r] is not None:
                y = y + add_ref[edges[r]].reshape(C, LANES)
            mean = jnp.sum(y, axis=0, keepdims=True) * np.float32(1 / C)
            y = y - mean
            var = jnp.sum(y * y, axis=0, keepdims=True) * np.float32(1 / C)
            parts.append((y * lax.rsqrt(var + EPS) * gain_ref[...]).astype(BF16))
        hidden = gelu(dot32(w1_ref[...], jnp.concatenate(parts, axis=1))).astype(BF16)
        o = dot32(w2_ref[block], hidden)
        for r in range(2):
            o_ref[pl.ds(i0 + r, C, stride=ROWS), :] = o[:, r * LANES : (r + 1) * LANES]

    mlp(0, (0, 1))
    mlp(2, (2, None))

    def inner(p, carry):
        mlp(2 * p, (None, None))
        return carry

    lax.fori_loop(2, 6, inner, 0)
    mlp(12, (None, 3))
    mlp(14, (4, 5))
    mask = mask_ref[...].astype(F32)

    def tile(first, count):
        o = o_ref[pl.ds(first * ROWS, count * ROWS), :].reshape(count, ROWS, LANES)
        return (x_ref[pl.ds(first, count)].astype(F32) + o) * mask[None]

    if last:
        def finish(g, carry):
            out_ref[pl.ds(8 * g, 8)] = tile(pl.multiple_of(8 * g, 8), 8).astype(BF16)
            return carry

        lax.fori_loop(0, GROUPS, finish, 0)
    else:
        emit_edges(tile, o_ref, out_ref, *edge_refs)


def run_block(last, block, x, y, band, r1, r2, w1, w2, gain, mask):
    state = jax.ShapeDtypeStruct((C, ROWS, LANES), BF16)
    shapes = (state,) if last else (state,) + EDGE_SHAPES
    return pl.pallas_call(
        lambda *refs: block_kernel(last, block, *refs),
        out_shape=shapes,
        in_specs=[VM] * 9,
        out_specs=(VM,) * len(shapes),
        scratch_shapes=[
            pltpu.VMEM((6, PAD // 8, 8, LANES), F32),
            pltpu.VMEM((6, PAD // 8, 8, LANES), F32),
            pltpu.VMEM((6, GROUPS, 8, LANES), F32),
            pltpu.VMEM((C * ROWS, LANES), F32),
        ],
        compiler_params=pltpu.CompilerParams(vmem_limit_bytes=20 * 2**20),
    )(x, y, band, r1, r2, w1, w2, gain, mask)


def local(field, land_mask, fold_partner, dw_kernel, norm_gain, w_in, w_out):
    zonal = lax.axis_size("zonal")
    merid = lax.axis_size("merid")
    total = fold_partner.shape[0]
    start = jnp.mod(fold_partner[0] - (LANES // 2 - 1), total)
    turn = start // LANES
    place = lambda m, z: z * merid + m
    even_pairs = [(m, m ^ 1) for m in range(merid)]
    odd_pairs = [(m, ((m - 1) ^ 1) + 1) for m in range(1, merid - 1)]

    def branch_of(shift):
        def branch(q1, q2, x, band, west, east):
            pairs = [(place(m, z), place(n, z)) for m, n in odd_pairs for z in range(zonal)]
            pairs += [(place(merid - 1, z), place(merid - 1, (shift - z) % zonal)) for z in range(zonal)]
            r2 = lax.ppermute(q2, ("zonal", "merid"), pairs)
            r1 = lax.ppermute(q1, "merid", even_pairs)
            return r1, r2, conv_own(x, band, west, east)

        return branch

    branches = [branch_of(t) for t in range(zonal)]
    taps = jnp.transpose(dw_kernel, (0, 2, 3, 1))
    w2 = jnp.swapaxes(w_out, 1, 2)
    x = field
    send, top, bot = first_edges(x)
    for b in range(BLOCKS):
        west = lax.ppermute(send, "zonal", [(z, (z + 1) % zonal) for z in range(zonal)])
        east = lax.ppermute(send, "zonal", [((z + 1) % zonal, z) for z in range(zonal)])
        band_main, band_side, w1, gain = make_bands(b, taps, w_in, norm_gain)
        q1, q2 = turn_edges(fold_partner, west, east, top, bot)
        r1, r2, y = lax.switch(turn, branches, q1, q2, x, band_main, west, east)
        last = b == BLOCKS - 1
        x, *edges = run_block(last, b, x, y, band_side, r1, r2, w1, w2, gain, land_mask)
        if not last:
            send, top, bot = edges
    return x


def solution(mesh):
    in_specs = (P(None, "merid", "zonal"), P("merid", "zonal"), P(), P(), P(), P(), P())
    out_specs = P(None, "merid", "zonal")
    return jax.shard_map(local, mesh=mesh, in_specs=in_specs, out_specs=out_specs, check_vma=False)
```

```python
import jax
import jax.numpy as jnp
import numpy as np
from jax import lax
from jax.experimental import pallas as pl
from jax.experimental.pallas import tpu as pltpu
from jax.sharding import PartitionSpec as P

BLOCKS = 3
C = 200
PAD = 208
H = 800
ROWS = 16
LANES = 128
GROUPS = C // 8
MAIN = 8 * ROWS
SIDE = 8 * 6
EPS = 1e-05
F32 = jnp.float32
BF16 = jnp.bfloat16
EDGE_ROWS = (0, 1, 2, 13, 14, 15)
SEND = 5 * PAD
SWAP = 4 * PAD
VM = pl.BlockSpec(memory_space=pltpu.VMEM)
SM = pl.BlockSpec(memory_space=pltpu.SMEM)


def dot32(a, b):
    return jnp.dot(a, b, preferred_element_type=F32)


def lanes_bf16(rows):
    return lax.broadcasted_iota(jnp.int32, (rows, LANES), 1).astype(F32).astype(BF16)


def pad_rows(v):
    return jnp.concatenate([v, jnp.zeros((PAD - C, LANES), v.dtype)], axis=0)


def band_kernel(block, taps_ref, w_in_ref, gain_ref, main_ref, side_ref, w1_ref, gains_ref):
    rows = [jnp.concatenate([taps_ref[block, a].astype(F32), jnp.zeros((1, C), F32)], axis=0) for a in range(7)]
    taps = jnp.concatenate(rows + [jnp.zeros((8, C), F32)], axis=0).T.astype(BF16)

    def place(first, second, tap_of, own, out_ref, at):
        depth = own.shape[1]
        tap = lax.broadcasted_iota(jnp.int32, (64, depth), 0)
        both = []
        for i in (first, second):
            spread = jnp.where(tap == tap_of(i), 1.0, 0.0).astype(BF16)
            both.append(dot32(taps, spread).reshape(GROUPS, 8, depth))
        both = jnp.concatenate(both, axis=1).astype(BF16)
        out_ref[:, pl.ds(at, 16), :] = both * own[None]

    lane = lax.broadcasted_iota(jnp.int32, (1, 7 * MAIN), 1)
    e, row = lane // MAIN, lane % ROWS

    def main_tap(i):
        a = row + 3 - i
        return jnp.where((a >= 0) & (a < 7), 8 * a + e, -1)

    wide = lax.broadcasted_iota(jnp.int32, (16, 7 * MAIN), 1)
    high = lax.broadcasted_iota(jnp.int32, (16, 7 * MAIN), 0)
    own_main = jnp.where((wide % MAIN) // ROWS == high % 8, 1.0, 0.0).astype(BF16)

    def main_pair(p, carry):
        place(2 * p, 2 * p + 1, main_tap, own_main, main_ref, pl.multiple_of(16 * p, 16))
        return carry

    lax.fori_loop(0, ROWS // 2, main_pair, 0)
    lane = lax.broadcasted_iota(jnp.int32, (1, 7 * SIDE), 1)
    e_side, slot = lane // SIDE, lane % SIDE
    k = slot // 8
    row_side = jnp.where(k < 3, k, k + ROWS)

    def side_tap(i):
        a = row_side - i
        return jnp.where((a >= 0) & (a < 7), 8 * a + e_side, -1)

    wide = lax.broadcasted_iota(jnp.int32, (16, 7 * SIDE), 1)
    high = lax.broadcasted_iota(jnp.int32, (16, 7 * SIDE), 0)
    own_side = jnp.where(wide % 8 == high % 8, 1.0, 0.0).astype(BF16)
    for p in range(3):
        place(EDGE_ROWS[2 * p], EDGE_ROWS[2 * p + 1], side_tap, own_side, side_ref, 16 * p)
    w1_ref[...] = w_in_ref[block].T
    gain = gain_ref[...].astype(F32)[block : block + 1]
    gains_ref[...] = jnp.broadcast_to(gain, (LANES, C)).T


def make_bands(block, taps, w_in, gain):
    return pl.pallas_call(
        lambda *refs: band_kernel(block, *refs),
        out_shape=(
            jax.ShapeDtypeStruct((GROUPS, MAIN, 7 * MAIN), BF16),
            jax.ShapeDtypeStruct((GROUPS, SIDE, 7 * SIDE), BF16),
            jax.ShapeDtypeStruct((H, C), BF16),
            jax.ShapeDtypeStruct((C, LANES), F32),
        ),
        in_specs=[VM] * 3,
        out_specs=(VM,) * 4,
        compiler_params=pltpu.CompilerParams(vmem_limit_bytes=20 * 2**20),
        cost_estimate=pl.CostEstimate(flops=2 * 16 * 256 * 256 * 1024, bytes_accessed=9_000_000, transcendentals=0),
    )(taps, w_in, gain)


def emit_edges(tile_of, o_ref, out_ref, send_ref, top_ref, bot_ref):
    lane = lanes_bf16(ROWS)

    def some(first, count):
        v = tile_of(first, count)
        o_ref[pl.ds(first * ROWS, count * ROWS), :] = v.reshape(count * ROWS, LANES)
        v = v.astype(BF16)
        if out_ref is not None:
            out_ref[pl.ds(first, count)] = v
        packed = pltpu.roll(v[0], 3, 1)
        for c in range(1, count):
            packed = jnp.where(lane >= 8 * c, pltpu.roll(v[c], 8 * c + 3, 1), packed)
        return packed

    def step(q, carry):
        send_ref[pl.ds(pl.multiple_of(16 * q, 16), 16), :] = some(pl.multiple_of(16 * q, 16), 16)
        return carry

    lax.fori_loop(0, 12, step, 0)
    send_ref[192:208, :] = some(192, 8)
    wide = lax.broadcasted_iota(jnp.int32, (C, LANES), 1)
    corner = jnp.zeros((C, LANES), F32)
    for k in range(3):
        low = o_ref[pl.ds(k, C, stride=ROWS), :]
        corner = jnp.where((wide >= 8 * k) & (wide < 64), pltpu.roll(low, 8 * k + 3, 1), corner)
        bot_ref[k] = low.astype(BF16)
    for k in range(3):
        high = o_ref[pl.ds(ROWS - 3 + k, C, stride=ROWS), :]
        corner = jnp.where(wide >= 64 + 8 * k, pltpu.roll(high, 64 + 8 * k + 3, 1), corner)
        high = high.astype(BF16)
        top_ref[k] = high
        send_ref[(2 + k) * PAD : (3 + k) * PAD, :] = pad_rows(high)
    send_ref[PAD : 2 * PAD, :] = pad_rows(corner.astype(BF16))


EDGE_SHAPES = (
    jax.ShapeDtypeStruct((SEND, LANES), BF16),
    jax.ShapeDtypeStruct((3, C, LANES), BF16),
    jax.ShapeDtypeStruct((3, C, LANES), BF16),
)


def first_kernel(x_ref, send_ref, top_ref, bot_ref, o_ref):
    emit_edges(lambda first, count: x_ref[pl.ds(first, count)].astype(F32), o_ref, None, send_ref, top_ref, bot_ref)


def first_edges(x):
    return pl.pallas_call(
        first_kernel,
        out_shape=EDGE_SHAPES,
        in_specs=[VM],
        out_specs=(VM,) * 3,
        scratch_shapes=[pltpu.VMEM((C * ROWS, LANES), F32)],
        compiler_params=pltpu.CompilerParams(vmem_limit_bytes=10 * 2**20),
    )(x)


def place_on_mesh():
    level = lax.axis_index("merid")
    return level == lax.axis_size("merid") - 1, level % 2


def turn_kernel(fold_ref, west_ref, east_ref, top_ref, bot_ref, q1_ref, q2_ref, rows_ref):
    at_top, odd = place_on_mesh()
    off = (fold_ref[0] + (LANES // 2 + 1)) % LANES - LANES // 2
    lane = lax.broadcasted_iota(jnp.int32, (PAD, LANES), 1)
    corner = jnp.where(
        (lane & 7) < 3, west_ref[PAD : 2 * PAD, :].astype(F32), east_ref[PAD : 2 * PAD, :].astype(F32)
    ).astype(BF16)
    rows_ref[3] = corner

    @pl.when(jnp.logical_not(at_top))
    def _():
        for k in range(3):
            rows_ref[k] = pad_rows(top_ref[k])

    @pl.when(at_top)
    def _():
        src = lax.broadcasted_iota(jnp.int32, (LANES, LANES), 0)
        dst = lax.broadcasted_iota(jnp.int32, (LANES, LANES), 1)
        slot = dst & 7
        col = jnp.where(slot < 3, slot - 3, slot + 125)
        used = slot < 6
        pick, pick_corner = [], []
        for part in range(3):
            local_col = src + 128 * (part - 1)
            pick.append(jnp.where(local_col + dst == off + 127, 1.0, 0.0).astype(BF16))
            hit = jnp.where(used & (local_col + col == off + 127), 1.0, 0.0)
            pick_corner.append([jnp.where(dst // 8 == k, hit, 0.0).astype(BF16) for k in range(3)])
        turned_corner = jnp.zeros((PAD, LANES), F32)
        for k in range(3):
            at = slice((4 - k) * PAD, (5 - k) * PAD)
            three = (west_ref[at, :], pad_rows(top_ref[2 - k]), east_ref[at, :])
            turned = jnp.zeros((PAD, LANES), F32)
            for part in range(3):
                turned += dot32(three[part], pick[part])
                turned_corner += dot32(three[part], pick_corner[part][k])
            rows_ref[k] = turned.astype(BF16)
        rows_ref[3] = turned_corner.astype(BF16)

    def put(up_ref, down_ref):
        for k in range(4):
            up_ref[k * PAD : (k + 1) * PAD, :] = rows_ref[k]
        for k in range(3):
            down_ref[k * PAD : (k + 1) * PAD, :] = pad_rows(bot_ref[k])
        down_ref[3 * PAD :, :] = corner

    pl.when(odd == 0)(lambda: put(q1_ref, q2_ref))
    pl.when(odd == 1)(lambda: put(q2_ref, q1_ref))


def turn_edges(fold, west, east, top, bot):
    return pl.pallas_call(
        turn_kernel,
        out_shape=(jax.ShapeDtypeStruct((SWAP, LANES), BF16),) * 2,
        in_specs=[SM] + [VM] * 4,
        out_specs=(VM, VM),
        scratch_shapes=[pltpu.VMEM((4, PAD, LANES), BF16)],
        compiler_params=pltpu.CompilerParams(vmem_limit_bytes=10 * 2**20),
    )(fold, west, east, top, bot)


def shifted(full, ends, lane, e):
    s = e - 3
    if s > 0:
        return pltpu.roll(jnp.where(lane < s, ends, full), LANES - s, 1)
    if s < 0:
        return pltpu.roll(jnp.where(lane >= LANES + s, ends, full), -s, 1)
    return full


UNROLL = 5


def conv_kernel(x_ref, band_ref, west_ref, east_ref, y_ref, side_ref, rhs_ref):
    lane = lanes_bf16(MAIN)
    tile_lane = lax.broadcasted_iota(jnp.int32, (ROWS, LANES), 1)
    for q in range(13):
        both = jnp.where(
            (tile_lane & 7) < 3,
            west_ref[16 * q : 16 * q + 16, :].astype(F32),
            east_ref[16 * q : 16 * q + 16, :].astype(F32),
        ).astype(BF16)
        for c in range(16 if q < 12 else 8):
            side_ref[16 * q + c] = pltpu.roll(both, LANES - (8 * c + 3), 1)

    def some(t, carry):
        for u in range(UNROLL):
            g = UNROLL * t + u
            full = x_ref[pl.ds(8 * g, 8)].reshape(MAIN, LANES)
            ends = side_ref[pl.ds(8 * g, 8)].reshape(MAIN, LANES)
            for e in range(7):
                rhs_ref[u, e * MAIN : (e + 1) * MAIN, :] = shifted(full, ends, lane, e)
            y_ref[:, g] = dot32(band_ref[g], rhs_ref[u]).reshape(ROWS, 8, LANES)
        return carry

    lax.fori_loop(0, GROUPS // UNROLL, some, 0)


def conv_own(x, band, west, east):
    return pl.pallas_call(
        conv_kernel,
        out_shape=jax.ShapeDtypeStruct((ROWS, GROUPS, 8, LANES), F32),
        in_specs=[VM] * 4,
        out_specs=VM,
        scratch_shapes=[
            pltpu.VMEM((C, ROWS, LANES), BF16),
            pltpu.VMEM((UNROLL, 7 * MAIN, LANES), BF16),
        ],
        compiler_params=pltpu.CompilerParams(vmem_limit_bytes=20 * 2**20),
        cost_estimate=pl.CostEstimate(flops=2 * 25 * 256 * 256 * 1024, bytes_accessed=9_000_000, transcendentals=0),
    )(x, band, west, east)


def gelu(h):
    return h * (0.5 + 0.5 * lax.erf(h * np.float32(0.5**0.5)))


def block_kernel(last, block, x_ref, y_ref, band_ref, r1_ref, r2_ref, w1_ref, w2_ref, gain_ref, mask_ref,
                 out_ref, *refs):
    edge_refs, (r32_ref, c32_ref, add_ref, o_ref) = refs[:-4], refs[-4:]
    odd = place_on_mesh()[1]

    def put(below_ref, above_ref):
        for base, ref, lane in ((0, below_ref, 64), (3, above_ref, 0)):
            corner = ref[3 * PAD :, :].astype(F32)
            for k in range(3):
                r32_ref[base + k] = ref[k * PAD : (k + 1) * PAD, :].astype(F32).reshape(PAD // 8, 8, LANES)
                c32_ref[base + k] = pltpu.roll(corner, LANES - (lane + 8 * k + 3), 1).reshape(PAD // 8, 8, LANES)

    pl.when(odd == 0)(lambda: put(r2_ref, r1_ref))
    pl.when(odd == 1)(lambda: put(r1_ref, r2_ref))
    lane = lanes_bf16(SIDE)

    def halo(g, carry):
        full = r32_ref[:, g].reshape(SIDE, LANES).astype(BF16)
        ends = c32_ref[:, g].reshape(SIDE, LANES).astype(BF16)
        rhs = jnp.concatenate([shifted(full, ends, lane, e) for e in range(7)], axis=0)
        add_ref[:, g] = dot32(band_ref[g], rhs).reshape(6, 8, LANES)
        return carry

    lax.fori_loop(0, GROUPS, halo, 0, unroll=5)

    def mlp(i0, edges):
        parts = []
        for r in range(2):
            y = y_ref[i0 + r].reshape(C, LANES)
            if edges[r] is not None:
                y = y + add_ref[edges[r]].reshape(C, LANES)
            mean = jnp.sum(y, axis=0, keepdims=True) * np.float32(1 / C)
            y = y - mean
            var = jnp.sum(y * y, axis=0, keepdims=True) * np.float32(1 / C)
            parts.append((y * lax.rsqrt(var + EPS) * gain_ref[...]).astype(BF16))
        hidden = gelu(dot32(w1_ref[...], jnp.concatenate(parts, axis=1))).astype(BF16)
        o = dot32(w2_ref[block], hidden)
        for r in range(2):
            o_ref[pl.ds(i0 + r, C, stride=ROWS), :] = o[:, r * LANES : (r + 1) * LANES]

    mlp(0, (0, 1))
    mlp(2, (2, None))

    def inner(p, carry):
        mlp(2 * p, (None, None))
        return carry

    lax.fori_loop(2, 6, inner, 0)
    mlp(12, (None, 3))
    mlp(14, (4, 5))
    mask = mask_ref[...]

    def tile(first, count):
        o = o_ref[pl.ds(first * ROWS, count * ROWS), :].reshape(count, ROWS, LANES)
        return (x_ref[pl.ds(first, count)].astype(F32) + o) * mask[None]

    if last:
        def finish(g, carry):
            out_ref[pl.ds(8 * g, 8)] = tile(pl.multiple_of(8 * g, 8), 8).astype(BF16)
            return carry

        lax.fori_loop(0, GROUPS, finish, 0)
    else:
        emit_edges(tile, o_ref, out_ref, *edge_refs)


def run_block(last, block, x, y, band, r1, r2, w1, w2, gain, mask):
    state = jax.ShapeDtypeStruct((C, ROWS, LANES), BF16)
    shapes = (state,) if last else (state,) + EDGE_SHAPES
    return pl.pallas_call(
        lambda *refs: block_kernel(last, block, *refs),
        out_shape=shapes,
        in_specs=[VM] * 9,
        out_specs=(VM,) * len(shapes),
        scratch_shapes=[
            pltpu.VMEM((6, PAD // 8, 8, LANES), F32),
            pltpu.VMEM((6, PAD // 8, 8, LANES), F32),
            pltpu.VMEM((6, GROUPS, 8, LANES), F32),
            pltpu.VMEM((C * ROWS, LANES), F32),
        ],
        compiler_params=pltpu.CompilerParams(vmem_limit_bytes=20 * 2**20),
    )(x, y, band, r1, r2, w1, w2, gain, mask)


def local(field, land_mask, fold_partner, dw_kernel, norm_gain, w_in, w_out):
    zonal = lax.axis_size("zonal")
    merid = lax.axis_size("merid")
    total = fold_partner.shape[0]
    start = jnp.mod(fold_partner[0] - (LANES // 2 - 1), total)
    turn = start // LANES
    place = lambda m, z: z * merid + m
    even_pairs = [(m, m ^ 1) for m in range(merid)]
    odd_pairs = [(m, ((m - 1) ^ 1) + 1) for m in range(1, merid - 1)]

    def branch_of(shift):
        def branch(q2, mask, *kept):
            pairs = [(place(m, z), place(n, z)) for m, n in odd_pairs for z in range(zonal)]
            pairs += [(place(merid - 1, z), place(merid - 1, (shift - z) % zonal)) for z in range(zonal)]
            return lax.ppermute(q2, ("zonal", "merid"), pairs), float_mask(mask, *kept)

        return branch

    branches = [branch_of(t) for t in range(zonal)]
    taps = jnp.transpose(dw_kernel, (0, 2, 3, 1))
    w2 = jnp.swapaxes(w_out, 1, 2)
    x = field
    send, top, bot = first_edges(x)
    for b in range(BLOCKS):
        west = lax.ppermute(send, "zonal", [(z, (z + 1) % zonal) for z in range(zonal)])
        east = lax.ppermute(send, "zonal", [((z + 1) % zonal, z) for z in range(zonal)])
        band_main, band_side, w1, gain = make_bands(b, taps, w_in, norm_gain)
        q1, q2 = turn_edges(fold_partner, west, east, top, bot)
        r1 = lax.ppermute(q1, "merid", even_pairs)
        y = conv_own(x, band_main, west, east)
        q2, y = lax.optimization_barrier((q2, y))
        r2, mask = lax.switch(turn, branches, q2, land_mask, x, y, band_side, w1, gain)
        last = b == BLOCKS - 1
        x, *edges = run_block(last, b, x, y, band_side, r1, r2, w1, w2, gain, mask)
        if not last:
            send, top, bot = edges
    return x


def mask_kernel(mask_ref, *refs):
    out_ref = refs[-1]
    out_ref[...] = mask_ref[...].astype(F32)


def float_mask(mask, *kept):
    return pl.pallas_call(
        mask_kernel,
        out_shape=jax.ShapeDtypeStruct((ROWS, LANES), F32),
        in_specs=[VM] + [pl.BlockSpec(memory_space=pl.ANY)] * len(kept),
        out_specs=VM,
        compiler_params=pltpu.CompilerParams(vmem_limit_bytes=4 * 2**20),
    )(mask, *kept)


def solution(mesh):
    in_specs = (P(None, "merid", "zonal"), P("merid", "zonal"), P(), P(), P(), P(), P())
    out_specs = P(None, "merid", "zonal")
    return jax.shard_map(local, mesh=mesh, in_specs=in_specs, out_specs=out_specs, check_vma=False)
```

```python
import jax
import jax.numpy as jnp
import numpy as np
from jax import lax
from jax.experimental import pallas as pl
from jax.experimental.pallas import tpu as pltpu
from jax.sharding import PartitionSpec as P

BLOCKS = 3
C = 200
PAD = 208
H = 800
ROWS = 16
LANES = 128
GROUPS = C // 8
MAIN = 8 * ROWS
SIDE = 8 * 6
EPS = 1e-05
F32 = jnp.float32
BF16 = jnp.bfloat16
EDGE_ROWS = (0, 1, 2, 13, 14, 15)
PACK = 40
SEND = PAD + 3 * C + 2 * PACK + 8
SWAP = 3 * C + PACK
BOT = 3 * C + 8
VM = pl.BlockSpec(memory_space=pltpu.VMEM)
SM = pl.BlockSpec(memory_space=pltpu.SMEM)


def dot32(a, b):
    return jnp.dot(a, b, preferred_element_type=F32)


def lanes_bf16(rows):
    return lax.broadcasted_iota(jnp.int32, (rows, LANES), 1).astype(F32).astype(BF16)


def pack_corner(v):
    lane = lax.broadcasted_iota(jnp.int32, (PACK, LANES), 1)
    packed = v[:PACK]
    for q in range(1, C // PACK):
        packed = jnp.where(lane >= 24 * q, pltpu.roll(v[PACK * q : PACK * (q + 1)], 24 * q, 1), packed)
    return packed


def band_kernel(block, taps_ref, w_in_ref, gain_ref, main_ref, side_ref, w1_ref, gains_ref):
    rows = [jnp.concatenate([taps_ref[block, a].astype(F32), jnp.zeros((1, C), F32)], axis=0) for a in range(7)]
    taps = jnp.concatenate(rows + [jnp.zeros((8, C), F32)], axis=0).T.astype(BF16)

    def place(first, second, tap_of, own, out_ref, at):
        depth = own.shape[1]
        tap = lax.broadcasted_iota(jnp.int32, (64, depth), 0)
        both = []
        for i in (first, second):
            spread = jnp.where(tap == tap_of(i), 1.0, 0.0).astype(BF16)
            both.append(dot32(taps, spread).reshape(GROUPS, 8, depth))
        both = jnp.concatenate(both, axis=1).astype(BF16)
        out_ref[:, pl.ds(at, 16), :] = both * own[None]

    lane = lax.broadcasted_iota(jnp.int32, (1, 7 * MAIN), 1)
    e, row = lane // MAIN, lane % ROWS

    def main_tap(i):
        a = row + 3 - i
        return jnp.where((a >= 0) & (a < 7), 8 * a + e, -1)

    wide = lax.broadcasted_iota(jnp.int32, (16, 7 * MAIN), 1)
    high = lax.broadcasted_iota(jnp.int32, (16, 7 * MAIN), 0)
    own_main = jnp.where((wide % MAIN) // ROWS == high % 8, 1.0, 0.0).astype(BF16)

    def main_pair(p, carry):
        place(2 * p, 2 * p + 1, main_tap, own_main, main_ref, pl.multiple_of(16 * p, 16))
        return carry

    lax.fori_loop(0, ROWS // 2, main_pair, 0)
    lane = lax.broadcasted_iota(jnp.int32, (1, 7 * SIDE), 1)
    e_side, slot = lane // SIDE, lane % SIDE
    k = slot // 8
    row_side = jnp.where(k < 3, k, k + ROWS)

    def side_tap(i):
        a = row_side - i
        return jnp.where((a >= 0) & (a < 7), 8 * a + e_side, -1)

    wide = lax.broadcasted_iota(jnp.int32, (16, 7 * SIDE), 1)
    high = lax.broadcasted_iota(jnp.int32, (16, 7 * SIDE), 0)
    own_side = jnp.where(wide % 8 == high % 8, 1.0, 0.0).astype(BF16)
    for p in range(3):
        place(EDGE_ROWS[2 * p], EDGE_ROWS[2 * p + 1], side_tap, own_side, side_ref, 16 * p)
    w1_ref[...] = w_in_ref[block].T
    gain = gain_ref[...].astype(F32)[block : block + 1]
    gains_ref[...] = jnp.broadcast_to(gain, (LANES, C)).T


def make_bands(block, taps, w_in, gain):
    return pl.pallas_call(
        lambda *refs: band_kernel(block, *refs),
        out_shape=(
            jax.ShapeDtypeStruct((GROUPS, MAIN, 7 * MAIN), BF16),
            jax.ShapeDtypeStruct((GROUPS, SIDE, 7 * SIDE), BF16),
            jax.ShapeDtypeStruct((H, C), BF16),
            jax.ShapeDtypeStruct((C, LANES), F32),
        ),
        in_specs=[VM] * 3,
        out_specs=(VM,) * 4,
        compiler_params=pltpu.CompilerParams(vmem_limit_bytes=20 * 2**20),
        cost_estimate=pl.CostEstimate(flops=2 * 16 * 256 * 256 * 1024, bytes_accessed=9_000_000, transcendentals=0),
    )(taps, w_in, gain)


def emit_edges(tile_of, o_ref, out_ref, send_ref, bot_ref):
    lane = lanes_bf16(ROWS)

    def some(first, count):
        v = tile_of(first, count)
        o_ref[pl.ds(first * ROWS, count * ROWS), :] = v.reshape(count * ROWS, LANES)
        v = v.astype(BF16)
        if out_ref is not None:
            out_ref[pl.ds(first, count)] = v
        packed = pltpu.roll(v[0], 3, 1)
        for c in range(1, count):
            packed = jnp.where(lane >= 8 * c, pltpu.roll(v[c], 8 * c + 3, 1), packed)
        return packed

    for q in range(12):
        send_ref[16 * q : 16 * q + 16, :] = some(16 * q, 16)
    send_ref[192:208, :] = some(192, 8)
    wide = lax.broadcasted_iota(jnp.int32, (C, LANES), 1)

    def edge(first):
        rows = [o_ref[pl.ds(first + k, C, stride=ROWS), :] for k in range(3)]
        corner = pltpu.roll(rows[0], 3, 1)
        for k in range(1, 3):
            corner = jnp.where(wide >= 8 * k, pltpu.roll(rows[k], 8 * k + 3, 1), corner)
        return rows, pack_corner(corner)

    fill = jnp.zeros((8, LANES), F32)
    low, low_corner = edge(0)
    bot_ref[...] = jnp.concatenate(low + [fill], axis=0).astype(BF16)
    high, high_corner = edge(ROWS - 3)
    send_ref[PAD:, :] = jnp.concatenate(high + [low_corner, high_corner, fill], axis=0).astype(BF16)


EDGE_SHAPES = (
    jax.ShapeDtypeStruct((SEND, LANES), BF16),
    jax.ShapeDtypeStruct((BOT, LANES), BF16),
)


def first_kernel(x_ref, send_ref, bot_ref, o_ref):
    emit_edges(lambda first, count: x_ref[pl.ds(first, count)].astype(F32), o_ref, None, send_ref, bot_ref)


def first_edges(x):
    return pl.pallas_call(
        first_kernel,
        out_shape=EDGE_SHAPES,
        in_specs=[VM],
        out_specs=(VM,) * 2,
        scratch_shapes=[pltpu.VMEM((C * ROWS, LANES), F32)],
        compiler_params=pltpu.CompilerParams(vmem_limit_bytes=10 * 2**20),
    )(x)


def place_on_mesh():
    level = lax.axis_index("merid")
    return level == lax.axis_size("merid") - 1, level % 2


def turn_kernel(fold_ref, west_ref, east_ref, send_ref, bot_ref, q1_ref, q2_ref, up_ref):
    at_top, odd = place_on_mesh()
    off = (fold_ref[0] + (LANES // 2 + 1)) % LANES - LANES // 2
    lane = lax.broadcasted_iota(jnp.int32, (PACK, LANES), 1)
    parts = [ref[PAD:, :] for ref in (west_ref, send_ref, east_ref)]
    wide = [part.astype(F32) for part in parts]

    def corner(at):
        return jnp.where((lane & 7) < 3, wide[0][at : at + PACK], wide[2][at : at + PACK])

    @pl.when(jnp.logical_not(at_top))
    def _():
        up = jnp.concatenate([wide[1][: 3 * C], corner(3 * C + PACK)], axis=0)
        up_ref[...] = up.astype(BF16)

    @pl.when(at_top)
    def _():
        src = lax.broadcasted_iota(jnp.int32, (LANES, LANES), 0)
        dst = lax.broadcasted_iota(jnp.int32, (LANES, LANES), 1)
        slot = dst & 7
        col = jnp.where(slot < 3, slot - 3, slot + 125)
        used = slot < 6
        turned = jnp.zeros((SEND - PAD, LANES), F32)
        turned_corner = jnp.zeros((C, LANES), F32)
        for n in range(3):
            local_col = src + 128 * (n - 1)
            pick = jnp.where(local_col + dst == off + 127, 1.0, 0.0).astype(BF16)
            turned += dot32(parts[n], pick)
            hit = jnp.where(used & (local_col + col == off + 127), 1.0, 0.0)
            for k in range(3):
                pick = jnp.where(dst // 8 == k, hit, 0.0).astype(BF16)
                turned_corner += dot32(wide[n][(2 - k) * C : (3 - k) * C].astype(BF16), pick)
        rows = [turned[(2 - k) * C : (3 - k) * C] for k in range(3)]
        up_ref[...] = jnp.concatenate(rows + [pack_corner(turned_corner)], axis=0).astype(BF16)

    def put(to_up_ref, to_down_ref):
        to_up_ref[...] = up_ref[...]
        down = jnp.concatenate([bot_ref[...].astype(F32)[: 3 * C], corner(3 * C)], axis=0)
        to_down_ref[...] = down.astype(BF16)

    pl.when(odd == 0)(lambda: put(q1_ref, q2_ref))
    pl.when(odd == 1)(lambda: put(q2_ref, q1_ref))


def turn_edges(fold, west, east, send, bot):
    return pl.pallas_call(
        turn_kernel,
        out_shape=(jax.ShapeDtypeStruct((SWAP, LANES), BF16),) * 2,
        in_specs=[SM] + [VM] * 4,
        out_specs=(VM, VM),
        scratch_shapes=[pltpu.VMEM((SWAP, LANES), BF16)],
        compiler_params=pltpu.CompilerParams(vmem_limit_bytes=10 * 2**20),
    )(fold, west, east, send, bot)


def shifted(full, ends, lane, e):
    s = e - 3
    if s > 0:
        return pltpu.roll(jnp.where(lane < s, ends, full), LANES - s, 1)
    if s < 0:
        return pltpu.roll(jnp.where(lane >= LANES + s, ends, full), -s, 1)
    return full


UNROLL = 5


def conv_kernel(x_ref, band_ref, west_ref, east_ref, y_ref, side_ref):
    lane = lanes_bf16(MAIN)
    tile_lane = lax.broadcasted_iota(jnp.int32, (ROWS, LANES), 1)
    for q in range(13):
        both = jnp.where(
            (tile_lane & 7) < 3,
            west_ref[16 * q : 16 * q + 16, :].astype(F32),
            east_ref[16 * q : 16 * q + 16, :].astype(F32),
        ).astype(BF16)
        for c in range(16 if q < 12 else 8):
            side_ref[16 * q + c] = pltpu.roll(both, LANES - (8 * c + 3), 1)

    def some(t, carry):
        for u in range(UNROLL):
            g = UNROLL * t + u
            full = x_ref[pl.ds(8 * g, 8)].reshape(MAIN, LANES)
            ends = side_ref[pl.ds(8 * g, 8)].reshape(MAIN, LANES)
            rhs = jnp.concatenate([shifted(full, ends, lane, e) for e in range(7)], axis=0)
            y_ref[:, g] = dot32(band_ref[g], rhs).reshape(ROWS, 8, LANES)
        return carry

    lax.fori_loop(0, GROUPS // UNROLL, some, 0)


def conv_own(x, band, west, east):
    return pl.pallas_call(
        conv_kernel,
        out_shape=jax.ShapeDtypeStruct((ROWS, GROUPS, 8, LANES), F32),
        in_specs=[VM] * 4,
        out_specs=VM,
        scratch_shapes=[
            pltpu.VMEM((C, ROWS, LANES), BF16),
        ],
        compiler_params=pltpu.CompilerParams(vmem_limit_bytes=20 * 2**20),
        cost_estimate=pl.CostEstimate(flops=2 * 25 * 256 * 256 * 1024, bytes_accessed=9_000_000, transcendentals=0),
    )(x, band, west, east)


def gelu(h):
    return h * (0.5 + 0.5 * lax.erf(h * np.float32(0.5**0.5)))


def block_kernel(last, block, x_ref, y_ref, band_ref, r1_ref, r2_ref, w1_ref, w2_ref, gain_ref, mask_ref,
                 out_ref, *refs):
    edge_refs, (r32_ref, c32_ref, add_ref, o_ref) = refs[:-4], refs[-4:]
    odd = place_on_mesh()[1]

    def put(below_ref, above_ref):
        for base, ref in ((0, below_ref), (3, above_ref)):
            v = ref[...].astype(F32)
            for k in range(3):
                r32_ref[base + k] = v[k * C : (k + 1) * C].reshape(GROUPS, 8, LANES)
                for q in range(C // PACK):
                    corner = pltpu.roll(v[3 * C :], LANES - (24 * q + 8 * k + 3), 1)
                    c32_ref[base + k, 5 * q : 5 * q + 5] = corner.reshape(5, 8, LANES)

    pl.when(odd == 0)(lambda: put(r2_ref, r1_ref))
    pl.when(odd == 1)(lambda: put(r1_ref, r2_ref))
    lane = lanes_bf16(SIDE)

    def halo(g, carry):
        full = r32_ref[:, g].reshape(SIDE, LANES).astype(BF16)
        ends = c32_ref[:, g].reshape(SIDE, LANES).astype(BF16)
        rhs = jnp.concatenate([shifted(full, ends, lane, e) for e in range(7)], axis=0)
        add_ref[:, g] = dot32(band_ref[g], rhs).reshape(6, 8, LANES)
        return carry

    lax.fori_loop(0, GROUPS, halo, 0, unroll=25)

    def mlp(i0, edges):
        parts = []
        for r in range(2):
            y = y_ref[i0 + r].reshape(C, LANES)
            if edges[r] is not None:
                y = y + add_ref[edges[r]].reshape(C, LANES)
            mean = jnp.sum(y, axis=0, keepdims=True) * np.float32(1 / C)
            y = y - mean
            var = jnp.sum(y * y, axis=0, keepdims=True) * np.float32(1 / C)
            parts.append((y * lax.rsqrt(var + EPS) * gain_ref[...]).astype(BF16))
        hidden = gelu(dot32(w1_ref[...], jnp.concatenate(parts, axis=1))).astype(BF16)
        o = dot32(w2_ref[block], hidden)
        for r in range(2):
            o_ref[pl.ds(i0 + r, C, stride=ROWS), :] = o[:, r * LANES : (r + 1) * LANES]

    edge_of = {row: n for n, row in enumerate(EDGE_ROWS)}
    for i in range(0, ROWS, 2):
        mlp(i, (edge_of.get(i), edge_of.get(i + 1)))
    mask = mask_ref[...]

    def tile(first, count):
        o = o_ref[pl.ds(first * ROWS, count * ROWS), :].reshape(count, ROWS, LANES)
        return (x_ref[pl.ds(first, count)].astype(F32) + o) * mask[None]

    if last:
        def finish(g, carry):
            out_ref[pl.ds(8 * g, 8)] = tile(pl.multiple_of(8 * g, 8), 8).astype(BF16)
            return carry

        lax.fori_loop(0, GROUPS, finish, 0)
    else:
        emit_edges(tile, o_ref, out_ref, *edge_refs)


def run_block(last, block, x, y, band, r1, r2, w1, w2, gain, mask):
    state = jax.ShapeDtypeStruct((C, ROWS, LANES), BF16)
    shapes = (state,) if last else (state,) + EDGE_SHAPES
    return pl.pallas_call(
        lambda *refs: block_kernel(last, block, *refs),
        out_shape=shapes,
        in_specs=[VM] * 9,
        out_specs=(VM,) * len(shapes),
        scratch_shapes=[
            pltpu.VMEM((6, GROUPS, 8, LANES), F32),
            pltpu.VMEM((6, GROUPS, 8, LANES), F32),
            pltpu.VMEM((6, GROUPS, 8, LANES), F32),
            pltpu.VMEM((C * ROWS, LANES), F32),
        ],
        compiler_params=pltpu.CompilerParams(vmem_limit_bytes=20 * 2**20),
    )(x, y, band, r1, r2, w1, w2, gain, mask)


def local(field, land_mask, fold_partner, dw_kernel, norm_gain, w_in, w_out):
    zonal = lax.axis_size("zonal")
    merid = lax.axis_size("merid")
    total = fold_partner.shape[0]
    start = jnp.mod(fold_partner[0] - (LANES // 2 - 1), total)
    turn = start // LANES
    place = lambda m, z: z * merid + m
    even_pairs = [(m, m ^ 1) for m in range(merid)]
    odd_pairs = [(m, ((m - 1) ^ 1) + 1) for m in range(1, merid - 1)]

    def branch_of(shift):
        def branch(q2, mask, *kept):
            pairs = [(place(m, z), place(n, z)) for m, n in odd_pairs for z in range(zonal)]
            pairs += [(place(merid - 1, z), place(merid - 1, (shift - z) % zonal)) for z in range(zonal)]
            return lax.ppermute(q2, ("zonal", "merid"), pairs), float_mask(mask, *kept)

        return branch

    branches = [branch_of(t) for t in range(zonal)]
    taps = jnp.transpose(dw_kernel, (0, 2, 3, 1))
    w2 = jnp.swapaxes(w_out, 1, 2)
    x = field
    send, bot = first_edges(x)
    for b in range(BLOCKS):
        west = lax.ppermute(send, "zonal", [(z, (z + 1) % zonal) for z in range(zonal)])
        east = lax.ppermute(send, "zonal", [((z + 1) % zonal, z) for z in range(zonal)])
        band_main, band_side, w1, gain = make_bands(b, taps, w_in, norm_gain)
        q1, q2 = turn_edges(fold_partner, west, east, send, bot)
        r1 = lax.ppermute(q1, "merid", even_pairs)
        y = conv_own(x, band_main, west, east)
        q2, y = lax.optimization_barrier((q2, y))
        r2, mask = lax.switch(turn, branches, q2, land_mask, x, y, band_side, w1, gain)
        last = b == BLOCKS - 1
        x, *edges = run_block(last, b, x, y, band_side, r1, r2, w1, w2, gain, mask)
        if not last:
            send, bot = edges
    return x


def mask_kernel(mask_ref, *refs):
    out_ref = refs[-1]
    out_ref[...] = mask_ref[...].astype(F32)


def float_mask(mask, *kept):
    return pl.pallas_call(
        mask_kernel,
        out_shape=jax.ShapeDtypeStruct((ROWS, LANES), F32),
        in_specs=[VM] + [pl.BlockSpec(memory_space=pl.ANY)] * len(kept),
        out_specs=VM,
        compiler_params=pltpu.CompilerParams(vmem_limit_bytes=4 * 2**20),
    )(mask, *kept)


def solution(mesh):
    in_specs = (P(None, "merid", "zonal"), P("merid", "zonal"), P(), P(), P(), P(), P())
    out_specs = P(None, "merid", "zonal")
    return jax.shard_map(local, mesh=mesh, in_specs=in_specs, out_specs=out_specs, check_vma=False)
```

```python
import jax
import jax.numpy as jnp
import numpy as np
from jax import lax
from jax.experimental import pallas as pl
from jax.experimental.pallas import tpu as pltpu
from jax.sharding import PartitionSpec as P

BLOCKS = 3
C = 200
PAD = 208
H = 800
ROWS = 16
LANES = 128
GROUPS = C // 8
MAIN = 8 * ROWS
SIDE = 8 * 6
EPS = 1e-05
F32 = jnp.float32
BF16 = jnp.bfloat16
EDGE_ROWS = (0, 1, 2, 13, 14, 15)
PACK = 40
SEND = PAD + 3 * C + 2 * PACK + 8
SWAP = 3 * C + PACK
BOT = 3 * C + 8
VM = pl.BlockSpec(memory_space=pltpu.VMEM)
SM = pl.BlockSpec(memory_space=pltpu.SMEM)


def dot32(a, b):
    return jnp.dot(a, b, preferred_element_type=F32)


def lanes_bf16(rows):
    return lax.broadcasted_iota(jnp.int32, (rows, LANES), 1).astype(F32).astype(BF16)


def pack_corner(v):
    lane = lax.broadcasted_iota(jnp.int32, (PACK, LANES), 1)
    packed = v[:PACK]
    for q in range(1, C // PACK):
        packed = jnp.where(lane >= 24 * q, pltpu.roll(v[PACK * q : PACK * (q + 1)], 24 * q, 1), packed)
    return packed


def band_kernel(block, taps_ref, w_in_ref, gain_ref, main_ref, side_ref, w1_ref, gains_ref):
    rows = [jnp.concatenate([taps_ref[block, a].astype(F32), jnp.zeros((1, C), F32)], axis=0) for a in range(7)]
    taps = jnp.concatenate(rows + [jnp.zeros((8, C), F32)], axis=0).T.astype(BF16)

    def place(first, second, tap_of, own, out_ref, at):
        depth = own.shape[1]
        tap = lax.broadcasted_iota(jnp.int32, (64, depth), 0)
        both = []
        for i in (first, second):
            spread = jnp.where(tap == tap_of(i), 1.0, 0.0).astype(BF16)
            both.append(dot32(taps, spread).reshape(GROUPS, 8, depth))
        both = jnp.concatenate(both, axis=1).astype(BF16)
        out_ref[:, pl.ds(at, 16), :] = both * own[None]

    lane = lax.broadcasted_iota(jnp.int32, (1, 7 * MAIN), 1)
    e, row = lane // MAIN, lane % ROWS

    def main_tap(i):
        a = row + 3 - i
        return jnp.where((a >= 0) & (a < 7), 8 * a + e, -1)

    wide = lax.broadcasted_iota(jnp.int32, (16, 7 * MAIN), 1)
    high = lax.broadcasted_iota(jnp.int32, (16, 7 * MAIN), 0)
    own_main = jnp.where((wide % MAIN) // ROWS == high % 8, 1.0, 0.0).astype(BF16)

    def main_pair(p, carry):
        place(2 * p, 2 * p + 1, main_tap, own_main, main_ref, pl.multiple_of(16 * p, 16))
        return carry

    lax.fori_loop(0, ROWS // 2, main_pair, 0)
    lane = lax.broadcasted_iota(jnp.int32, (1, 7 * SIDE), 1)
    e_side, slot = lane // SIDE, lane % SIDE
    k = slot // 8
    row_side = jnp.where(k < 3, k, k + ROWS)

    def side_tap(i):
        a = row_side - i
        return jnp.where((a >= 0) & (a < 7), 8 * a + e_side, -1)

    wide = lax.broadcasted_iota(jnp.int32, (16, 7 * SIDE), 1)
    high = lax.broadcasted_iota(jnp.int32, (16, 7 * SIDE), 0)
    own_side = jnp.where(wide % 8 == high % 8, 1.0, 0.0).astype(BF16)
    for p in range(3):
        place(EDGE_ROWS[2 * p], EDGE_ROWS[2 * p + 1], side_tap, own_side, side_ref, 16 * p)
    w1_ref[...] = w_in_ref[block].T
    gain = gain_ref[...].astype(F32)[block : block + 1]
    gains_ref[...] = jnp.broadcast_to(gain, (LANES, C)).T


def make_bands(block, taps, w_in, gain):
    return pl.pallas_call(
        lambda *refs: band_kernel(block, *refs),
        out_shape=(
            jax.ShapeDtypeStruct((GROUPS, MAIN, 7 * MAIN), BF16),
            jax.ShapeDtypeStruct((GROUPS, SIDE, 7 * SIDE), BF16),
            jax.ShapeDtypeStruct((H, C), BF16),
            jax.ShapeDtypeStruct((C, LANES), F32),
        ),
        in_specs=[VM] * 3,
        out_specs=(VM,) * 4,
        compiler_params=pltpu.CompilerParams(vmem_limit_bytes=14 * 2**20),
        cost_estimate=pl.CostEstimate(flops=2 * 16 * 256 * 256 * 1024, bytes_accessed=9_000_000, transcendentals=0),
    )(taps, w_in, gain)


def emit_edges(tile_of, o_ref, out_ref, send_ref, bot_ref):
    lane = lanes_bf16(ROWS)

    def some(first, count):
        v = tile_of(first, count)
        o_ref[pl.ds(first * ROWS, count * ROWS), :] = v.reshape(count * ROWS, LANES)
        v = v.astype(BF16)
        if out_ref is not None:
            out_ref[pl.ds(first, count)] = v
        packed = pltpu.roll(v[0], 3, 1)
        for c in range(1, count):
            packed = jnp.where(lane >= 8 * c, pltpu.roll(v[c], 8 * c + 3, 1), packed)
        return packed

    for q in range(12):
        send_ref[16 * q : 16 * q + 16, :] = some(16 * q, 16)
    send_ref[192:208, :] = some(192, 8)
    wide = lax.broadcasted_iota(jnp.int32, (C, LANES), 1)

    def edge(first):
        rows = [o_ref[pl.ds(first + k, C, stride=ROWS), :] for k in range(3)]
        corner = pltpu.roll(rows[0], 3, 1)
        for k in range(1, 3):
            corner = jnp.where(wide >= 8 * k, pltpu.roll(rows[k], 8 * k + 3, 1), corner)
        return rows, pack_corner(corner)

    fill = jnp.zeros((8, LANES), F32)
    low, low_corner = edge(0)
    bot_ref[...] = jnp.concatenate(low + [fill], axis=0).astype(BF16)
    high, high_corner = edge(ROWS - 3)
    send_ref[PAD:, :] = jnp.concatenate(high + [low_corner, high_corner, fill], axis=0).astype(BF16)


EDGE_SHAPES = (
    jax.ShapeDtypeStruct((SEND, LANES), BF16),
    jax.ShapeDtypeStruct((BOT, LANES), BF16),
)


def first_kernel(x_ref, send_ref, bot_ref, o_ref):
    emit_edges(lambda first, count: x_ref[pl.ds(first, count)].astype(F32), o_ref, None, send_ref, bot_ref)


def first_edges(x):
    return pl.pallas_call(
        first_kernel,
        out_shape=EDGE_SHAPES,
        in_specs=[VM],
        out_specs=(VM,) * 2,
        scratch_shapes=[pltpu.VMEM((C * ROWS, LANES), F32)],
        compiler_params=pltpu.CompilerParams(vmem_limit_bytes=6 * 2**20),
    )(x)


def place_on_mesh():
    level = lax.axis_index("merid")
    return level == lax.axis_size("merid") - 1, level % 2


def turn_kernel(fold_ref, west_ref, east_ref, send_ref, bot_ref, q1_ref, q2_ref, up_ref):
    at_top, odd = place_on_mesh()
    off = (fold_ref[0] + (LANES // 2 + 1)) % LANES - LANES // 2
    lane = lax.broadcasted_iota(jnp.int32, (PACK, LANES), 1)
    parts = [ref[PAD:, :] for ref in (west_ref, send_ref, east_ref)]
    wide = [part.astype(F32) for part in parts]

    def corner(at):
        return jnp.where((lane & 7) < 3, wide[0][at : at + PACK], wide[2][at : at + PACK])

    @pl.when(jnp.logical_not(at_top))
    def _():
        up = jnp.concatenate([wide[1][: 3 * C], corner(3 * C + PACK)], axis=0)
        up_ref[...] = up.astype(BF16)

    @pl.when(at_top)
    def _():
        src = lax.broadcasted_iota(jnp.int32, (LANES, LANES), 0)
        dst = lax.broadcasted_iota(jnp.int32, (LANES, LANES), 1)
        slot = dst & 7
        col = jnp.where(slot < 3, slot - 3, slot + 125)
        used = slot < 6
        turned = jnp.zeros((SEND - PAD, LANES), F32)
        turned_corner = jnp.zeros((C, LANES), F32)
        for n in range(3):
            local_col = src + 128 * (n - 1)
            pick = jnp.where(local_col + dst == off + 127, 1.0, 0.0).astype(BF16)
            turned += dot32(parts[n], pick)
            hit = jnp.where(used & (local_col + col == off + 127), 1.0, 0.0)
            for k in range(3):
                pick = jnp.where(dst // 8 == k, hit, 0.0).astype(BF16)
                turned_corner += dot32(wide[n][(2 - k) * C : (3 - k) * C].astype(BF16), pick)
        rows = [turned[(2 - k) * C : (3 - k) * C] for k in range(3)]
        up_ref[...] = jnp.concatenate(rows + [pack_corner(turned_corner)], axis=0).astype(BF16)

    def put(to_up_ref, to_down_ref):
        to_up_ref[...] = up_ref[...]
        down = jnp.concatenate([bot_ref[...].astype(F32)[: 3 * C], corner(3 * C)], axis=0)
        to_down_ref[...] = down.astype(BF16)

    pl.when(odd == 0)(lambda: put(q1_ref, q2_ref))
    pl.when(odd == 1)(lambda: put(q2_ref, q1_ref))


def turn_edges(fold, west, east, send, bot):
    return pl.pallas_call(
        turn_kernel,
        out_shape=(jax.ShapeDtypeStruct((SWAP, LANES), BF16),) * 2,
        in_specs=[SM] + [VM] * 4,
        out_specs=(VM, VM),
        scratch_shapes=[pltpu.VMEM((SWAP, LANES), BF16)],
        compiler_params=pltpu.CompilerParams(vmem_limit_bytes=6 * 2**20),
    )(fold, west, east, send, bot)


def shifted(full, ends, lane, e):
    s = e - 3
    if s > 0:
        return pltpu.roll(jnp.where(lane < s, ends, full), LANES - s, 1)
    if s < 0:
        return pltpu.roll(jnp.where(lane >= LANES + s, ends, full), -s, 1)
    return full


UNROLL = 5


def conv_kernel(x_ref, band_ref, west_ref, east_ref, y_ref, side_ref):
    lane = lanes_bf16(MAIN)
    tile_lane = lax.broadcasted_iota(jnp.int32, (ROWS, LANES), 1)
    for q in range(13):
        both = jnp.where(
            (tile_lane & 7) < 3,
            west_ref[16 * q : 16 * q + 16, :].astype(F32),
            east_ref[16 * q : 16 * q + 16, :].astype(F32),
        ).astype(BF16)
        for c in range(16 if q < 12 else 8):
            side_ref[16 * q + c] = pltpu.roll(both, LANES - (8 * c + 3), 1)

    def some(t, carry):
        for u in range(UNROLL):
            g = UNROLL * t + u
            full = x_ref[pl.ds(8 * g, 8)].reshape(MAIN, LANES)
            ends = side_ref[pl.ds(8 * g, 8)].reshape(MAIN, LANES)
            rhs = jnp.concatenate([shifted(full, ends, lane, e) for e in range(7)], axis=0)
            y_ref[:, g] = dot32(band_ref[g], rhs).reshape(ROWS, 8, LANES)
        return carry

    lax.fori_loop(0, GROUPS // UNROLL, some, 0)


def conv_own(x, band, west, east):
    return pl.pallas_call(
        conv_kernel,
        out_shape=jax.ShapeDtypeStruct((ROWS, GROUPS, 8, LANES), F32),
        in_specs=[VM] * 4,
        out_specs=VM,
        scratch_shapes=[
            pltpu.VMEM((C, ROWS, LANES), BF16),
        ],
        compiler_params=pltpu.CompilerParams(vmem_limit_bytes=14 * 2**20),
        cost_estimate=pl.CostEstimate(flops=2 * 25 * 256 * 256 * 1024, bytes_accessed=9_000_000, transcendentals=0),
    )(x, band, west, east)


def gelu(h):
    return h * (0.5 + 0.5 * lax.erf(h * np.float32(0.5**0.5)))


def block_kernel(last, block, x_ref, y_ref, band_ref, r1_ref, r2_ref, r3_ref, w1_ref, w2_ref, gain_ref, mask_ref,
                 out_ref, *refs):
    edge_refs, (r32_ref, c32_ref, add_ref, o_ref) = refs[:-4], refs[-4:]
    at_top, odd = place_on_mesh()

    def put(below_ref, above_ref):
        for base, ref in ((0, below_ref), (3, above_ref)):
            v = ref[...].astype(F32)
            for k in range(3):
                r32_ref[base + k] = v[k * C : (k + 1) * C].reshape(GROUPS, 8, LANES)
                for q in range(C // PACK):
                    corner = pltpu.roll(v[3 * C :], LANES - (24 * q + 8 * k + 3), 1)
                    c32_ref[base + k, 5 * q : 5 * q + 5] = corner.reshape(5, 8, LANES)

    pl.when(odd == 0)(lambda: put(r2_ref, r1_ref))
    pl.when((odd == 1) & jnp.logical_not(at_top))(lambda: put(r1_ref, r2_ref))
    pl.when(at_top)(lambda: put(r1_ref, r3_ref))
    lane = lanes_bf16(SIDE)

    def halo(g, carry):
        full = r32_ref[:, g].reshape(SIDE, LANES).astype(BF16)
        ends = c32_ref[:, g].reshape(SIDE, LANES).astype(BF16)
        rhs = jnp.concatenate([shifted(full, ends, lane, e) for e in range(7)], axis=0)
        add_ref[:, g] = dot32(band_ref[g], rhs).reshape(6, 8, LANES)
        return carry

    lax.fori_loop(0, GROUPS, halo, 0, unroll=25)

    def mlp(i0, edges):
        parts = []
        for r in range(2):
            y = y_ref[i0 + r].reshape(C, LANES)
            if edges[r] is not None:
                y = y + add_ref[edges[r]].reshape(C, LANES)
            mean = jnp.sum(y, axis=0, keepdims=True) * np.float32(1 / C)
            y = y - mean
            var = jnp.sum(y * y, axis=0, keepdims=True) * np.float32(1 / C)
            parts.append((y * lax.rsqrt(var + EPS) * gain_ref[...]).astype(BF16))
        hidden = gelu(dot32(w1_ref[...], jnp.concatenate(parts, axis=1))).astype(BF16)
        o = dot32(w2_ref[block], hidden)
        for r in range(2):
            o_ref[pl.ds(i0 + r, C, stride=ROWS), :] = o[:, r * LANES : (r + 1) * LANES]

    edge_of = {row: n for n, row in enumerate(EDGE_ROWS)}
    for i in range(0, ROWS, 2):
        mlp(i, (edge_of.get(i), edge_of.get(i + 1)))
    mask = mask_ref[...]

    def tile(first, count):
        o = o_ref[pl.ds(first * ROWS, count * ROWS), :].reshape(count, ROWS, LANES)
        return (x_ref[pl.ds(first, count)].astype(F32) + o) * mask[None]

    if last:
        def finish(g, carry):
            out_ref[pl.ds(8 * g, 8)] = tile(pl.multiple_of(8 * g, 8), 8).astype(BF16)
            return carry

        lax.fori_loop(0, GROUPS, finish, 0)
    else:
        emit_edges(tile, o_ref, out_ref, *edge_refs)


def run_block(last, block, x, y, band, r1, r2, r3, w1, w2, gain, mask):
    state = jax.ShapeDtypeStruct((C, ROWS, LANES), BF16)
    shapes = (state,) if last else (state,) + EDGE_SHAPES
    return pl.pallas_call(
        lambda *refs: block_kernel(last, block, *refs),
        out_shape=shapes,
        in_specs=[VM] * 10,
        out_specs=(VM,) * len(shapes),
        scratch_shapes=[
            pltpu.VMEM((6, GROUPS, 8, LANES), F32),
            pltpu.VMEM((6, GROUPS, 8, LANES), F32),
            pltpu.VMEM((6, GROUPS, 8, LANES), F32),
            pltpu.VMEM((C * ROWS, LANES), F32),
        ],
        compiler_params=pltpu.CompilerParams(vmem_limit_bytes=14 * 2**20),
    )(x, y, band, r1, r2, r3, w1, w2, gain, mask)


def local(field, land_mask, fold_partner, dw_kernel, norm_gain, w_in, w_out):
    zonal = lax.axis_size("zonal")
    merid = lax.axis_size("merid")
    total = fold_partner.shape[0]
    start = jnp.mod(fold_partner[0] - (LANES // 2 - 1), total)
    turn = start // LANES
    place = lambda m, z: z * merid + m
    even_pairs = [(m, m ^ 1) for m in range(merid)]
    odd_pairs = [(m, ((m - 1) ^ 1) + 1) for m in range(1, merid - 1)]

    def branch_of(shift):
        def branch(rows, mask, *kept):
            pairs = [(place(merid - 1, z), place(merid - 1, (shift - z) % zonal)) for z in range(zonal)]
            return lax.ppermute(rows, ("zonal", "merid"), pairs), float_mask(mask, *kept)

        return branch

    branches = [branch_of(t) for t in range(zonal)]
    taps = jnp.transpose(dw_kernel, (0, 2, 3, 1))
    w2 = jnp.swapaxes(w_out, 1, 2)
    x = field
    send, bot = first_edges(x)
    for b in range(BLOCKS):
        west = lax.ppermute(send, "zonal", [(z, (z + 1) % zonal) for z in range(zonal)])
        east = lax.ppermute(send, "zonal", [((z + 1) % zonal, z) for z in range(zonal)])
        band_main, band_side, w1, gain = make_bands(b, taps, w_in, norm_gain)
        q1, q2 = turn_edges(fold_partner, west, east, send, bot)
        r1 = lax.ppermute(q1, "merid", even_pairs)
        r2 = lax.ppermute(q2, "merid", odd_pairs)
        y = conv_own(x, band_main, west, east)
        q2, y = lax.optimization_barrier((q2, y))
        r3, mask = lax.switch(turn, branches, q2, land_mask, x, y, band_side, w1, gain)
        last = b == BLOCKS - 1
        x, *edges = run_block(last, b, x, y, band_side, r1, r2, r3, w1, w2, gain, mask)
        if not last:
            send, bot = edges
    return x


def mask_kernel(mask_ref, *refs):
    out_ref = refs[-1]
    out_ref[...] = mask_ref[...].astype(F32)


def float_mask(mask, *kept):
    return pl.pallas_call(
        mask_kernel,
        out_shape=jax.ShapeDtypeStruct((ROWS, LANES), F32),
        in_specs=[VM] + [pl.BlockSpec(memory_space=pl.ANY)] * len(kept),
        out_specs=VM,
        compiler_params=pltpu.CompilerParams(vmem_limit_bytes=4 * 2**20),
    )(mask, *kept)


def solution(mesh):
    in_specs = (P(None, "merid", "zonal"), P("merid", "zonal"), P(), P(), P(), P(), P())
    out_specs = P(None, "merid", "zonal")
    return jax.shard_map(local, mesh=mesh, in_specs=in_specs, out_specs=out_specs, check_vma=False)
```

```python
import jax
import jax.numpy as jnp
import numpy as np
from jax import lax
from jax.experimental import pallas as pl
from jax.experimental.pallas import tpu as pltpu
from jax.sharding import PartitionSpec as P

BLOCKS = 3
C = 200
PAD = 208
H = 800
ROWS = 16
LANES = 128
GROUPS = C // 8
MAIN = 8 * ROWS
SIDE = 8 * 6
EPS = 1e-05
F32 = jnp.float32
BF16 = jnp.bfloat16
EDGE_ROWS = (0, 1, 2, 13, 14, 15)
PACK = 40
SEND = PAD + 3 * C + 2 * PACK + 8
SWAP = 3 * C + PACK
BOT = 3 * C + 8
VM = pl.BlockSpec(memory_space=pltpu.VMEM)
SM = pl.BlockSpec(memory_space=pltpu.SMEM)
ANY = pl.BlockSpec(memory_space=pl.ANY)


def dot32(a, b):
    return jnp.dot(a, b, preferred_element_type=F32)


def lanes_bf16(rows):
    return lax.broadcasted_iota(jnp.int32, (rows, LANES), 1).astype(F32).astype(BF16)


def pack_corner(v):
    lane = lax.broadcasted_iota(jnp.int32, (PACK, LANES), 1)
    packed = v[:PACK]
    for q in range(1, C // PACK):
        packed = jnp.where(lane >= 24 * q, pltpu.roll(v[PACK * q : PACK * (q + 1)], 24 * q, 1), packed)
    return packed


def band_kernel(block, taps_ref, w_in_ref, gain_ref, main_ref, side_ref, w1_ref, gains_ref):
    rows = [jnp.concatenate([taps_ref[block, a].astype(F32), jnp.zeros((1, C), F32)], axis=0) for a in range(7)]
    taps = jnp.concatenate(rows + [jnp.zeros((8, C), F32)], axis=0).T.astype(BF16)

    def place(first, second, tap_of, own, out_ref, at):
        depth = own.shape[1]
        tap = lax.broadcasted_iota(jnp.int32, (64, depth), 0)
        both = []
        for i in (first, second):
            spread = jnp.where(tap == tap_of(i), 1.0, 0.0).astype(BF16)
            both.append(dot32(taps, spread).reshape(GROUPS, 8, depth))
        both = jnp.concatenate(both, axis=1).astype(BF16)
        out_ref[:, pl.ds(at, 16), :] = both * own[None]

    lane = lax.broadcasted_iota(jnp.int32, (1, 7 * MAIN), 1)
    e, row = lane // MAIN, lane % ROWS

    def main_tap(i):
        a = row + 3 - i
        return jnp.where((a >= 0) & (a < 7), 8 * a + e, -1)

    wide = lax.broadcasted_iota(jnp.int32, (16, 7 * MAIN), 1)
    high = lax.broadcasted_iota(jnp.int32, (16, 7 * MAIN), 0)
    own_main = jnp.where((wide % MAIN) // ROWS == high % 8, 1.0, 0.0).astype(BF16)

    def main_pair(p, carry):
        place(2 * p, 2 * p + 1, main_tap, own_main, main_ref, pl.multiple_of(16 * p, 16))
        return carry

    lax.fori_loop(0, ROWS // 2, main_pair, 0)
    lane = lax.broadcasted_iota(jnp.int32, (1, 7 * SIDE), 1)
    e_side, slot = lane // SIDE, lane % SIDE
    k = slot // 8
    row_side = jnp.where(k < 3, k, k + ROWS)

    def side_tap(i):
        a = row_side - i
        return jnp.where((a >= 0) & (a < 7), 8 * a + e_side, -1)

    wide = lax.broadcasted_iota(jnp.int32, (16, 7 * SIDE), 1)
    high = lax.broadcasted_iota(jnp.int32, (16, 7 * SIDE), 0)
    own_side = jnp.where(wide % 8 == high % 8, 1.0, 0.0).astype(BF16)
    for p in range(3):
        place(EDGE_ROWS[2 * p], EDGE_ROWS[2 * p + 1], side_tap, own_side, side_ref, 16 * p)
    w1_ref[...] = w_in_ref[block].T
    gain = gain_ref[...].astype(F32)[block : block + 1]
    gains_ref[...] = jnp.broadcast_to(gain, (LANES, C)).T


def make_bands(block, taps, w_in, gain):
    return pl.pallas_call(
        lambda *refs: band_kernel(block, *refs),
        out_shape=(
            jax.ShapeDtypeStruct((GROUPS, MAIN, 7 * MAIN), BF16),
            jax.ShapeDtypeStruct((GROUPS, SIDE, 7 * SIDE), BF16),
            jax.ShapeDtypeStruct((H, C), BF16),
            jax.ShapeDtypeStruct((C, LANES), F32),
        ),
        in_specs=[VM] * 3,
        out_specs=(VM,) * 4,
        compiler_params=pltpu.CompilerParams(vmem_limit_bytes=14 * 2**20),
        cost_estimate=pl.CostEstimate(flops=2 * 16 * 256 * 256 * 1024, bytes_accessed=9_000_000, transcendentals=0),
    )(taps, w_in, gain)


def emit_edges(tile_of, o_ref, out_ref, send_ref, bot_ref):
    lane = lanes_bf16(ROWS)

    def some(first, count):
        v = tile_of(first, count)
        o_ref[pl.ds(first * ROWS, count * ROWS), :] = v.reshape(count * ROWS, LANES)
        v = v.astype(BF16)
        if out_ref is not None:
            out_ref[pl.ds(first, count)] = v
        packed = pltpu.roll(v[0], 3, 1)
        for c in range(1, count):
            packed = jnp.where(lane >= 8 * c, pltpu.roll(v[c], 8 * c + 3, 1), packed)
        return packed

    for q in range(12):
        send_ref[16 * q : 16 * q + 16, :] = some(16 * q, 16)
    send_ref[192:208, :] = some(192, 8)
    wide = lax.broadcasted_iota(jnp.int32, (C, LANES), 1)

    def edge(first):
        rows = [o_ref[pl.ds(first + k, C, stride=ROWS), :] for k in range(3)]
        corner = pltpu.roll(rows[0], 3, 1)
        for k in range(1, 3):
            corner = jnp.where(wide >= 8 * k, pltpu.roll(rows[k], 8 * k + 3, 1), corner)
        return rows, pack_corner(corner)

    fill = jnp.zeros((8, LANES), F32)
    low, low_corner = edge(0)
    bot_ref[...] = jnp.concatenate(low + [fill], axis=0).astype(BF16)
    high, high_corner = edge(ROWS - 3)
    send_ref[PAD:, :] = jnp.concatenate(high + [low_corner, high_corner, fill], axis=0).astype(BF16)


EDGE_SHAPES = (
    jax.ShapeDtypeStruct((SEND, LANES), BF16),
    jax.ShapeDtypeStruct((BOT, LANES), BF16),
)


def first_kernel(x_ref, send_ref, bot_ref, o_ref):
    emit_edges(lambda first, count: x_ref[pl.ds(first, count)].astype(F32), o_ref, None, send_ref, bot_ref)


def first_edges(x):
    return pl.pallas_call(
        first_kernel,
        out_shape=EDGE_SHAPES,
        in_specs=[VM],
        out_specs=(VM,) * 2,
        scratch_shapes=[pltpu.VMEM((C * ROWS, LANES), F32)],
        compiler_params=pltpu.CompilerParams(vmem_limit_bytes=6 * 2**20),
    )(x)


def place_on_mesh():
    level = lax.axis_index("merid")
    return level == lax.axis_size("merid") - 1, level % 2


def turn_kernel(fold_ref, west_ref, east_ref, send_ref, bot_ref, q1_ref, q2_ref, up_ref):
    at_top, odd = place_on_mesh()
    off = (fold_ref[0] + (LANES // 2 + 1)) % LANES - LANES // 2
    lane = lax.broadcasted_iota(jnp.int32, (PACK, LANES), 1)
    parts = [ref[PAD:, :] for ref in (west_ref, send_ref, east_ref)]
    wide = [part.astype(F32) for part in parts]

    def corner(at):
        return jnp.where((lane & 7) < 3, wide[0][at : at + PACK], wide[2][at : at + PACK])

    @pl.when(jnp.logical_not(at_top))
    def _():
        up = jnp.concatenate([wide[1][: 3 * C], corner(3 * C + PACK)], axis=0)
        up_ref[...] = up.astype(BF16)

    @pl.when(at_top)
    def _():
        src = lax.broadcasted_iota(jnp.int32, (LANES, 2 * LANES), 0)
        dst = lax.broadcasted_iota(jnp.int32, (LANES, 2 * LANES), 1)
        col = jnp.where(dst < LANES, dst, jnp.where(dst < LANES + 3, dst - LANES - 3, dst - 3))
        used = dst < LANES + 6
        turned = jnp.zeros((SEND - PAD, 2 * LANES), F32)
        for n in range(3):
            hit = used & (src + 128 * (n - 1) + col == off + 127)
            turned += dot32(parts[n], jnp.where(hit, 1.0, 0.0).astype(BF16))
        rows = [turned[(2 - k) * C : (3 - k) * C, :LANES] for k in range(3)]
        ends = [turned[(2 - k) * C : (3 - k) * C, LANES:] for k in range(3)]
        full_lane = lax.broadcasted_iota(jnp.int32, (C, LANES), 1)
        turned_corner = ends[0]
        for k in range(1, 3):
            turned_corner = jnp.where(full_lane >= 8 * k, pltpu.roll(ends[k], 8 * k, 1), turned_corner)
        up_ref[...] = jnp.concatenate(rows + [pack_corner(turned_corner)], axis=0).astype(BF16)

    def put(to_up_ref, to_down_ref):
        to_up_ref[...] = up_ref[...]
        down = jnp.concatenate([bot_ref[...].astype(F32)[: 3 * C], corner(3 * C)], axis=0)
        to_down_ref[...] = down.astype(BF16)

    pl.when(odd == 0)(lambda: put(q1_ref, q2_ref))
    pl.when(odd == 1)(lambda: put(q2_ref, q1_ref))


def turn_edges(fold, west, east, send, bot):
    return pl.pallas_call(
        turn_kernel,
        out_shape=(jax.ShapeDtypeStruct((SWAP, LANES), BF16),) * 2,
        in_specs=[SM] + [VM] * 4,
        out_specs=(VM, VM),
        scratch_shapes=[pltpu.VMEM((SWAP, LANES), BF16)],
        compiler_params=pltpu.CompilerParams(vmem_limit_bytes=6 * 2**20),
    )(fold, west, east, send, bot)


def shifted(full, ends, lane, e):
    s = e - 3
    if s > 0:
        return pltpu.roll(jnp.where(lane < s, ends, full), LANES - s, 1)
    if s < 0:
        return pltpu.roll(jnp.where(lane >= LANES + s, ends, full), -s, 1)
    return full


UNROLL = 5


def conv_kernel(x_ref, band_ref, west_ref, east_ref, y_far, side_ref, y_ref, sem):
    lane = lanes_bf16(MAIN)
    tile_lane = lax.broadcasted_iota(jnp.int32, (ROWS, LANES), 1)
    for q in range(13):
        both = jnp.where(
            (tile_lane & 7) < 3,
            west_ref[16 * q : 16 * q + 16, :].astype(F32),
            east_ref[16 * q : 16 * q + 16, :].astype(F32),
        ).astype(BF16)
        for c in range(16 if q < 12 else 8):
            side_ref[16 * q + c] = pltpu.roll(both, LANES - (8 * c + 3), 1)

    def some(t, carry):
        for u in range(UNROLL):
            g = UNROLL * t + u
            full = x_ref[pl.ds(8 * g, 8)].reshape(MAIN, LANES)
            ends = side_ref[pl.ds(8 * g, 8)].reshape(MAIN, LANES)
            rhs = jnp.concatenate([shifted(full, ends, lane, e) for e in range(7)], axis=0)
            y_ref[:, g] = dot32(band_ref[g], rhs).reshape(ROWS, 8, LANES)
        part = pl.ds(UNROLL * t, UNROLL)
        pltpu.make_async_copy(y_ref.at[:, part], y_far.at[:, part], sem).start()
        return carry

    lax.fori_loop(0, GROUPS // UNROLL, some, 0)
    pltpu.make_async_copy(y_ref, y_far, sem).wait()


def conv_own(x, band, west, east):
    return pl.pallas_call(
        conv_kernel,
        out_shape=jax.ShapeDtypeStruct((ROWS, GROUPS, 8, LANES), F32),
        in_specs=[VM] * 4,
        out_specs=ANY,
        scratch_shapes=[
            pltpu.VMEM((C, ROWS, LANES), BF16),
            pltpu.VMEM((ROWS, GROUPS, 8, LANES), F32),
            pltpu.SemaphoreType.DMA(()),
        ],
        compiler_params=pltpu.CompilerParams(vmem_limit_bytes=14 * 2**20),
        cost_estimate=pl.CostEstimate(flops=2 * 25 * 256 * 256 * 1024, bytes_accessed=9_000_000, transcendentals=0),
    )(x, band, west, east)


def gelu(h):
    return h * (0.5 + 0.5 * lax.erf(h * np.float32(0.5**0.5)))


def block_kernel(last, block, x_ref, y_far, band_ref, r1_ref, r2_ref, r3_ref, w1_ref, w2_ref, gain_ref, mask_ref,
                 out_ref, *refs):
    edge_refs, (r32_ref, c32_ref, add_ref, o_ref, y_ref, sem) = refs[:-6], refs[-6:]
    fetch = pltpu.make_async_copy(y_far, y_ref, sem)
    fetch.start()
    at_top, odd = place_on_mesh()

    def put(below_ref, above_ref):
        for base, ref in ((0, below_ref), (3, above_ref)):
            v = ref[...].astype(F32)
            for k in range(3):
                r32_ref[base + k] = v[k * C : (k + 1) * C].reshape(GROUPS, 8, LANES)
                for q in range(C // PACK):
                    corner = pltpu.roll(v[3 * C :], LANES - (24 * q + 8 * k + 3), 1)
                    c32_ref[base + k, 5 * q : 5 * q + 5] = corner.reshape(5, 8, LANES)

    pl.when(odd == 0)(lambda: put(r2_ref, r1_ref))
    pl.when((odd == 1) & jnp.logical_not(at_top))(lambda: put(r1_ref, r2_ref))
    pl.when(at_top)(lambda: put(r1_ref, r3_ref))
    lane = lanes_bf16(SIDE)

    def halo(g, carry):
        full = r32_ref[:, g].reshape(SIDE, LANES).astype(BF16)
        ends = c32_ref[:, g].reshape(SIDE, LANES).astype(BF16)
        rhs = jnp.concatenate([shifted(full, ends, lane, e) for e in range(7)], axis=0)
        add_ref[:, g] = dot32(band_ref[g], rhs).reshape(6, 8, LANES)
        return carry

    lax.fori_loop(0, GROUPS, halo, 0, unroll=25)

    fetch.wait()

    def mlp(i0, edges):
        parts = []
        for r in range(2):
            y = y_ref[i0 + r].reshape(C, LANES)
            if edges[r] is not None:
                y = y + add_ref[edges[r]].reshape(C, LANES)
            mean = jnp.sum(y, axis=0, keepdims=True) * np.float32(1 / C)
            y = y - mean
            var = jnp.sum(y * y, axis=0, keepdims=True) * np.float32(1 / C)
            parts.append((y * lax.rsqrt(var + EPS) * gain_ref[...]).astype(BF16))
        hidden = gelu(dot32(w1_ref[...], jnp.concatenate(parts, axis=1))).astype(BF16)
        o = dot32(w2_ref[block], hidden)
        for r in range(2):
            o_ref[pl.ds(i0 + r, C, stride=ROWS), :] = o[:, r * LANES : (r + 1) * LANES]

    edge_of = {row: n for n, row in enumerate(EDGE_ROWS)}
    for i in range(0, ROWS, 2):
        mlp(i, (edge_of.get(i), edge_of.get(i + 1)))
    mask = mask_ref[...]

    def tile(first, count):
        o = o_ref[pl.ds(first * ROWS, count * ROWS), :].reshape(count, ROWS, LANES)
        return (x_ref[pl.ds(first, count)].astype(F32) + o) * mask[None]

    if last:
        def finish(g, carry):
            out_ref[pl.ds(8 * g, 8)] = tile(pl.multiple_of(8 * g, 8), 8).astype(BF16)
            return carry

        lax.fori_loop(0, GROUPS, finish, 0)
    else:
        emit_edges(tile, o_ref, out_ref, *edge_refs)


def run_block(last, block, x, y, band, r1, r2, r3, w1, w2, gain, mask):
    state = jax.ShapeDtypeStruct((C, ROWS, LANES), BF16)
    shapes = (state,) if last else (state,) + EDGE_SHAPES
    return pl.pallas_call(
        lambda *refs: block_kernel(last, block, *refs),
        out_shape=shapes,
        in_specs=[VM, ANY] + [VM] * 8,
        out_specs=(VM,) * len(shapes),
        scratch_shapes=[
            pltpu.VMEM((6, GROUPS, 8, LANES), F32),
            pltpu.VMEM((6, GROUPS, 8, LANES), F32),
            pltpu.VMEM((6, GROUPS, 8, LANES), F32),
            pltpu.VMEM((C * ROWS, LANES), F32),
            pltpu.VMEM((ROWS, GROUPS, 8, LANES), F32),
            pltpu.SemaphoreType.DMA(()),
        ],
        compiler_params=pltpu.CompilerParams(vmem_limit_bytes=16 * 2**20),
    )(x, y, band, r1, r2, r3, w1, w2, gain, mask)


def local(field, land_mask, fold_partner, dw_kernel, norm_gain, w_in, w_out):
    zonal = lax.axis_size("zonal")
    merid = lax.axis_size("merid")
    total = fold_partner.shape[0]
    start = jnp.mod(fold_partner[0] - (LANES // 2 - 1), total)
    turn = start // LANES
    place = lambda m, z: z * merid + m
    even_pairs = [(m, m ^ 1) for m in range(merid)]
    odd_pairs = [(m, ((m - 1) ^ 1) + 1) for m in range(1, merid - 1)]

    def branch_of(shift):
        def branch(rows, mask, *kept):
            pairs = [(place(merid - 1, z), place(merid - 1, (shift - z) % zonal)) for z in range(zonal)]
            return lax.ppermute(rows, ("zonal", "merid"), pairs), float_mask(mask, *kept)

        return branch

    branches = [branch_of(t) for t in range(zonal)]
    taps = jnp.transpose(dw_kernel, (0, 2, 3, 1))
    w2 = jnp.swapaxes(w_out, 1, 2)
    x = field
    send, bot = first_edges(x)
    for b in range(BLOCKS):
        west = lax.ppermute(send, "zonal", [(z, (z + 1) % zonal) for z in range(zonal)])
        east = lax.ppermute(send, "zonal", [((z + 1) % zonal, z) for z in range(zonal)])
        band_main, band_side, w1, gain = make_bands(b, taps, w_in, norm_gain)
        q1, q2 = turn_edges(fold_partner, west, east, send, bot)
        r1 = lax.ppermute(q1, "merid", even_pairs)
        r2 = lax.ppermute(q2, "merid", odd_pairs)
        y = conv_own(x, band_main, west, east)
        q2, y = lax.optimization_barrier((q2, y))
        r3, mask = lax.switch(turn, branches, q2, land_mask, x, y, band_side, w1, gain)
        last = b == BLOCKS - 1
        x, *edges = run_block(last, b, x, y, band_side, r1, r2, r3, w1, w2, gain, mask)
        if not last:
            send, bot = edges
    return x


def mask_kernel(mask_ref, *refs):
    out_ref = refs[-1]
    out_ref[...] = mask_ref[...].astype(F32)


def float_mask(mask, *kept):
    return pl.pallas_call(
        mask_kernel,
        out_shape=jax.ShapeDtypeStruct((ROWS, LANES), F32),
        in_specs=[VM] + [pl.BlockSpec(memory_space=pl.ANY)] * len(kept),
        out_specs=VM,
        compiler_params=pltpu.CompilerParams(vmem_limit_bytes=4 * 2**20),
    )(mask, *kept)


def solution(mesh):
    in_specs = (P(None, "merid", "zonal"), P("merid", "zonal"), P(), P(), P(), P(), P())
    out_specs = P(None, "merid", "zonal")
    return jax.shard_map(local, mesh=mesh, in_specs=in_specs, out_specs=out_specs, check_vma=False)
```

```python
import jax
import jax.numpy as jnp
import numpy as np
from jax import lax
from jax.experimental import pallas as pl
from jax.experimental.pallas import tpu as pltpu
from jax.sharding import PartitionSpec as P

BLOCKS = 3
C = 200
PAD = 208
H = 800
ROWS = 16
LANES = 128
GROUPS = C // 8
MAIN = 8 * ROWS
SIDE = 8 * 6
EPS = 1e-05
F32 = jnp.float32
BF16 = jnp.bfloat16
EDGE_ROWS = (0, 1, 2, 13, 14, 15)
PACK = 40
SEND = PAD + 3 * C + 2 * PACK + 8
SWAP = 3 * C + PACK
BOT = 3 * C + 8
VM = pl.BlockSpec(memory_space=pltpu.VMEM)
SM = pl.BlockSpec(memory_space=pltpu.SMEM)
ANY = pl.BlockSpec(memory_space=pl.ANY)


def dot32(a, b):
    return jnp.dot(a, b, preferred_element_type=F32)


def lanes_bf16(rows):
    return lax.broadcasted_iota(jnp.int32, (rows, LANES), 1).astype(F32).astype(BF16)


def pack_corner(v):
    lane = lax.broadcasted_iota(jnp.int32, (PACK, LANES), 1)
    packed = v[:PACK]
    for q in range(1, C // PACK):
        packed = jnp.where(lane >= 24 * q, pltpu.roll(v[PACK * q : PACK * (q + 1)], 24 * q, 1), packed)
    return packed


def band_kernel(block, taps_ref, w_in_ref, gain_ref, main_ref, side_ref, w1_ref, gains_ref):
    rows = [jnp.concatenate([taps_ref[block, a].astype(F32), jnp.zeros((1, C), F32)], axis=0) for a in range(7)]
    taps = jnp.concatenate(rows + [jnp.zeros((8, C), F32)], axis=0).T.astype(BF16)

    def place(first, second, tap_of, own, out_ref, at):
        depth = own.shape[1]
        tap = lax.broadcasted_iota(jnp.int32, (64, depth), 0)
        both = []
        for i in (first, second):
            spread = jnp.where(tap == tap_of(i), 1.0, 0.0).astype(BF16)
            both.append(dot32(taps, spread).reshape(GROUPS, 8, depth))
        both = jnp.concatenate(both, axis=1).astype(BF16)
        out_ref[:, pl.ds(at, 16), :] = both * own[None]

    lane = lax.broadcasted_iota(jnp.int32, (1, 7 * MAIN), 1)
    e, row = lane // MAIN, lane % ROWS

    def main_tap(i):
        a = row + 3 - i
        return jnp.where((a >= 0) & (a < 7), 8 * a + e, -1)

    wide = lax.broadcasted_iota(jnp.int32, (16, 7 * MAIN), 1)
    high = lax.broadcasted_iota(jnp.int32, (16, 7 * MAIN), 0)
    own_main = jnp.where((wide % MAIN) // ROWS == high % 8, 1.0, 0.0).astype(BF16)

    def main_pair(p, carry):
        place(2 * p, 2 * p + 1, main_tap, own_main, main_ref, pl.multiple_of(16 * p, 16))
        return carry

    lax.fori_loop(0, ROWS // 2, main_pair, 0, unroll=4)
    lane = lax.broadcasted_iota(jnp.int32, (1, 7 * SIDE), 1)
    e_side, slot = lane // SIDE, lane % SIDE
    k = slot // 8
    row_side = jnp.where(k < 3, k, k + ROWS)

    def side_tap(i):
        a = row_side - i
        return jnp.where((a >= 0) & (a < 7), 8 * a + e_side, -1)

    wide = lax.broadcasted_iota(jnp.int32, (16, 7 * SIDE), 1)
    high = lax.broadcasted_iota(jnp.int32, (16, 7 * SIDE), 0)
    own_side = jnp.where(wide % 8 == high % 8, 1.0, 0.0).astype(BF16)
    for p in range(3):
        place(EDGE_ROWS[2 * p], EDGE_ROWS[2 * p + 1], side_tap, own_side, side_ref, 16 * p)
    w1_ref[...] = w_in_ref[block].T
    gain = gain_ref[...].astype(F32)[block : block + 1]
    gains_ref[...] = jnp.broadcast_to(gain, (LANES, C)).T


def make_bands(block, taps, w_in, gain):
    return pl.pallas_call(
        lambda *refs: band_kernel(block, *refs),
        out_shape=(
            jax.ShapeDtypeStruct((GROUPS, MAIN, 7 * MAIN), BF16),
            jax.ShapeDtypeStruct((GROUPS, SIDE, 7 * SIDE), BF16),
            jax.ShapeDtypeStruct((H, C), BF16),
            jax.ShapeDtypeStruct((C, LANES), F32),
        ),
        in_specs=[VM] * 3,
        out_specs=(VM,) * 4,
        compiler_params=pltpu.CompilerParams(vmem_limit_bytes=14 * 2**20),
        cost_estimate=pl.CostEstimate(flops=2 * 16 * 256 * 256 * 1024, bytes_accessed=9_000_000, transcendentals=0),
    )(taps, w_in, gain)


def emit_edges(tile_of, o_ref, out_ref, send_ref, bot_ref):
    lane = lanes_bf16(ROWS)

    def some(first, count):
        v = tile_of(first, count)
        o_ref[pl.ds(first * ROWS, count * ROWS), :] = v.reshape(count * ROWS, LANES)
        v = v.astype(BF16)
        if out_ref is not None:
            out_ref[pl.ds(first, count)] = v
        packed = pltpu.roll(v[0], 3, 1)
        for c in range(1, count):
            packed = jnp.where(lane >= 8 * c, pltpu.roll(v[c], 8 * c + 3, 1), packed)
        return packed

    for q in range(12):
        send_ref[16 * q : 16 * q + 16, :] = some(16 * q, 16)
    send_ref[192:208, :] = some(192, 8)
    wide = lax.broadcasted_iota(jnp.int32, (C, LANES), 1)

    def edge(first):
        rows = [o_ref[pl.ds(first + k, C, stride=ROWS), :] for k in range(3)]
        corner = pltpu.roll(rows[0], 3, 1)
        for k in range(1, 3):
            corner = jnp.where(wide >= 8 * k, pltpu.roll(rows[k], 8 * k + 3, 1), corner)
        return rows, pack_corner(corner)

    fill = jnp.zeros((8, LANES), F32)
    low, low_corner = edge(0)
    bot_ref[...] = jnp.concatenate(low + [fill], axis=0).astype(BF16)
    high, high_corner = edge(ROWS - 3)
    send_ref[PAD:, :] = jnp.concatenate(high + [low_corner, high_corner, fill], axis=0).astype(BF16)


EDGE_SHAPES = (
    jax.ShapeDtypeStruct((SEND, LANES), BF16),
    jax.ShapeDtypeStruct((BOT, LANES), BF16),
)


def first_kernel(x_ref, send_ref, bot_ref, o_ref):
    emit_edges(lambda first, count: x_ref[pl.ds(first, count)].astype(F32), o_ref, None, send_ref, bot_ref)


def first_edges(x):
    return pl.pallas_call(
        first_kernel,
        out_shape=EDGE_SHAPES,
        in_specs=[VM],
        out_specs=(VM,) * 2,
        scratch_shapes=[pltpu.VMEM((C * ROWS, LANES), F32)],
        compiler_params=pltpu.CompilerParams(vmem_limit_bytes=6 * 2**20),
    )(x)


def place_on_mesh():
    level = lax.axis_index("merid")
    return level == lax.axis_size("merid") - 1, level % 2


def turn_kernel(fold_ref, west_ref, east_ref, send_ref, bot_ref, q1_ref, q2_ref, up_ref):
    at_top, odd = place_on_mesh()
    off = (fold_ref[0] + (LANES // 2 + 1)) % LANES - LANES // 2
    lane = lax.broadcasted_iota(jnp.int32, (PACK, LANES), 1)
    parts = [ref[PAD:, :] for ref in (west_ref, send_ref, east_ref)]
    wide = [part.astype(F32) for part in parts]

    def corner(at):
        return jnp.where((lane & 7) < 3, wide[0][at : at + PACK], wide[2][at : at + PACK])

    @pl.when(jnp.logical_not(at_top))
    def _():
        up = jnp.concatenate([wide[1][: 3 * C], corner(3 * C + PACK)], axis=0)
        up_ref[...] = up.astype(BF16)

    @pl.when(at_top)
    def _():
        src = lax.broadcasted_iota(jnp.int32, (LANES, 2 * LANES), 0)
        dst = lax.broadcasted_iota(jnp.int32, (LANES, 2 * LANES), 1)
        col = jnp.where(dst < LANES, dst, jnp.where(dst < LANES + 3, dst - LANES - 3, dst - 3))
        used = dst < LANES + 6
        turned = jnp.zeros((SEND - PAD, 2 * LANES), F32)
        for n in range(3):
            hit = used & (src + 128 * (n - 1) + col == off + 127)
            turned += dot32(parts[n], jnp.where(hit, 1.0, 0.0).astype(BF16))
        rows = [turned[(2 - k) * C : (3 - k) * C, :LANES] for k in range(3)]
        ends = [turned[(2 - k) * C : (3 - k) * C, LANES:] for k in range(3)]
        full_lane = lax.broadcasted_iota(jnp.int32, (C, LANES), 1)
        turned_corner = ends[0]
        for k in range(1, 3):
            turned_corner = jnp.where(full_lane >= 8 * k, pltpu.roll(ends[k], 8 * k, 1), turned_corner)
        up_ref[...] = jnp.concatenate(rows + [pack_corner(turned_corner)], axis=0).astype(BF16)

    def put(to_up_ref, to_down_ref):
        to_up_ref[...] = up_ref[...]
        down = jnp.concatenate([bot_ref[...].astype(F32)[: 3 * C], corner(3 * C)], axis=0)
        to_down_ref[...] = down.astype(BF16)

    pl.when(odd == 0)(lambda: put(q1_ref, q2_ref))
    pl.when(odd == 1)(lambda: put(q2_ref, q1_ref))


def turn_edges(fold, west, east, send, bot):
    return pl.pallas_call(
        turn_kernel,
        out_shape=(jax.ShapeDtypeStruct((SWAP, LANES), BF16),) * 2,
        in_specs=[SM] + [VM] * 4,
        out_specs=(VM, VM),
        scratch_shapes=[pltpu.VMEM((SWAP, LANES), BF16)],
        compiler_params=pltpu.CompilerParams(vmem_limit_bytes=6 * 2**20),
    )(fold, west, east, send, bot)


def shifted(full, ends, lane, e):
    s = e - 3
    if s > 0:
        return pltpu.roll(jnp.where(lane < s, ends, full), LANES - s, 1)
    if s < 0:
        return pltpu.roll(jnp.where(lane >= LANES + s, ends, full), -s, 1)
    return full


UNROLL = 5


def conv_kernel(x_ref, band_ref, west_ref, east_ref, y_far, side_ref, y_ref, sem):
    lane = lanes_bf16(MAIN)
    tile_lane = lax.broadcasted_iota(jnp.int32, (ROWS, LANES), 1)
    for q in range(13):
        both = jnp.where(
            (tile_lane & 7) < 3,
            west_ref[16 * q : 16 * q + 16, :].astype(F32),
            east_ref[16 * q : 16 * q + 16, :].astype(F32),
        ).astype(BF16)
        for c in range(16 if q < 12 else 8):
            side_ref[16 * q + c] = pltpu.roll(both, LANES - (8 * c + 3), 1)

    def some(t, carry):
        for u in range(UNROLL):
            g = UNROLL * t + u
            full = x_ref[pl.ds(8 * g, 8)].reshape(MAIN, LANES)
            ends = side_ref[pl.ds(8 * g, 8)].reshape(MAIN, LANES)
            rhs = jnp.concatenate([shifted(full, ends, lane, e) for e in range(7)], axis=0)
            y_ref[:, g] = dot32(band_ref[g], rhs).reshape(ROWS, 8, LANES)
        part = pl.ds(UNROLL * t, UNROLL)
        pltpu.make_async_copy(y_ref.at[:, part], y_far.at[:, part], sem).start()
        return carry

    lax.fori_loop(0, GROUPS // UNROLL, some, 0)
    pltpu.make_async_copy(y_ref, y_far, sem).wait()


def conv_own(x, band, west, east):
    return pl.pallas_call(
        conv_kernel,
        out_shape=jax.ShapeDtypeStruct((ROWS, GROUPS, 8, LANES), F32),
        in_specs=[VM] * 4,
        out_specs=ANY,
        scratch_shapes=[
            pltpu.VMEM((C, ROWS, LANES), BF16),
            pltpu.VMEM((ROWS, GROUPS, 8, LANES), F32),
            pltpu.SemaphoreType.DMA(()),
        ],
        compiler_params=pltpu.CompilerParams(vmem_limit_bytes=14 * 2**20),
        cost_estimate=pl.CostEstimate(flops=2 * 25 * 256 * 256 * 1024, bytes_accessed=9_000_000, transcendentals=0),
    )(x, band, west, east)


def gelu(h):
    return h * (0.5 + 0.5 * lax.erf(h * np.float32(0.5**0.5)))


def block_kernel(last, block, x_ref, y_far, band_ref, r1_ref, r2_ref, r3_ref, w1_ref, w2_ref, gain_ref, mask_ref,
                 out_ref, *refs):
    edge_refs, (r32_ref, c32_ref, add_ref, o_ref, y_ref, sem) = refs[:-6], refs[-6:]
    fetch = pltpu.make_async_copy(y_far, y_ref, sem)
    fetch.start()
    at_top, odd = place_on_mesh()

    def put(below_ref, above_ref):
        for base, ref in ((0, below_ref), (3, above_ref)):
            v = ref[...].astype(F32)
            for k in range(3):
                r32_ref[base + k] = v[k * C : (k + 1) * C].reshape(GROUPS, 8, LANES)
                for q in range(C // PACK):
                    corner = pltpu.roll(v[3 * C :], LANES - (24 * q + 8 * k + 3), 1)
                    c32_ref[base + k, 5 * q : 5 * q + 5] = corner.reshape(5, 8, LANES)

    pl.when(odd == 0)(lambda: put(r2_ref, r1_ref))
    pl.when((odd == 1) & jnp.logical_not(at_top))(lambda: put(r1_ref, r2_ref))
    pl.when(at_top)(lambda: put(r1_ref, r3_ref))
    lane = lanes_bf16(SIDE)

    def halo(g, carry):
        full = r32_ref[:, g].reshape(SIDE, LANES).astype(BF16)
        ends = c32_ref[:, g].reshape(SIDE, LANES).astype(BF16)
        rhs = jnp.concatenate([shifted(full, ends, lane, e) for e in range(7)], axis=0)
        add_ref[:, g] = dot32(band_ref[g], rhs).reshape(6, 8, LANES)
        return carry

    lax.fori_loop(0, GROUPS, halo, 0, unroll=25)

    fetch.wait()

    def mlp(i0, edges):
        parts = []
        for r in range(2):
            y = y_ref[i0 + r].reshape(C, LANES)
            if edges[r] is not None:
                y = y + add_ref[edges[r]].reshape(C, LANES)
            mean = jnp.sum(y, axis=0, keepdims=True) * np.float32(1 / C)
            y = y - mean
            var = jnp.sum(y * y, axis=0, keepdims=True) * np.float32(1 / C)
            parts.append((y * lax.rsqrt(var + EPS) * gain_ref[...]).astype(BF16))
        hidden = gelu(dot32(w1_ref[...], jnp.concatenate(parts, axis=1))).astype(BF16)
        o = dot32(w2_ref[block], hidden)
        for r in range(2):
            o_ref[pl.ds(i0 + r, C, stride=ROWS), :] = o[:, r * LANES : (r + 1) * LANES]

    edge_of = {row: n for n, row in enumerate(EDGE_ROWS)}
    for i in range(0, ROWS, 2):
        mlp(i, (edge_of.get(i), edge_of.get(i + 1)))
    mask = mask_ref[...]

    def tile(first, count):
        o = o_ref[pl.ds(first * ROWS, count * ROWS), :].reshape(count, ROWS, LANES)
        return (x_ref[pl.ds(first, count)].astype(F32) + o) * mask[None]

    if last:
        def finish(g, carry):
            out_ref[pl.ds(8 * g, 8)] = tile(pl.multiple_of(8 * g, 8), 8).astype(BF16)
            return carry

        lax.fori_loop(0, GROUPS, finish, 0)
    else:
        emit_edges(tile, o_ref, out_ref, *edge_refs)


def run_block(last, block, x, y, band, r1, r2, r3, w1, w2, gain, mask):
    state = jax.ShapeDtypeStruct((C, ROWS, LANES), BF16)
    shapes = (state,) if last else (state,) + EDGE_SHAPES
    return pl.pallas_call(
        lambda *refs: block_kernel(last, block, *refs),
        out_shape=shapes,
        in_specs=[VM, ANY] + [VM] * 8,
        out_specs=(VM,) * len(shapes),
        scratch_shapes=[
            pltpu.VMEM((6, GROUPS, 8, LANES), F32),
            pltpu.VMEM((6, GROUPS, 8, LANES), F32),
            pltpu.VMEM((6, GROUPS, 8, LANES), F32),
            pltpu.VMEM((C * ROWS, LANES), F32),
            pltpu.VMEM((ROWS, GROUPS, 8, LANES), F32),
            pltpu.SemaphoreType.DMA(()),
        ],
        compiler_params=pltpu.CompilerParams(vmem_limit_bytes=16 * 2**20),
    )(x, y, band, r1, r2, r3, w1, w2, gain, mask)


def local(field, land_mask, fold_partner, dw_kernel, norm_gain, w_in, w_out):
    zonal = lax.axis_size("zonal")
    merid = lax.axis_size("merid")
    total = fold_partner.shape[0]
    start = jnp.mod(fold_partner[0] - (LANES // 2 - 1), total)
    turn = start // LANES
    place = lambda m, z: z * merid + m
    even_pairs = [(m, m ^ 1) for m in range(merid)]
    odd_pairs = [(m, ((m - 1) ^ 1) + 1) for m in range(1, merid - 1)]

    def branch_of(shift):
        def branch(rows, mask, *kept):
            pairs = [(place(merid - 1, z), place(merid - 1, (shift - z) % zonal)) for z in range(zonal)]
            return lax.ppermute(rows, ("zonal", "merid"), pairs), float_mask(mask, *kept)

        return branch

    branches = [branch_of(t) for t in range(zonal)]
    taps = jnp.transpose(dw_kernel, (0, 2, 3, 1))
    w2 = jnp.swapaxes(w_out, 1, 2)
    x = field
    send, bot = first_edges(x)
    for b in range(BLOCKS):
        west = lax.ppermute(send, "zonal", [(z, (z + 1) % zonal) for z in range(zonal)])
        east = lax.ppermute(send, "zonal", [((z + 1) % zonal, z) for z in range(zonal)])
        band_main, band_side, w1, gain = make_bands(b, taps, w_in, norm_gain)
        q1, q2 = turn_edges(fold_partner, west, east, send, bot)
        r1 = lax.ppermute(q1, "merid", even_pairs)
        r2 = lax.ppermute(q2, "merid", odd_pairs)
        y = conv_own(x, band_main, west, east)
        q2, y = lax.optimization_barrier((q2, y))
        r3, mask = lax.switch(turn, branches, q2, land_mask, x, y, band_side, w1, gain)
        last = b == BLOCKS - 1
        x, *edges = run_block(last, b, x, y, band_side, r1, r2, r3, w1, w2, gain, mask)
        if not last:
            send, bot = edges
    return x


def mask_kernel(mask_ref, *refs):
    out_ref = refs[-1]
    out_ref[...] = mask_ref[...].astype(F32)


def float_mask(mask, *kept):
    return pl.pallas_call(
        mask_kernel,
        out_shape=jax.ShapeDtypeStruct((ROWS, LANES), F32),
        in_specs=[VM] + [pl.BlockSpec(memory_space=pl.ANY)] * len(kept),
        out_specs=VM,
        compiler_params=pltpu.CompilerParams(vmem_limit_bytes=4 * 2**20),
    )(mask, *kept)


def solution(mesh):
    in_specs = (P(None, "merid", "zonal"), P("merid", "zonal"), P(), P(), P(), P(), P())
    out_specs = P(None, "merid", "zonal")
    return jax.shard_map(local, mesh=mesh, in_specs=in_specs, out_specs=out_specs, check_vma=False)
```

```python
import jax
import jax.numpy as jnp
import numpy as np
from jax import lax
from jax.experimental import pallas as pl
from jax.experimental.pallas import tpu as pltpu
from jax.sharding import PartitionSpec as P

BLOCKS = 3
C = 200
PAD = 208
H = 800
ROWS = 16
LANES = 128
GROUPS = C // 8
MAIN = 8 * ROWS
SIDE = 8 * 6
EPS = 1e-05
F32 = jnp.float32
BF16 = jnp.bfloat16
EDGE_ROWS = (0, 1, 2, 13, 14, 15)
PACK = 40
SEND = PAD + 3 * C + 2 * PACK + 8
SWAP = 3 * C + PACK
BOT = 3 * C + 8
VM = pl.BlockSpec(memory_space=pltpu.VMEM)
SM = pl.BlockSpec(memory_space=pltpu.SMEM)
ANY = pl.BlockSpec(memory_space=pl.ANY)


def dot32(a, b):
    return jnp.dot(a, b, preferred_element_type=F32)


def lanes_bf16(rows):
    return lax.broadcasted_iota(jnp.int32, (rows, LANES), 1).astype(F32).astype(BF16)


def pack_corner(v):
    lane = lax.broadcasted_iota(jnp.int32, (PACK, LANES), 1)
    packed = v[:PACK]
    for q in range(1, C // PACK):
        packed = jnp.where(lane >= 24 * q, pltpu.roll(v[PACK * q : PACK * (q + 1)], 24 * q, 1), packed)
    return packed


def band_kernel(block, taps_ref, w_in_ref, gain_ref, main_ref, side_ref, w1_ref, gains_ref):
    rows = [jnp.concatenate([taps_ref[block, a].astype(F32), jnp.zeros((1, C), F32)], axis=0) for a in range(7)]
    taps = jnp.concatenate(rows + [jnp.zeros((8, C), F32)], axis=0).T.astype(BF16)

    def place(first, second, tap_of, own, out_ref, at):
        depth = own.shape[1]
        tap = lax.broadcasted_iota(jnp.int32, (64, depth), 0)
        both = []
        for i in (first, second):
            spread = jnp.where(tap == tap_of(i), 1.0, 0.0).astype(BF16)
            both.append(dot32(taps, spread).reshape(GROUPS, 8, depth))
        both = jnp.concatenate(both, axis=1).astype(BF16)
        out_ref[:, pl.ds(at, 16), :] = both * own[None]

    lane = lax.broadcasted_iota(jnp.int32, (1, 7 * MAIN), 1)
    e, row = lane // MAIN, lane % ROWS

    def main_tap(i):
        a = row + 3 - i
        return jnp.where((a >= 0) & (a < 7), 8 * a + e, -1)

    wide = lax.broadcasted_iota(jnp.int32, (16, 7 * MAIN), 1)
    high = lax.broadcasted_iota(jnp.int32, (16, 7 * MAIN), 0)
    own_main = jnp.where((wide % MAIN) // ROWS == high % 8, 1.0, 0.0).astype(BF16)

    def main_pair(p, carry):
        place(2 * p, 2 * p + 1, main_tap, own_main, main_ref, pl.multiple_of(16 * p, 16))
        return carry

    lax.fori_loop(0, ROWS // 2, main_pair, 0, unroll=4)
    lane = lax.broadcasted_iota(jnp.int32, (1, 7 * SIDE), 1)
    e_side, slot = lane // SIDE, lane % SIDE
    k = slot // 8
    row_side = jnp.where(k < 3, k, k + ROWS)

    def side_tap(i):
        a = row_side - i
        return jnp.where((a >= 0) & (a < 7), 8 * a + e_side, -1)

    wide = lax.broadcasted_iota(jnp.int32, (16, 7 * SIDE), 1)
    high = lax.broadcasted_iota(jnp.int32, (16, 7 * SIDE), 0)
    own_side = jnp.where(wide % 8 == high % 8, 1.0, 0.0).astype(BF16)
    for p in range(3):
        place(EDGE_ROWS[2 * p], EDGE_ROWS[2 * p + 1], side_tap, own_side, side_ref, 16 * p)
    w1_ref[...] = w_in_ref[block].T
    gain = gain_ref[...].astype(F32)[block : block + 1]
    gains_ref[...] = jnp.broadcast_to(gain, (LANES, C)).T


def make_bands(block, taps, w_in, gain):
    return pl.pallas_call(
        lambda *refs: band_kernel(block, *refs),
        out_shape=(
            jax.ShapeDtypeStruct((GROUPS, MAIN, 7 * MAIN), BF16),
            jax.ShapeDtypeStruct((GROUPS, SIDE, 7 * SIDE), BF16),
            jax.ShapeDtypeStruct((H, C), BF16),
            jax.ShapeDtypeStruct((C, LANES), F32),
        ),
        in_specs=[VM] * 3,
        out_specs=(VM,) * 4,
        compiler_params=pltpu.CompilerParams(vmem_limit_bytes=14 * 2**20),
        cost_estimate=pl.CostEstimate(flops=2 * 16 * 256 * 256 * 1024, bytes_accessed=9_000_000, transcendentals=0),
    )(taps, w_in, gain)


def emit_edges(tile_of, o_ref, out_ref, send_ref, bot_ref):
    lane = lanes_bf16(ROWS)

    def some(first, count):
        v = tile_of(first, count)
        o_ref[pl.ds(first * ROWS, count * ROWS), :] = v.reshape(count * ROWS, LANES)
        v = v.astype(BF16)
        if out_ref is not None:
            out_ref[pl.ds(first, count)] = v
        packed = pltpu.roll(v[0], 3, 1)
        for c in range(1, count):
            packed = jnp.where(lane >= 8 * c, pltpu.roll(v[c], 8 * c + 3, 1), packed)
        return packed

    for q in range(12):
        send_ref[16 * q : 16 * q + 16, :] = some(16 * q, 16)
    send_ref[192:208, :] = some(192, 8)
    wide = lax.broadcasted_iota(jnp.int32, (C, LANES), 1)

    def edge(first):
        rows = [o_ref[pl.ds(first + k, C, stride=ROWS), :] for k in range(3)]
        corner = pltpu.roll(rows[0], 3, 1)
        for k in range(1, 3):
            corner = jnp.where(wide >= 8 * k, pltpu.roll(rows[k], 8 * k + 3, 1), corner)
        return rows, pack_corner(corner)

    fill = jnp.zeros((8, LANES), F32)
    low, low_corner = edge(0)
    bot_ref[...] = jnp.concatenate(low + [fill], axis=0).astype(BF16)
    high, high_corner = edge(ROWS - 3)
    send_ref[PAD:, :] = jnp.concatenate(high + [low_corner, high_corner, fill], axis=0).astype(BF16)


EDGE_SHAPES = (
    jax.ShapeDtypeStruct((SEND, LANES), BF16),
    jax.ShapeDtypeStruct((BOT, LANES), BF16),
)


def first_kernel(x_ref, send_ref, bot_ref, o_ref):
    emit_edges(lambda first, count: x_ref[pl.ds(first, count)].astype(F32), o_ref, None, send_ref, bot_ref)


def first_edges(x):
    return pl.pallas_call(
        first_kernel,
        out_shape=EDGE_SHAPES,
        in_specs=[VM],
        out_specs=(VM,) * 2,
        scratch_shapes=[pltpu.VMEM((C * ROWS, LANES), F32)],
        compiler_params=pltpu.CompilerParams(vmem_limit_bytes=6 * 2**20),
    )(x)


def place_on_mesh():
    level = lax.axis_index("merid")
    return level == lax.axis_size("merid") - 1, level % 2


def turn_kernel(fold_ref, west_ref, east_ref, send_ref, bot_ref, q1_ref, q2_ref, up_ref):
    at_top, odd = place_on_mesh()
    off = (fold_ref[0] + (LANES // 2 + 1)) % LANES - LANES // 2
    lane = lax.broadcasted_iota(jnp.int32, (PACK, LANES), 1)
    parts = [ref[PAD:, :] for ref in (west_ref, send_ref, east_ref)]
    wide = [part.astype(F32) for part in parts]

    def corner(at):
        return jnp.where((lane & 7) < 3, wide[0][at : at + PACK], wide[2][at : at + PACK])

    @pl.when(jnp.logical_not(at_top))
    def _():
        up = jnp.concatenate([wide[1][: 3 * C], corner(3 * C + PACK)], axis=0)
        up_ref[...] = up.astype(BF16)

    @pl.when(at_top)
    def _():
        src = lax.broadcasted_iota(jnp.int32, (LANES, 2 * LANES), 0)
        dst = lax.broadcasted_iota(jnp.int32, (LANES, 2 * LANES), 1)
        col = jnp.where(dst < LANES, dst, jnp.where(dst < LANES + 3, dst - LANES - 3, dst - 3))
        used = dst < LANES + 6
        turned = jnp.zeros((SEND - PAD, 2 * LANES), F32)
        for n in range(3):
            hit = used & (src + 128 * (n - 1) + col == off + 127)
            turned += dot32(parts[n], jnp.where(hit, 1.0, 0.0).astype(BF16))
        rows = [turned[(2 - k) * C : (3 - k) * C, :LANES] for k in range(3)]
        ends = [turned[(2 - k) * C : (3 - k) * C, LANES:] for k in range(3)]
        full_lane = lax.broadcasted_iota(jnp.int32, (C, LANES), 1)
        turned_corner = ends[0]
        for k in range(1, 3):
            turned_corner = jnp.where(full_lane >= 8 * k, pltpu.roll(ends[k], 8 * k, 1), turned_corner)
        up_ref[...] = jnp.concatenate(rows + [pack_corner(turned_corner)], axis=0).astype(BF16)

    def put(to_up_ref, to_down_ref):
        to_up_ref[...] = up_ref[...]
        down = jnp.concatenate([bot_ref[...].astype(F32)[: 3 * C], corner(3 * C)], axis=0)
        to_down_ref[...] = down.astype(BF16)

    pl.when(odd == 0)(lambda: put(q1_ref, q2_ref))
    pl.when(odd == 1)(lambda: put(q2_ref, q1_ref))


def turn_edges(fold, west, east, send, bot):
    return pl.pallas_call(
        turn_kernel,
        out_shape=(jax.ShapeDtypeStruct((SWAP, LANES), BF16),) * 2,
        in_specs=[SM] + [VM] * 4,
        out_specs=(VM, VM),
        scratch_shapes=[pltpu.VMEM((SWAP, LANES), BF16)],
        compiler_params=pltpu.CompilerParams(vmem_limit_bytes=6 * 2**20),
    )(fold, west, east, send, bot)


def shifted(full, ends, lane, e):
    s = e - 3
    if s > 0:
        return pltpu.roll(jnp.where(lane < s, ends, full), LANES - s, 1)
    if s < 0:
        return pltpu.roll(jnp.where(lane >= LANES + s, ends, full), -s, 1)
    return full


UNROLL = 5


def conv_kernel(x_ref, band_ref, west_ref, east_ref, y_far, side_ref, y_ref, sem):
    lane = lanes_bf16(MAIN)
    tile_lane = lax.broadcasted_iota(jnp.int32, (ROWS, LANES), 1)
    for q in range(13):
        both = jnp.where(
            (tile_lane & 7) < 3,
            west_ref[16 * q : 16 * q + 16, :].astype(F32),
            east_ref[16 * q : 16 * q + 16, :].astype(F32),
        ).astype(BF16)
        for c in range(16 if q < 12 else 8):
            side_ref[16 * q + c] = pltpu.roll(both, LANES - (8 * c + 3), 1)

    def some(t, carry):
        for u in range(UNROLL):
            g = UNROLL * t + u
            full = x_ref[pl.ds(8 * g, 8)].reshape(MAIN, LANES)
            ends = side_ref[pl.ds(8 * g, 8)].reshape(MAIN, LANES)
            rhs = jnp.concatenate([shifted(full, ends, lane, e) for e in range(7)], axis=0)
            y_ref[:, g] = dot32(band_ref[g], rhs).reshape(ROWS, 8, LANES)
        part = pl.ds(UNROLL * t, UNROLL)
        pltpu.make_async_copy(y_ref.at[:, part], y_far.at[:, part], sem).start()
        return carry

    lax.fori_loop(0, GROUPS // UNROLL, some, 0)
    pltpu.make_async_copy(y_ref, y_far, sem).wait()


def conv_own(x, band, west, east):
    return pl.pallas_call(
        conv_kernel,
        out_shape=jax.ShapeDtypeStruct((ROWS, GROUPS, 8, LANES), F32),
        in_specs=[VM] * 4,
        out_specs=ANY,
        scratch_shapes=[
            pltpu.VMEM((C, ROWS, LANES), BF16),
            pltpu.VMEM((ROWS, GROUPS, 8, LANES), F32),
            pltpu.SemaphoreType.DMA(()),
        ],
        compiler_params=pltpu.CompilerParams(vmem_limit_bytes=14 * 2**20),
        cost_estimate=pl.CostEstimate(flops=2 * 25 * 256 * 256 * 1024, bytes_accessed=9_000_000, transcendentals=0),
    )(x, band, west, east)


def gelu(h):
    return h * (0.5 + 0.5 * lax.erf(h * np.float32(0.5**0.5)))


def block_kernel(last, block, x_ref, y_far, band_ref, r1_ref, r2_ref, r3_ref, w1_ref, w2_ref, gain_ref, mask_ref,
                 out_ref, *refs):
    edge_refs, (r32_ref, c32_ref, add_ref, o_ref, y_ref, sem) = refs[:-6], refs[-6:]
    fetch = pltpu.make_async_copy(y_far, y_ref, sem)
    fetch.start()
    at_top, odd = place_on_mesh()

    def put(below_ref, above_ref):
        for base, ref in ((0, below_ref), (3, above_ref)):
            v = ref[...].astype(F32)
            for k in range(3):
                r32_ref[base + k] = v[k * C : (k + 1) * C].reshape(GROUPS, 8, LANES)
                for q in range(C // PACK):
                    corner = pltpu.roll(v[3 * C :], LANES - (24 * q + 8 * k + 3), 1)
                    c32_ref[base + k, 5 * q : 5 * q + 5] = corner.reshape(5, 8, LANES)

    pl.when(odd == 0)(lambda: put(r2_ref, r1_ref))
    pl.when((odd == 1) & jnp.logical_not(at_top))(lambda: put(r1_ref, r2_ref))
    pl.when(at_top)(lambda: put(r1_ref, r3_ref))
    lane = lanes_bf16(SIDE)

    def halo(g, carry):
        full = r32_ref[:, g].reshape(SIDE, LANES).astype(BF16)
        ends = c32_ref[:, g].reshape(SIDE, LANES).astype(BF16)
        rhs = jnp.concatenate([shifted(full, ends, lane, e) for e in range(7)], axis=0)
        add_ref[:, g] = dot32(band_ref[g], rhs).reshape(6, 8, LANES)
        return carry

    lax.fori_loop(0, GROUPS, halo, 0, unroll=25)

    fetch.wait()

    def mlp(i0, edges):
        parts = []
        for r in range(2):
            y = y_ref[i0 + r].reshape(C, LANES)
            if edges[r] is not None:
                y = y + add_ref[edges[r]].reshape(C, LANES)
            mean = jnp.sum(y, axis=0, keepdims=True) * np.float32(1 / C)
            y = y - mean
            var = jnp.sum(y * y, axis=0, keepdims=True) * np.float32(1 / C)
            parts.append((y * lax.rsqrt(var + EPS) * gain_ref[...]).astype(BF16))
        hidden = gelu(dot32(w1_ref[...], jnp.concatenate(parts, axis=1))).astype(BF16)
        o = dot32(w2_ref[block], hidden)
        for r in range(2):
            o_ref[pl.ds(i0 + r, C, stride=ROWS), :] = o[:, r * LANES : (r + 1) * LANES]

    edge_of = {row: n for n, row in enumerate(EDGE_ROWS)}
    for i in range(0, ROWS, 2):
        mlp(i, (edge_of.get(i), edge_of.get(i + 1)))
    mask = mask_ref[...]

    def tile(first, count):
        o = o_ref[pl.ds(first * ROWS, count * ROWS), :].reshape(count, ROWS, LANES)
        return (x_ref[pl.ds(first, count)].astype(F32) + o) * mask[None]

    if last:
        whole = edge_refs[0]
        for g in range(GROUPS):
            whole[8 * g : 8 * g + 8] = tile(8 * g, 8).astype(BF16)
            if g % 5 == 4:
                part = pl.ds(8 * (g - 4), 40)
                pltpu.make_async_copy(whole.at[part], out_ref.at[part], sem).start()
        pltpu.make_async_copy(whole, out_ref, sem).wait()
    else:
        emit_edges(tile, o_ref, out_ref, *edge_refs)


def run_block(last, block, x, y, band, r1, r2, r3, w1, w2, gain, mask):
    state = jax.ShapeDtypeStruct((C, ROWS, LANES), BF16)
    shapes = (state,) if last else (state,) + EDGE_SHAPES
    return pl.pallas_call(
        lambda *refs: block_kernel(last, block, *refs),
        out_shape=shapes,
        in_specs=[VM, ANY] + [VM] * 8,
        out_specs=(ANY,) if last else (VM,) * len(shapes),
        scratch_shapes=([pltpu.VMEM((C, ROWS, LANES), BF16)] if last else [])
        + [
            pltpu.VMEM((6, GROUPS, 8, LANES), F32),
            pltpu.VMEM((6, GROUPS, 8, LANES), F32),
            pltpu.VMEM((6, GROUPS, 8, LANES), F32),
            pltpu.VMEM((C * ROWS, LANES), F32),
            pltpu.VMEM((ROWS, GROUPS, 8, LANES), F32),
            pltpu.SemaphoreType.DMA(()),
        ],
        compiler_params=pltpu.CompilerParams(vmem_limit_bytes=16 * 2**20),
    )(x, y, band, r1, r2, r3, w1, w2, gain, mask)


def local(field, land_mask, fold_partner, dw_kernel, norm_gain, w_in, w_out):
    zonal = lax.axis_size("zonal")
    merid = lax.axis_size("merid")
    total = fold_partner.shape[0]
    start = jnp.mod(fold_partner[0] - (LANES // 2 - 1), total)
    turn = start // LANES
    place = lambda m, z: z * merid + m
    even_pairs = [(m, m ^ 1) for m in range(merid)]
    odd_pairs = [(m, ((m - 1) ^ 1) + 1) for m in range(1, merid - 1)]

    def branch_of(shift):
        def branch(rows, mask, *kept):
            pairs = [(place(merid - 1, z), place(merid - 1, (shift - z) % zonal)) for z in range(zonal)]
            return lax.ppermute(rows, ("zonal", "merid"), pairs), float_mask(mask, *kept)

        return branch

    branches = [branch_of(t) for t in range(zonal)]
    taps = jnp.transpose(dw_kernel, (0, 2, 3, 1))
    w2 = jnp.swapaxes(w_out, 1, 2)
    x = field
    send, bot = first_edges(x)
    for b in range(BLOCKS):
        west = lax.ppermute(send, "zonal", [(z, (z + 1) % zonal) for z in range(zonal)])
        east = lax.ppermute(send, "zonal", [((z + 1) % zonal, z) for z in range(zonal)])
        band_main, band_side, w1, gain = make_bands(b, taps, w_in, norm_gain)
        q1, q2 = turn_edges(fold_partner, west, east, send, bot)
        r1 = lax.ppermute(q1, "merid", even_pairs)
        r2 = lax.ppermute(q2, "merid", odd_pairs)
        y = conv_own(x, band_main, west, east)
        q2, y = lax.optimization_barrier((q2, y))
        r3, mask = lax.switch(turn, branches, q2, land_mask, x, y, band_side, w1, gain)
        last = b == BLOCKS - 1
        x, *edges = run_block(last, b, x, y, band_side, r1, r2, r3, w1, w2, gain, mask)
        if not last:
            send, bot = edges
    return x


def mask_kernel(mask_ref, *refs):
    out_ref = refs[-1]
    out_ref[...] = mask_ref[...].astype(F32)


def float_mask(mask, *kept):
    return pl.pallas_call(
        mask_kernel,
        out_shape=jax.ShapeDtypeStruct((ROWS, LANES), F32),
        in_specs=[VM] + [pl.BlockSpec(memory_space=pl.ANY)] * len(kept),
        out_specs=VM,
        compiler_params=pltpu.CompilerParams(vmem_limit_bytes=4 * 2**20),
    )(mask, *kept)


def solution(mesh):
    in_specs = (P(None, "merid", "zonal"), P("merid", "zonal"), P(), P(), P(), P(), P())
    out_specs = P(None, "merid", "zonal")
    return jax.shard_map(local, mesh=mesh, in_specs=in_specs, out_specs=out_specs, check_vma=False)
```

```python
import jax
import jax.numpy as jnp
import numpy as np
from jax import lax
from jax.experimental import pallas as pl
from jax.experimental.pallas import tpu as pltpu
from jax.sharding import PartitionSpec as P

BLOCKS = 3
C = 200
PAD = 208
H = 800
ROWS = 16
LANES = 128
GROUPS = C // 8
MAIN = 8 * ROWS
SIDE = 8 * 6
EPS = 1e-05
F32 = jnp.float32
BF16 = jnp.bfloat16
EDGE_ROWS = (0, 1, 2, 13, 14, 15)
PACK = 40
SEND = PAD + 3 * C + 2 * PACK + 8
SWAP = 3 * C + PACK
BOT = 3 * C + 8
VM = pl.BlockSpec(memory_space=pltpu.VMEM)
SM = pl.BlockSpec(memory_space=pltpu.SMEM)
ANY = pl.BlockSpec(memory_space=pl.ANY)


def dot32(a, b):
    return jnp.dot(a, b, preferred_element_type=F32)


def lanes_bf16(rows):
    return lax.broadcasted_iota(jnp.int32, (rows, LANES), 1).astype(F32).astype(BF16)


def pack_corner(v):
    lane = lax.broadcasted_iota(jnp.int32, (PACK, LANES), 1)
    packed = v[:PACK]
    for q in range(1, C // PACK):
        packed = jnp.where(lane >= 24 * q, pltpu.roll(v[PACK * q : PACK * (q + 1)], 24 * q, 1), packed)
    return packed


def band_kernel(block, taps_ref, w_in_ref, gain_ref, main_ref, side_ref, w1_ref, gains_ref):
    rows = [jnp.concatenate([taps_ref[block, a].astype(F32), jnp.zeros((1, C), F32)], axis=0) for a in range(7)]
    taps = jnp.concatenate(rows + [jnp.zeros((8, C), F32)], axis=0).T.astype(BF16)

    def place(first, second, tap_of, own, out_ref, at):
        depth = own.shape[1]
        tap = lax.broadcasted_iota(jnp.int32, (64, depth), 0)
        both = []
        for i in (first, second):
            spread = jnp.where(tap == tap_of(i), 1.0, 0.0).astype(BF16)
            both.append(dot32(taps, spread).reshape(GROUPS, 8, depth))
        both = jnp.concatenate(both, axis=1).astype(BF16)
        out_ref[:, pl.ds(at, 16), :] = both * own[None]

    lane = lax.broadcasted_iota(jnp.int32, (1, 7 * MAIN), 1)
    e, row = lane // MAIN, lane % ROWS

    def main_tap(i):
        a = row + 3 - i
        return jnp.where((a >= 0) & (a < 7), 8 * a + e, -1)

    wide = lax.broadcasted_iota(jnp.int32, (16, 7 * MAIN), 1)
    high = lax.broadcasted_iota(jnp.int32, (16, 7 * MAIN), 0)
    own_main = jnp.where((wide % MAIN) // ROWS == high % 8, 1.0, 0.0).astype(BF16)

    def main_pair(p, carry):
        place(2 * p, 2 * p + 1, main_tap, own_main, main_ref, pl.multiple_of(16 * p, 16))
        return carry

    lax.fori_loop(0, ROWS // 2, main_pair, 0, unroll=8)
    lane = lax.broadcasted_iota(jnp.int32, (1, 7 * SIDE), 1)
    e_side, slot = lane // SIDE, lane % SIDE
    k = slot // 8
    row_side = jnp.where(k < 3, k, k + ROWS)

    def side_tap(i):
        a = row_side - i
        return jnp.where((a >= 0) & (a < 7), 8 * a + e_side, -1)

    wide = lax.broadcasted_iota(jnp.int32, (16, 7 * SIDE), 1)
    high = lax.broadcasted_iota(jnp.int32, (16, 7 * SIDE), 0)
    own_side = jnp.where(wide % 8 == high % 8, 1.0, 0.0).astype(BF16)
    for p in range(3):
        place(EDGE_ROWS[2 * p], EDGE_ROWS[2 * p + 1], side_tap, own_side, side_ref, 16 * p)
    w1_ref[...] = w_in_ref[block].T
    gain = gain_ref[...].astype(F32)[block : block + 1]
    gains_ref[...] = jnp.broadcast_to(gain, (LANES, C)).T


def make_bands(block, taps, w_in, gain):
    return pl.pallas_call(
        lambda *refs: band_kernel(block, *refs),
        out_shape=(
            jax.ShapeDtypeStruct((GROUPS, MAIN, 7 * MAIN), BF16),
            jax.ShapeDtypeStruct((GROUPS, SIDE, 7 * SIDE), BF16),
            jax.ShapeDtypeStruct((H, C), BF16),
            jax.ShapeDtypeStruct((C, LANES), F32),
        ),
        in_specs=[VM] * 3,
        out_specs=(VM,) * 4,
        compiler_params=pltpu.CompilerParams(vmem_limit_bytes=14 * 2**20),
        cost_estimate=pl.CostEstimate(flops=2 * 16 * 256 * 256 * 1024, bytes_accessed=9_000_000, transcendentals=0),
    )(taps, w_in, gain)


def emit_edges(tile_of, o_ref, out_ref, send_ref, bot_ref):
    lane = lanes_bf16(ROWS)

    def some(first, count):
        v = tile_of(first, count)
        o_ref[pl.ds(first * ROWS, count * ROWS), :] = v.reshape(count * ROWS, LANES)
        v = v.astype(BF16)
        if out_ref is not None:
            out_ref[pl.ds(first, count)] = v
        packed = pltpu.roll(v[0], 3, 1)
        for c in range(1, count):
            packed = jnp.where(lane >= 8 * c, pltpu.roll(v[c], 8 * c + 3, 1), packed)
        return packed

    for q in range(12):
        send_ref[16 * q : 16 * q + 16, :] = some(16 * q, 16)
    send_ref[192:208, :] = some(192, 8)
    wide = lax.broadcasted_iota(jnp.int32, (C, LANES), 1)

    def edge(first):
        rows = [o_ref[pl.ds(first + k, C, stride=ROWS), :] for k in range(3)]
        corner = pltpu.roll(rows[0], 3, 1)
        for k in range(1, 3):
            corner = jnp.where(wide >= 8 * k, pltpu.roll(rows[k], 8 * k + 3, 1), corner)
        return rows, pack_corner(corner)

    fill = jnp.zeros((8, LANES), F32)
    low, low_corner = edge(0)
    bot_ref[...] = jnp.concatenate(low + [fill], axis=0).astype(BF16)
    high, high_corner = edge(ROWS - 3)
    send_ref[PAD:, :] = jnp.concatenate(high + [low_corner, high_corner, fill], axis=0).astype(BF16)


EDGE_SHAPES = (
    jax.ShapeDtypeStruct((SEND, LANES), BF16),
    jax.ShapeDtypeStruct((BOT, LANES), BF16),
)


def first_kernel(x_ref, send_ref, bot_ref, o_ref):
    emit_edges(lambda first, count: x_ref[pl.ds(first, count)].astype(F32), o_ref, None, send_ref, bot_ref)


def first_edges(x):
    return pl.pallas_call(
        first_kernel,
        out_shape=EDGE_SHAPES,
        in_specs=[VM],
        out_specs=(VM,) * 2,
        scratch_shapes=[pltpu.VMEM((C * ROWS, LANES), F32)],
        compiler_params=pltpu.CompilerParams(vmem_limit_bytes=6 * 2**20),
    )(x)


def place_on_mesh():
    level = lax.axis_index("merid")
    return level == lax.axis_size("merid") - 1, level % 2


def turn_kernel(fold_ref, west_ref, east_ref, send_ref, bot_ref, q1_ref, q2_ref, up_ref):
    at_top, odd = place_on_mesh()
    off = (fold_ref[0] + (LANES // 2 + 1)) % LANES - LANES // 2
    lane = lax.broadcasted_iota(jnp.int32, (PACK, LANES), 1)
    parts = [ref[PAD:, :] for ref in (west_ref, send_ref, east_ref)]
    wide = [part.astype(F32) for part in parts]

    def corner(at):
        return jnp.where((lane & 7) < 3, wide[0][at : at + PACK], wide[2][at : at + PACK])

    @pl.when(jnp.logical_not(at_top))
    def _():
        up = jnp.concatenate([wide[1][: 3 * C], corner(3 * C + PACK)], axis=0)
        up_ref[...] = up.astype(BF16)

    @pl.when(at_top)
    def _():
        src = lax.broadcasted_iota(jnp.int32, (LANES, 2 * LANES), 0)
        dst = lax.broadcasted_iota(jnp.int32, (LANES, 2 * LANES), 1)
        col = jnp.where(dst < LANES, dst, jnp.where(dst < LANES + 3, dst - LANES - 3, dst - 3))
        used = dst < LANES + 6
        turned = jnp.zeros((SEND - PAD, 2 * LANES), F32)
        for n in range(3):
            hit = used & (src + 128 * (n - 1) + col == off + 127)
            turned += dot32(parts[n], jnp.where(hit, 1.0, 0.0).astype(BF16))
        rows = [turned[(2 - k) * C : (3 - k) * C, :LANES] for k in range(3)]
        ends = [turned[(2 - k) * C : (3 - k) * C, LANES:] for k in range(3)]
        full_lane = lax.broadcasted_iota(jnp.int32, (C, LANES), 1)
        turned_corner = ends[0]
        for k in range(1, 3):
            turned_corner = jnp.where(full_lane >= 8 * k, pltpu.roll(ends[k], 8 * k, 1), turned_corner)
        up_ref[...] = jnp.concatenate(rows + [pack_corner(turned_corner)], axis=0).astype(BF16)

    def put(to_up_ref, to_down_ref):
        to_up_ref[...] = up_ref[...]
        down = jnp.concatenate([bot_ref[...].astype(F32)[: 3 * C], corner(3 * C)], axis=0)
        to_down_ref[...] = down.astype(BF16)

    pl.when(odd == 0)(lambda: put(q1_ref, q2_ref))
    pl.when(odd == 1)(lambda: put(q2_ref, q1_ref))


def turn_edges(fold, west, east, send, bot):
    return pl.pallas_call(
        turn_kernel,
        out_shape=(jax.ShapeDtypeStruct((SWAP, LANES), BF16),) * 2,
        in_specs=[SM] + [VM] * 4,
        out_specs=(VM, VM),
        scratch_shapes=[pltpu.VMEM((SWAP, LANES), BF16)],
        compiler_params=pltpu.CompilerParams(vmem_limit_bytes=6 * 2**20),
    )(fold, west, east, send, bot)


def shifted(full, ends, lane, e):
    s = e - 3
    if s > 0:
        return pltpu.roll(jnp.where(lane < s, ends, full), LANES - s, 1)
    if s < 0:
        return pltpu.roll(jnp.where(lane >= LANES + s, ends, full), -s, 1)
    return full


UNROLL = 5


def conv_kernel(x_ref, band_ref, west_ref, east_ref, y_far, side_ref, y_ref, sem):
    lane = lanes_bf16(MAIN)
    tile_lane = lax.broadcasted_iota(jnp.int32, (ROWS, LANES), 1)
    for q in range(13):
        both = jnp.where(
            (tile_lane & 7) < 3,
            west_ref[16 * q : 16 * q + 16, :].astype(F32),
            east_ref[16 * q : 16 * q + 16, :].astype(F32),
        ).astype(BF16)
        for c in range(16 if q < 12 else 8):
            side_ref[16 * q + c] = pltpu.roll(both, LANES - (8 * c + 3), 1)

    def some(t, carry):
        for u in range(UNROLL):
            g = UNROLL * t + u
            full = x_ref[pl.ds(8 * g, 8)].reshape(MAIN, LANES)
            ends = side_ref[pl.ds(8 * g, 8)].reshape(MAIN, LANES)
            rhs = jnp.concatenate([shifted(full, ends, lane, e) for e in range(7)], axis=0)
            y_ref[:, g] = dot32(band_ref[g], rhs).reshape(ROWS, 8, LANES)
        part = pl.ds(UNROLL * t, UNROLL)
        pltpu.make_async_copy(y_ref.at[:, part], y_far.at[:, part], sem).start()
        return carry

    lax.fori_loop(0, GROUPS // UNROLL, some, 0)
    pltpu.make_async_copy(y_ref, y_far, sem).wait()


def conv_own(x, band, west, east):
    return pl.pallas_call(
        conv_kernel,
        out_shape=jax.ShapeDtypeStruct((ROWS, GROUPS, 8, LANES), F32),
        in_specs=[VM] * 4,
        out_specs=ANY,
        scratch_shapes=[
            pltpu.VMEM((C, ROWS, LANES), BF16),
            pltpu.VMEM((ROWS, GROUPS, 8, LANES), F32),
            pltpu.SemaphoreType.DMA(()),
        ],
        compiler_params=pltpu.CompilerParams(vmem_limit_bytes=14 * 2**20),
        cost_estimate=pl.CostEstimate(flops=2 * 25 * 256 * 256 * 1024, bytes_accessed=9_000_000, transcendentals=0),
    )(x, band, west, east)


def gelu(h):
    return h * (0.5 + 0.5 * lax.erf(h * np.float32(0.5**0.5)))


def block_kernel(last, block, x_ref, y_far, band_ref, r1_ref, r2_ref, r3_ref, w1_ref, w2_ref, gain_ref, mask_ref,
                 out_ref, *refs):
    edge_refs, (r32_ref, c32_ref, add_ref, o_ref, y_ref, sem) = refs[:-6], refs[-6:]
    fetch = pltpu.make_async_copy(y_far, y_ref, sem)
    fetch.start()
    at_top, odd = place_on_mesh()

    def put(below_ref, above_ref):
        for base, ref in ((0, below_ref), (3, above_ref)):
            v = ref[...].astype(F32)
            for k in range(3):
                r32_ref[base + k] = v[k * C : (k + 1) * C].reshape(GROUPS, 8, LANES)
                for q in range(C // PACK):
                    corner = pltpu.roll(v[3 * C :], LANES - (24 * q + 8 * k + 3), 1)
                    c32_ref[base + k, 5 * q : 5 * q + 5] = corner.reshape(5, 8, LANES)

    pl.when(odd == 0)(lambda: put(r2_ref, r1_ref))
    pl.when((odd == 1) & jnp.logical_not(at_top))(lambda: put(r1_ref, r2_ref))
    pl.when(at_top)(lambda: put(r1_ref, r3_ref))
    lane = lanes_bf16(SIDE)

    def halo(g, carry):
        full = r32_ref[:, g].reshape(SIDE, LANES).astype(BF16)
        ends = c32_ref[:, g].reshape(SIDE, LANES).astype(BF16)
        rhs = jnp.concatenate([shifted(full, ends, lane, e) for e in range(7)], axis=0)
        add_ref[:, g] = dot32(band_ref[g], rhs).reshape(6, 8, LANES)
        return carry

    lax.fori_loop(0, GROUPS, halo, 0, unroll=25)

    fetch.wait()

    def mlp(i0, edges):
        parts = []
        for r in range(2):
            y = y_ref[i0 + r].reshape(C, LANES)
            if edges[r] is not None:
                y = y + add_ref[edges[r]].reshape(C, LANES)
            mean = jnp.sum(y, axis=0, keepdims=True) * np.float32(1 / C)
            y = y - mean
            var = jnp.sum(y * y, axis=0, keepdims=True) * np.float32(1 / C)
            parts.append((y * lax.rsqrt(var + EPS) * gain_ref[...]).astype(BF16))
        hidden = gelu(dot32(w1_ref[...], jnp.concatenate(parts, axis=1))).astype(BF16)
        o = dot32(w2_ref[block], hidden)
        for r in range(2):
            o_ref[pl.ds(i0 + r, C, stride=ROWS), :] = o[:, r * LANES : (r + 1) * LANES]

    edge_of = {row: n for n, row in enumerate(EDGE_ROWS)}
    for i in range(0, ROWS, 2):
        mlp(i, (edge_of.get(i), edge_of.get(i + 1)))
    mask = mask_ref[...]

    def tile(first, count):
        o = o_ref[pl.ds(first * ROWS, count * ROWS), :].reshape(count, ROWS, LANES)
        return (x_ref[pl.ds(first, count)].astype(F32) + o) * mask[None]

    if last:
        whole = edge_refs[0]
        for g in range(GROUPS):
            whole[8 * g : 8 * g + 8] = tile(8 * g, 8).astype(BF16)
            if g % 5 == 4:
                part = pl.ds(8 * (g - 4), 40)
                pltpu.make_async_copy(whole.at[part], out_ref.at[part], sem).start()
        pltpu.make_async_copy(whole, out_ref, sem).wait()
    else:
        emit_edges(tile, o_ref, out_ref, *edge_refs)


def run_block(last, block, x, y, band, r1, r2, r3, w1, w2, gain, mask):
    state = jax.ShapeDtypeStruct((C, ROWS, LANES), BF16)
    shapes = (state,) if last else (state,) + EDGE_SHAPES
    return pl.pallas_call(
        lambda *refs: block_kernel(last, block, *refs),
        out_shape=shapes,
        in_specs=[VM, ANY] + [VM] * 8,
        out_specs=(ANY,) if last else (VM,) * len(shapes),
        scratch_shapes=([pltpu.VMEM((C, ROWS, LANES), BF16)] if last else [])
        + [
            pltpu.VMEM((6, GROUPS, 8, LANES), F32),
            pltpu.VMEM((6, GROUPS, 8, LANES), F32),
            pltpu.VMEM((6, GROUPS, 8, LANES), F32),
            pltpu.VMEM((C * ROWS, LANES), F32),
            pltpu.VMEM((ROWS, GROUPS, 8, LANES), F32),
            pltpu.SemaphoreType.DMA(()),
        ],
        compiler_params=pltpu.CompilerParams(vmem_limit_bytes=16 * 2**20),
    )(x, y, band, r1, r2, r3, w1, w2, gain, mask)


def local(field, land_mask, fold_partner, dw_kernel, norm_gain, w_in, w_out):
    zonal = lax.axis_size("zonal")
    merid = lax.axis_size("merid")
    total = fold_partner.shape[0]
    start = jnp.mod(fold_partner[0] - (LANES // 2 - 1), total)
    turn = start // LANES
    place = lambda m, z: z * merid + m
    even_pairs = [(m, m ^ 1) for m in range(merid)]
    odd_pairs = [(m, ((m - 1) ^ 1) + 1) for m in range(1, merid - 1)]

    def branch_of(shift):
        def branch(rows, mask, *kept):
            pairs = [(place(merid - 1, z), place(merid - 1, (shift - z) % zonal)) for z in range(zonal)]
            return lax.ppermute(rows, ("zonal", "merid"), pairs), float_mask(mask, *kept)

        return branch

    branches = [branch_of(t) for t in range(zonal)]
    taps = jnp.transpose(dw_kernel, (0, 2, 3, 1))
    w2 = jnp.swapaxes(w_out, 1, 2)
    x = field
    send, bot = first_edges(x)
    for b in range(BLOCKS):
        west = lax.ppermute(send, "zonal", [(z, (z + 1) % zonal) for z in range(zonal)])
        east = lax.ppermute(send, "zonal", [((z + 1) % zonal, z) for z in range(zonal)])
        band_main, band_side, w1, gain = make_bands(b, taps, w_in, norm_gain)
        q1, q2 = turn_edges(fold_partner, west, east, send, bot)
        r1 = lax.ppermute(q1, "merid", even_pairs)
        r2 = lax.ppermute(q2, "merid", odd_pairs)
        y = conv_own(x, band_main, west, east)
        q2, y = lax.optimization_barrier((q2, y))
        r3, mask = lax.switch(turn, branches, q2, land_mask, x, y, band_side, w1, gain)
        last = b == BLOCKS - 1
        x, *edges = run_block(last, b, x, y, band_side, r1, r2, r3, w1, w2, gain, mask)
        if not last:
            send, bot = edges
    return x


def mask_kernel(mask_ref, *refs):
    out_ref = refs[-1]
    out_ref[...] = mask_ref[...].astype(F32)


def float_mask(mask, *kept):
    return pl.pallas_call(
        mask_kernel,
        out_shape=jax.ShapeDtypeStruct((ROWS, LANES), F32),
        in_specs=[VM] + [pl.BlockSpec(memory_space=pl.ANY)] * len(kept),
        out_specs=VM,
        compiler_params=pltpu.CompilerParams(vmem_limit_bytes=4 * 2**20),
    )(mask, *kept)


def solution(mesh):
    in_specs = (P(None, "merid", "zonal"), P("merid", "zonal"), P(), P(), P(), P(), P())
    out_specs = P(None, "merid", "zonal")
    return jax.shard_map(local, mesh=mesh, in_specs=in_specs, out_specs=out_specs, check_vma=False)
```
